512 devices in a mesh: gx: 8 (over y_hi, x), gy: 4 (over y_lo), gz: 16 (over z, core).
Axes of the slice: x: 4, y: 8 (y_hi: 2, y_lo: 4; y = y_hi * 4 + y_lo), z: 8, core: 2. Of those that a mesh axis runs over, the one named last changes fastest.
Arguments:
- design: float32 [64, 32, 4096], P('gx', 'gy', 'gz'), may hold values from 0 to 1
- flags: int32 [64, 32, 4096], P('gx', 'gy', 'gz'), may hold values from 0 to 7
- displacement: float32 [3, 64, 32, 4096], P(None, 'gx', 'gy', 'gz'), may hold values from -6 to 6
- adjoint: float32 [3, 64, 32, 4096], P(None, 'gx', 'gy', 'gz'), may hold values from -6 to 6
- pressure: float32 [64, 32, 4096], P('gx', 'gy', 'gz'), may hold values from -6 to 6
- multiplier: float32 [64, 32, 4096], P('gx', 'gy', 'gz'), may hold values from -6 to 6
Outputs:
- sensitivity: float32 [64, 32, 4096], P('gx', 'gy', 'gz')
The draws below stay inside these ranges and needn't reach their ends.
Inputs may be any that keep to these rules, and one draw needn't show every extreme that they name: `flags`: 0 marks a passive void element, 1 a passive solid one, every other value a design element.
All inputs are finite; a program needn't handle non-finite values.
Results may differ from the reference program's by a relative error of at most 0.00019.
Values sent between devices are 32-bit elements; how exact they have to be, the bound alone decides.
A program may use at most 64 MiB of HBM per device.

```python
import math
import jax
import jax.numpy as jnp
import numpy as np
from jax import lax

NX = 64
NY = 32
NZ = 4096


def place_ends(array, rng, smallest, largest):
    longest = array.shape.index(max(array.shape))
    spots = []
    for shift in (0, 1):
        where = [jax.random.randint(jax.random.fold_in(rng, axis), (), 0, length) for axis, length in enumerate(array.shape)]
        where[longest] = (where[longest] + shift) % array.shape[longest]
        spots.append(tuple(where))
    return array.at[spots[0]].set(smallest).at[spots[1]].set(largest)


def block_levels(own_key, dims, split, low, top_value):
    factor_of = 1.0
    for position, shards_of in split:
        draws = jax.random.uniform(jax.random.fold_in(jax.random.fold_in(own_key, 6), position), (shards_of,), jnp.float32, low / len(split), top_value / len(split))
        factor_of = factor_of * jnp.repeat(jnp.exp(draws), dims[position] // shards_of).reshape((-1,) + (1,) * (len(dims) - 1 - position))
    return factor_of


def centred(own_key, extent, deviation, reach, shards=(), held_as=jnp.bfloat16):
    level = block_levels(own_key, extent, shards, -0.22, 0.18) if shards else 1.0
    drawn = jax.random.normal(own_key, extent, jnp.float32) * deviation * level
    return jnp.minimum(jnp.maximum(drawn, -reach), reach).astype(held_as)


def setup_inputs(seed: int = 0) -> dict:
    key_list = jax.random.split(jax.random.key(seed), 7)
    design = jnp.clip(1.0 * jax.random.uniform(key_list[0], (NX, NY, NZ), jnp.float32) ** block_levels(key_list[0], (NX, NY, NZ), ((0, 8), (1, 4), (2, 16)), -0.2, 0.2), 0.0, 1.0)
    flags = place_ends(jax.random.randint(key_list[1], (NX, NY, NZ), 0, 8), jax.random.fold_in(key_list[1], 1), 0, 7).astype(jnp.int32)
    displacement = centred(key_list[2], (3, NX, NY, NZ), 1.0, 6.0, ((1, 8), (2, 4), (3, 16)), jnp.float32)
    adjoint = centred(key_list[3], (3, NX, NY, NZ), 1.0, 6.0, ((1, 8), (2, 4), (3, 16)), jnp.float32)
    pressure = centred(key_list[4], (NX, NY, NZ), 1.0, 6.0, ((0, 8), (1, 4), (2, 16)), jnp.float32)
    multiplier = centred(key_list[5], (NX, NY, NZ), 1.0, 6.0, ((0, 8), (1, 4), (2, 16)), jnp.float32)
    return {"design": design, "flags": flags, "displacement": displacement, "adjoint": adjoint, "pressure": pressure, "multiplier": multiplier}


poisson = 0.45
sharpness = 4.0
threshold = 0.5
stiff_floor = 0.001
cone_radius = 3.5

def element_tables():
    root = 1.0 / np.sqrt(3.0)
    points = [(1.0 - root) / 2.0, (1.0 + root) / 2.0]
    shear = 1.0 / (2.0 * (1.0 + poisson))
    project = np.zeros((6, 6))
    for place, entry in enumerate([1.0, 1.0, 1.0, 0.5, 0.5, 0.5]):
        project[place, place] = entry
    project[:3, :3] -= 1.0 / 3.0
    elastic = 2.0 * shear * project
    stiffness = np.zeros((24, 24))
    coupling = np.zeros(24)
    for point_x in points:
        for point_y in points:
            for point_z in points:
                deriv = np.zeros((3, 8))
                for corner in range(8):
                    bit_x, bit_y, bit_z = (corner & 1, corner >> 1 & 1, corner >> 2 & 1)
                    fac_x = point_x if bit_x else 1.0 - point_x
                    fac_y = point_y if bit_y else 1.0 - point_y
                    fac_z = point_z if bit_z else 1.0 - point_z
                    sig_x = 1.0 if bit_x else -1.0
                    sig_y = 1.0 if bit_y else -1.0
                    sig_z = 1.0 if bit_z else -1.0
                    deriv[0, corner] = sig_x * fac_y * fac_z
                    deriv[1, corner] = fac_x * sig_y * fac_z
                    deriv[2, corner] = fac_x * fac_y * sig_z
                strain = np.zeros((6, 24))
                for corner in range(8):
                    column = 3 * corner
                    strain[0, column] = deriv[0, corner]
                    strain[1, column + 1] = deriv[1, corner]
                    strain[2, column + 2] = deriv[2, corner]
                    strain[3, column] = deriv[1, corner]
                    strain[3, column + 1] = deriv[0, corner]
                    strain[4, column + 1] = deriv[2, corner]
                    strain[4, column + 2] = deriv[1, corner]
                    strain[5, column] = deriv[2, corner]
                    strain[5, column + 2] = deriv[0, corner]
                stiffness += 0.125 * strain.T @ elastic @ strain
                coupling += 0.125 * (strain[0] + strain[1] + strain[2])
    bulk = 1.0 / (3.0 * (1.0 - 2.0 * poisson))
    return (stiffness.astype(np.float32), coupling.astype(np.float32), float(bulk))

def cone_offsets():
    found = []
    for off_x in range(-3, 4):
        for off_y in range(-3, 4):
            for off_z in range(-3, 4):
                radius = math.sqrt(off_x * off_x + off_y * off_y + off_z * off_z)
                if radius < cone_radius:
                    found.append((off_x, off_y, off_z, cone_radius - radius))
    return found

def cone_sum(padded, count_x, count_y, count_z):
    total = jnp.zeros((count_x, count_y, count_z), jnp.float32)
    for off_x, off_y, off_z, weight in cone_offsets():
        piece = lax.slice(padded, (3 + off_x, 3 + off_y, 3 + off_z), (3 + off_x + count_x, 3 + off_y + count_y, 3 + off_z + count_z))
        total = total + jnp.float32(weight) * piece
    return total

def element_energy(forward_ext, adjoint_ext, pressure, multiplier, count_x, count_y, count_z):
    stiff_np, coup_np, bulk = element_tables()
    stiffness = jnp.asarray(stiff_np, jnp.float32)
    coupling = jnp.asarray(coup_np, jnp.float32)

    def gather_dofs(field):
        pieces = []
        for corner in range(8):
            bit_x, bit_y, bit_z = (corner & 1, corner >> 1 & 1, corner >> 2 & 1)
            pieces.append(field[:, bit_x:bit_x + count_x, bit_y:bit_y + count_y, bit_z:bit_z + count_z])
        return jnp.concatenate(pieces, 0)
    forward = gather_dofs(forward_ext)
    backward = gather_dofs(adjoint_ext)
    pushed = jnp.einsum('ij,jxyz->ixyz', stiffness, forward, precision=lax.Precision.HIGHEST)
    energy = lax.optimization_barrier(jnp.sum(backward * pushed, axis=0))
    energy = energy + jnp.einsum('j,jxyz->xyz', coupling, backward, precision=lax.Precision.HIGHEST) * pressure
    energy = energy + multiplier * jnp.einsum('j,jxyz->xyz', coupling, forward, precision=lax.Precision.HIGHEST)
    energy = energy - multiplier * pressure / jnp.float32(bulk)
    return energy

def projection(filtered, flags, energy, weight_total):
    denom = math.tanh(sharpness * threshold) + math.tanh(sharpness * (1.0 - threshold))
    hyper = jnp.tanh(sharpness * (filtered - threshold))
    smooth = (math.tanh(sharpness * threshold) + hyper) / denom
    deriv = sharpness * (1.0 - hyper * hyper) / denom
    active = flags >= 2
    projected = jnp.where(active, smooth, jnp.where(flags == 1, 1.0, 0.0)).astype(jnp.float32)
    slope = jnp.where(active, deriv, 0.0).astype(jnp.float32)
    return -3.0 * projected * projected * (1.0 - stiff_floor) * energy * slope / weight_total

def reference(design, flags, displacement, adjoint, pressure, multiplier):
    nodes = jnp.concatenate([displacement, adjoint], 0)
    nodes = jnp.pad(nodes, ((0, 0), (0, 1), (0, 1), (0, 1)))

    def block_energy(start):
        slab = lax.dynamic_slice_in_dim(nodes, start, 5, 1)
        press = lax.dynamic_slice_in_dim(pressure, start, 4, 0)
        mult = lax.dynamic_slice_in_dim(multiplier, start, 4, 0)
        return element_energy(slab[:3], slab[3:], press, mult, 4, NY, NZ)
    starts = (jnp.arange(NX // 4) * 4).astype(jnp.int32)
    energy = lax.map(block_energy, starts).reshape(NX, NY, NZ)
    ones_padded = jnp.pad(jnp.ones((NX, NY, NZ), jnp.float32), 3)
    weight_total = cone_sum(ones_padded, NX, NY, NZ)
    filtered = cone_sum(jnp.pad(design, 3), NX, NY, NZ) / weight_total
    chain = projection(filtered, flags, energy, weight_total)
    summed = cone_sum(jnp.pad(chain, 3), NX, NY, NZ)
    return jnp.where(flags >= 2, summed, 0.0).astype(jnp.float32)
```

```python
import functools
import itertools
import math

import jax
import jax.numpy as jnp
from jax import lax
from jax.experimental import pallas as pl
from jax.experimental.pallas import tpu as pltpu
from jax.sharding import PartitionSpec as P

poisson = 0.45
sharpness = 4.0
threshold = 0.5
stiff_floor = 0.001
cone_radius = 3.5

AXES = ("gx", "gy", "gz")
NX, NY, NZ = 8, 8, 256
MESH = pl.DeviceIdType.MESH
OFFSETS = sorted(
    (o for o in itertools.product((-1, 0, 1), repeat=3) if any(o)), key=lambda o: (-abs(o[0]), o)
)


def cone_weight(a, b, c):
    r2 = a * a + b * b + c * c
    return cone_radius - math.sqrt(r2) if r2 < cone_radius * cone_radius else 0.0


def place(grid):
    return [lax.axis_index(a) for a in AXES]


def peer(grid, offset):
    at = [lax.axis_index(a) for a in AXES]
    target = tuple(a + o for a, o in zip(at, offset))
    ok = None
    for t, o, n in zip(target, offset, grid):
        if o:
            inside = t >= 0 if o < 0 else t < n
            ok = inside if ok is None else ok & inside
    return target, ok


def opposite(offset):
    return tuple(-o for o in offset)


class Exchange:
    def __init__(self, grid, send, recv):
        self.grid, self.send, self.recv = grid, send, recv
        self.items = []

    def copy(self, index):
        offset, src, dst = self.items[index]
        target, ok = peer(self.grid, offset)
        return ok, pltpu.make_async_remote_copy(
            src_ref=src, dst_ref=dst, send_sem=self.send.at[index], recv_sem=self.recv.at[index],
            device_id=target, device_id_type=MESH,
        )

    def start(self, offset, src, dst):
        self.items.append((offset, src, dst))
        ok, copy = self.copy(len(self.items) - 1)
        pl.when(ok)(copy.start)

    def finish_recv(self, index):
        offset, src, dst = self.items[index]
        _, ok = peer(self.grid, opposite(offset))
        _, copy = self.copy(index)
        pl.when(ok)(copy.wait_recv)

        @pl.when(jnp.logical_not(ok))
        def _():
            dst[...] = jnp.zeros(dst.shape, jnp.float32)

    def finish_send(self, index):
        ok, copy = self.copy(index)
        pl.when(ok)(copy.wait_send)


def roll(value, by, axis):
    by = by % value.shape[axis]
    return value if by == 0 else pltpu.roll(value, by, axis)


def iota(shape, dim):
    return lax.broadcasted_iota(jnp.int32, shape, dim)


def cone_sum(vol, ysum, emit):
    row = iota((2, 8, 384), 1)

    def rows(p, _):
        at = pl.ds(2 * p, 2)
        low, high = vol[at, 0:8, :], vol[at, 8:16, :]
        for b in (1, 2, 3):
            up = roll(jnp.where(row < b, high, low), -b, 1)
            down = roll(jnp.where(row >= 8 - b, high, low), b, 1)
            ysum[b - 1, at] = up + down
        return 0

    lax.fori_loop(0, 7, rows, 0)
    lane = iota((2, 8, 128), 2)

    def planes(p, _):
        x = 2 * p
        sums = {}

        def get(b, k):
            return vol[pl.ds(x + k, 2), 0:8, :] if b == 0 else ysum[b - 1, pl.ds(x + k, 2)]

        for a in range(4):
            for b in range(4):
                if a * a + b * b < 12.25:
                    sums[a, b] = get(b, 3) if a == 0 else get(b, 3 - a) + get(b, 3 + a)
        groups = {}
        for (a, b), value in sums.items():
            key = (min(a, b), max(a, b))
            groups[key] = groups[key] + value if key in groups else value
        total = None
        for c in range(4):
            g = None
            for (a, b), value in groups.items():
                w = cone_weight(a, b, c)
                if w > 0:
                    g = value * w if g is None else g + value * w
            g0, g1, gh = g[:, :, 0:128], g[:, :, 128:256], g[:, :, 256:384]
            if c == 0:
                t0, t1 = g0, g1
            else:
                t0 = t0 + roll(jnp.where(lane < c, g1, g0), -c, 2) + roll(
                    jnp.where(lane >= 128 - c, gh, g0), c, 2)
                t1 = t1 + roll(jnp.where(lane < c, gh, g1), -c, 2) + roll(
                    jnp.where(lane >= 128 - c, g0, g1), c, 2)
        emit(x, t0, t1)
        return 0

    lax.fori_loop(0, 4, planes, 0)


def inverse_weight(grid, out):
    gx, gy, gz = [lax.axis_index(a) for a in AXES]
    y = gy * NY + iota((NY, NZ), 0)
    z = gz * NZ + iota((NY, NZ), 1)

    def pairs(pos, by, size):
        return (pos + by < size).astype(jnp.float32) + (pos - by >= 0).astype(jnp.float32)

    ys = [None] + [pairs(y, b, grid[1] * NY) for b in (1, 2, 3)]
    zs = [None] + [pairs(z, c, grid[2] * NZ) for c in (1, 2, 3)]
    fs = []
    for a in range(4):
        f = jnp.full((NY, NZ), 0.0, jnp.float32)
        for b in range(4):
            for c in range(4):
                w = cone_weight(a, b, c)
                if w > 0:
                    term = jnp.float32(w)
                    term = term if b == 0 else term * ys[b]
                    term = term if c == 0 else term * zs[c]
                    f = f + term
        fs.append(f)
    for x in range(NX):
        px = gx * NX + x
        w = fs[0]
        for a in (1, 2, 3):
            w = w + fs[a] * pairs(px, a, grid[0] * NX)
        out[x] = 1.0 / w


def assemble(vol, ybuf, edge, strip):
    row = iota((8, 256), 0)
    rowl = iota((8, 128), 0)
    lane = iota((8, 128), 1)
    for i in range(8):
        vol[3 + i, 8:16, 0:256] = jnp.where(row < 4, ybuf[0, i], ybuf[1, i])
    for k in range(3):
        vol[k, 8:16, 0:256] = jnp.where(row < 4, edge[0, 0, k], edge[0, 1, k])
        vol[11 + k, 8:16, 0:256] = jnp.where(row < 4, edge[1, 0, k], edge[1, 1, k])
    both = {}
    for dx in range(3):
        for dy in range(3):
            both[dx, dy] = jnp.where((lane & 15) < 12, strip[0, dx, dy], strip[1, dx, dy])
    for dx in range(3):
        main = both[dx, 1]
        side = jnp.where(rowl < 4, both[dx, 2], both[dx, 0])
        first, count, at = ((5, 3, 0), (0, 8, 3), (0, 3, 11))[dx]
        for k in range(count):
            vol[at + k, 0:8, 256:384] = roll(main, -16 * (first + k), 1)
            vol[at + k, 8:16, 256:384] = roll(side, -16 * (first + k), 1)
    return both


def send_volume(ex, vol, ybuf, edge, strip, pack):
    center = vol.at[pl.ds(3, 8), pl.ds(0, 8), pl.ds(0, 256)]
    low3 = vol.at[pl.ds(3, 3), pl.ds(0, 8), pl.ds(0, 256)]
    high3 = vol.at[pl.ds(8, 3), pl.ds(0, 8), pl.ds(0, 256)]
    for o in OFFSETS:
        dx, dy, dz = o
        if dz:
            ex.start(o, pack.at[0 if dz < 0 else 1], strip.at[0 if dz < 0 else 1, 1 - dx, 1 - dy])
        elif dx and dy:
            ex.start(o, low3 if dx < 0 else high3, edge.at[1 if dx < 0 else 0, 0 if dy < 0 else 1])
        elif dx:
            lands = pl.ds(11, 3) if dx < 0 else pl.ds(0, 3)
            ex.start(o, low3 if dx < 0 else high3, vol.at[lands, pl.ds(0, 8), pl.ds(0, 256)])
        else:
            ex.start(o, center, ybuf.at[0 if dy < 0 else 1])


def pack_strips(vol, pack, nodes):
    lane = iota((8, 128), 1)
    down, up = None, None
    for i in range(8):
        first, last = vol[3 + i, 0:8, 0:128], vol[3 + i, 0:8, 128:256]
        d, u = roll(first, 16 * i, 1), roll(last, 16 * i, 1)
        if i == 0:
            down, up = d, u
        else:
            down = jnp.where((lane >= 16 * i) & (lane < 16 * i + 3), d, down)
            up = jnp.where((lane >= 16 * i - 3) & (lane < 16 * i), u, up)
        if nodes is not None:
            for f in range(6):
                n = roll(nodes[f, i, :, 0:128], 16 * i + 3 + f, 1)
                down = jnp.where(lane == 16 * i + 3 + f, n, down)
    pack[0] = down
    pack[1] = up


def node_modes(nodes, rows, corner, both, modes):
    lane = iota((8, 128), 1)
    row = iota((8, 128), 0)
    for p in range(9):
        dx = 2 if p == 8 else 1
        base = 0 if p == 8 else 16 * p
        for f in range(6):
            n0, n1 = nodes[f, p, :, 0:128], nodes[f, p, :, 128:256]
            if p == 8:
                top = corner[f:f + 1, :]
            else:
                top = rows[f, p:p + 1, :]
            e0, e1 = top[:, 0:128], top[:, 128:256]
            h = roll(both[dx, 1], -(base + 3 + f), 1)
            eh = roll(both[dx, 2], -(base + 3 + f), 1)
            up = lambda v: roll(v, -1, 1)
            s0 = up(jnp.where(lane == 0, n1, n0))
            s1 = up(jnp.where(lane == 0, h, n1))
            m0 = roll(jnp.where(row == 0, jnp.broadcast_to(e0, (8, 128)), n0), -1, 0)
            m1 = roll(jnp.where(row == 0, jnp.broadcast_to(e1, (8, 128)), n1), -1, 0)
            mh = roll(jnp.where(row == 0, eh, h), -1, 0)
            q0 = up(jnp.where(lane == 0, m1, m0))
            q1 = up(jnp.where(lane == 0, mh, m1))
            for half, (n, s, m, q) in enumerate(((n0, s0, m0, q0), (n1, s1, m1, q1))):
                a, d = n + s, s - n
                ay, dy = m + q, q - m
                at = pl.ds(128 * half, 128)
                modes[p, f, 0, :, at] = a + ay
                modes[p, f, 1, :, at] = d + dy
                modes[p, f, 2, :, at] = ay - a
                modes[p, f, 3, :, at] = dy - d


def element_energy(modes, x, press, mult):
    shear = 1.0 / (2.0 * (1.0 + poisson))
    bulk = 1.0 / (3.0 * (1.0 - 2.0 * poisson))

    def both_of(f, m):
        return modes[x, f, m], modes[x + 1, f, m]

    def field(base):
        out = []
        for c in range(3):
            aa, ad, da, dd = (both_of(base + c, m) for m in range(4))
            out.append(dict(
                X=aa[1] - aa[0], Y=da[0] + da[1], Z=ad[0] + ad[1],
                XY=da[1] - da[0], XZ=ad[1] - ad[0], YZ=dd[0] + dd[1], XYZ=dd[1] - dd[0]))
        return out

    u, l = field(0), field(3)

    def strains(v):
        a, b, c = v
        one = (a["X"], b["Y"], c["Z"], a["Y"] + b["X"], b["Z"] + c["Y"], a["Z"] + c["X"])
        xi = (None, b["XY"], c["XZ"], a["XY"], b["XZ"] + c["XY"], a["XZ"])
        eta = (a["XY"], None, c["YZ"], b["XY"], b["YZ"], a["YZ"] + c["XY"])
        zeta = (a["XZ"], b["YZ"], None, a["YZ"] + b["XZ"], c["YZ"], c["XZ"])
        return one, xi, eta, zeta

    su, sl = strains(u), strains(l)
    total = None
    for kind in range(4):
        eu, el = su[kind], sl[kind]
        normal, tr_u, tr_l = None, None, None
        for k in range(3):
            if eu[k] is not None:
                t = eu[k] * el[k]
                normal = t if normal is None else normal + t
                tr_u = eu[k] if tr_u is None else tr_u + eu[k]
                tr_l = el[k] if tr_l is None else tr_l + el[k]
        gamma = eu[3] * el[3] + eu[4] * el[4] + eu[5] * el[5]
        scale = shear / 16.0 if kind == 0 else shear / 48.0
        part = (2.0 * (normal - tr_u * tr_l * (1.0 / 3.0)) + gamma) * scale
        if kind == 0:
            div_u, div_l = tr_u * 0.25, tr_l * 0.25
        total = part if total is None else total + part
    pure = u[0]["XYZ"] * l[0]["XYZ"] + u[1]["XYZ"] * l[1]["XYZ"] + u[2]["XYZ"] * l[2]["XYZ"]
    total = total + pure * (shear * (10.0 / 3.0) / 144.0)
    return total + div_l * press + mult * div_u - mult * press * (1.0 / bulk)


def kernel(grid, design, flags, disp, adj, press, mult, out,
           vol, vol2, ysum, ybuf, edge, strip, ybuf2, edge2, strip2, pack, pack2,
           nodes, node_rows, rows_in, node_corner, corner_in, modes,
           fl, pr, mu, inv, energy, load_sem, send1, recv1, send2, recv2):
    barrier = pltpu.get_barrier_semaphore()
    count = jnp.int32(0)
    for o in OFFSETS:
        target, ok = peer(grid, o)

        @pl.when(ok)
        def _():
            pl.semaphore_signal(barrier, inc=1, device_id=target, device_id_type=MESH)

        count = count + ok.astype(jnp.int32)

    loads = [
        (design, vol.at[pl.ds(3, 8), pl.ds(0, 8), pl.ds(0, 256)]),
        (disp, nodes.at[pl.ds(0, 3), pl.ds(0, 8)]),
        (adj, nodes.at[pl.ds(3, 3), pl.ds(0, 8)]),
        (flags, fl), (press, pr), (mult, mu),
    ]
    loads = [pltpu.make_async_copy(s, d, load_sem.at[k]) for k, (s, d) in enumerate(loads)]
    for c in loads:
        c.start()
    inverse_weight(grid, inv)
    for c in loads:
        c.wait()
    pack_strips(vol, pack, nodes)
    for f in range(6):
        for i in range(8):
            node_rows[f, i:i + 1, :] = nodes[f, i, 0:1, :]
        node_corner[f:f + 1, :] = nodes[f, 0, 0:1, :]
    node_corner[6:8, :] = jnp.zeros((2, 256), jnp.float32)
    pl.semaphore_wait(barrier, count)

    ex = Exchange(grid, send1, recv1)
    send_volume(ex, vol, ybuf, edge, strip, pack)
    ex.start((-1, 0, 0), nodes.at[:, 0], nodes.at[:, 8])
    ex.start((-1, -1, 0), node_corner, corner_in)
    ex.start((0, -1, 0), node_rows, rows_in)
    for k in range(len(ex.items)):
        ex.finish_recv(k)
    both = assemble(vol, ybuf, edge, strip)
    node_modes(nodes, rows_in, corner_in, both, modes)

    def energies(x, _):
        energy[x] = element_energy(modes, x, pr[x], mu[x])
        return 0

    lax.fori_loop(0, 8, energies, 0)

    denom = math.tanh(sharpness * threshold) + math.tanh(sharpness * (1.0 - threshold))
    base = math.tanh(sharpness * threshold)

    def chain(x, t0, t1):
        for half, t in enumerate((t0, t1)):
            at = pl.ds(128 * half, 128)
            planes = pl.ds(x, 2)
            w = inv[planes, :, at]
            hyper = jnp.tanh(sharpness * (t * w - threshold))
            smooth = (base + hyper) * (1.0 / denom)
            slope = (1.0 - hyper * hyper) * (sharpness / denom)
            value = smooth * smooth * slope * (energy[planes, :, at] * w) * (-3.0 * (1.0 - stiff_floor))
            vol2[pl.ds(x + 3, 2), 0:8, at] = jnp.where(fl[planes, :, at] >= 2, value, 0.0)

    cone_sum(vol, ysum, chain)
    pack_strips(vol2, pack2, None)
    ex2 = Exchange(grid, send2, recv2)
    send_volume(ex2, vol2, ybuf2, edge2, strip2, pack2)
    for k in range(len(ex2.items)):
        ex2.finish_recv(k)
    assemble(vol2, ybuf2, edge2, strip2)

    def final(x, t0, t1):
        planes = pl.ds(x, 2)
        for half, t in enumerate((t0, t1)):
            at = pl.ds(128 * half, 128)
            out[planes, :, at] = jnp.where(fl[planes, :, at] >= 2, t, 0.0)

    cone_sum(vol2, ysum, final)
    for k in range(len(ex.items)):
        ex.finish_send(k)
    for k in range(len(ex2.items)):
        ex2.finish_send(k)


def on_device(grid, *args):
    f32, i32 = jnp.float32, jnp.int32
    V = pltpu.VMEM
    vol = V((14, 16, 384), f32)
    ybuf, edge, strip, pack = V((2, 8, 8, 256), f32), V((2, 2, 3, 8, 256), f32), V((2, 3, 3, 8, 128), f32), V((2, 8, 128), f32)
    brick = V((8, 8, 256), f32)
    dma = pltpu.SemaphoreType.DMA
    return pl.pallas_call(
        functools.partial(kernel, grid),
        out_shape=jax.ShapeDtypeStruct((8, 8, 256), f32),
        in_specs=[pl.BlockSpec(memory_space=pl.ANY)] * 6,
        out_specs=pl.BlockSpec(memory_space=pltpu.VMEM),
        scratch_shapes=[
            vol, vol, V((3, 14, 8, 384), f32), ybuf, edge, strip, ybuf, edge, strip, pack, pack,
            V((6, 9, 8, 256), f32), V((6, 8, 256), f32), V((6, 8, 256), f32), V((8, 256), f32), V((8, 256), f32),
            V((9, 6, 4, 8, 256), f32),
            V((8, 8, 256), i32), brick, brick, brick, brick,
            dma((6,)), dma((29,)), dma((29,)), dma((26,)), dma((26,)),
        ],
        compiler_params=pltpu.CompilerParams(
            collective_id=0, has_side_effects=True, vmem_limit_bytes=32 << 20),
        name="sensitivity",
    )(*args)


def solution(mesh):
    grid = tuple(mesh.shape[a] for a in AXES)
    brick = P("gx", "gy", "gz")
    field = P(None, "gx", "gy", "gz")
    return jax.shard_map(
        functools.partial(on_device, grid), mesh=mesh,
        in_specs=(brick, brick, field, field, brick, brick), out_specs=brick, check_vma=False,
    )
```

```python
import functools
import itertools
import math

import jax
import jax.numpy as jnp
from jax import lax
from jax.experimental import pallas as pl
from jax.experimental.pallas import tpu as pltpu
from jax.sharding import PartitionSpec as P

poisson = 0.45
sharpness = 4.0
threshold = 0.5
stiff_floor = 0.001
cone_radius = 3.5

AXES = ("gx", "gy", "gz")
NX, NY, NZ = 8, 8, 256
MESH = pl.DeviceIdType.MESH
NEAR = [(0, 0, 1), (0, 0, -1), (0, 1, 1), (0, -1, 1), (0, 1, -1), (0, -1, -1), (0, 1, 0), (0, -1, 0)]
OFFSETS = [(-1, 0, 0), (1, 0, 0)] + NEAR
COEF = -3.0 * (1.0 - stiff_floor)


def cone_weight(a, b, c):
    r2 = a * a + b * b + c * c
    return cone_radius - math.sqrt(r2) if r2 < cone_radius * cone_radius else 0.0


def place(grid):
    return [lax.axis_index(a) for a in AXES]


def peer(grid, offset):
    at = [lax.axis_index(a) for a in AXES]
    target = tuple(a + o for a, o in zip(at, offset))
    ok = None
    for t, o, n in zip(target, offset, grid):
        if o:
            inside = t >= 0 if o < 0 else t < n
            ok = inside if ok is None else ok & inside
    return target, ok


def opposite(offset):
    return tuple(-o for o in offset)


class Exchange:
    def __init__(self, grid, send, recv):
        self.grid, self.send, self.recv = grid, send, recv
        self.items = []

    def copy(self, index):
        offset, src, dst = self.items[index]
        target, ok = peer(self.grid, offset)
        return ok, pltpu.make_async_remote_copy(
            src_ref=src, dst_ref=dst, send_sem=self.send.at[index], recv_sem=self.recv.at[index],
            device_id=target, device_id_type=MESH,
        )

    def start(self, offset, src, dst):
        self.items.append((offset, src, dst))
        ok, copy = self.copy(len(self.items) - 1)
        pl.when(ok)(copy.start)

    def finish_recv(self, index):
        offset, src, dst = self.items[index]
        _, ok = peer(self.grid, opposite(offset))
        _, copy = self.copy(index)
        pl.when(ok)(copy.wait_recv)

        @pl.when(jnp.logical_not(ok))
        def _():
            dst[...] = jnp.zeros(dst.shape, jnp.float32)

    def finish_send(self, index):
        ok, copy = self.copy(index)
        pl.when(ok)(copy.wait_send)


def roll(value, by, axis):
    by = by % value.shape[axis]
    return value if by == 0 else pltpu.roll(value, by, axis)


def iota(shape, dim):
    return lax.broadcasted_iota(jnp.int32, shape, dim)


def cone_sum(vol, ysum, emit):
    row = iota((2, 8, 384), 1)

    def rows(p, _):
        at = pl.ds(2 * p, 2)
        low, high = vol[at, 0:8, :], vol[at, 8:16, :]
        for b in (1, 2, 3):
            up = roll(jnp.where(row < b, high, low), -b, 1)
            down = roll(jnp.where(row >= 8 - b, high, low), b, 1)
            ysum[b - 1, at] = up + down
        return 0

    lax.fori_loop(0, 7, rows, 0)
    lane = iota((2, 8, 128), 2)

    def planes(p, _):
        x = 2 * p
        sums = {}

        def get(b, k):
            return vol[pl.ds(x + k, 2), 0:8, :] if b == 0 else ysum[b - 1, pl.ds(x + k, 2)]

        for a in range(4):
            for b in range(4):
                if a * a + b * b < 12.25:
                    sums[a, b] = get(b, 3) if a == 0 else get(b, 3 - a) + get(b, 3 + a)
        groups = {}
        for (a, b), value in sums.items():
            key = (min(a, b), max(a, b))
            groups[key] = groups[key] + value if key in groups else value
        total = None
        for c in range(4):
            g = None
            for (a, b), value in groups.items():
                w = cone_weight(a, b, c)
                if w > 0:
                    g = value * w if g is None else g + value * w
            g0, g1, gh = g[:, :, 0:128], g[:, :, 128:256], g[:, :, 256:384]
            if c == 0:
                t0, t1 = g0, g1
            else:
                t0 = t0 + roll(jnp.where(lane < c, g1, g0), -c, 2) + roll(
                    jnp.where(lane >= 128 - c, gh, g0), c, 2)
                t1 = t1 + roll(jnp.where(lane < c, gh, g1), -c, 2) + roll(
                    jnp.where(lane >= 128 - c, g0, g1), c, 2)
        emit(x, t0, t1)
        return 0

    lax.fori_loop(0, 4, planes, 0)


def inverse_weight(grid, out):
    gx, gy, gz = [lax.axis_index(a) for a in AXES]
    y = gy * NY + iota((NY, NZ), 0)
    z = gz * NZ + iota((NY, NZ), 1)

    def pairs(pos, by, size):
        def inside(v):
            return ((v >= 0) & (v < size)).astype(jnp.float32)
        return inside(pos + by) + inside(pos - by) if by else inside(pos)

    ys = [None] + [pairs(y, b, grid[1] * NY) for b in (1, 2, 3)]
    zs = [None] + [pairs(z, c, grid[2] * NZ) for c in (1, 2, 3)]
    fs = []
    for a in range(4):
        f = jnp.full((NY, NZ), 0.0, jnp.float32)
        for b in range(4):
            for c in range(4):
                w = cone_weight(a, b, c)
                if w > 0:
                    term = jnp.float32(w)
                    term = term if b == 0 else term * ys[b]
                    term = term if c == 0 else term * zs[c]
                    f = f + term
        fs.append(f)
    for k in range(14):
        px = gx * NX + k - 3
        w = fs[0] * pairs(px, 0, grid[0] * NX)
        for a in (1, 2, 3):
            w = w + fs[a] * pairs(px, a, grid[0] * NX)
        out[k] = 1.0 / w


def pack_rows(vol, first, half, rows):
    row = iota((8, 256), 0)
    for k in range(half):
        a, b = vol[first + k, 0:8, 0:256], vol[first + half + k, 0:8, 0:256]
        b = roll(b, 4, 0)
        rows[0, k] = jnp.where(row < 4, a, b)
        rows[1, k] = jnp.where(row < 4, b, a)


def pack_strips(vol, planes, slot, pack, nodes):
    lane = iota((8, 128), 1)
    down, up = None, None
    for i in range(planes):
        first, last = vol[i, 0:8, 0:128], vol[i, 0:8, 128:256]
        d, u = roll(first, slot * i, 1), roll(last, slot * i, 1)
        if i == 0:
            down, up = d, u
        else:
            down = jnp.where((lane >= slot * i) & (lane < slot * i + 3), d, down)
            up = jnp.where((lane >= slot * i - 3) & (lane < slot * i), u, up)
        if nodes is not None:
            for f in range(6):
                n = roll(nodes[f, 1 + i, :, 0:128], slot * i + 3 + f, 1)
                down = jnp.where(lane == slot * i + 3 + f, n, down)
    pack[0] = down
    pack[1] = up


def send_near(ex, rows, pack, rows_in, strip):
    for o in NEAR:
        _, dy, dz = o
        if dz:
            k = 0 if dz < 0 else 1
            ex.start(o, pack.at[k], strip.at[k, 1 - dy])
        else:
            k = 0 if dy < 0 else 1
            ex.start(o, rows.at[k], rows_in.at[k])


def assemble(vol, half, slot, rows_in, strip):
    row = iota((8, 256), 0)
    rowl = iota((8, 128), 0)
    lane = iota((8, 128), 1)
    for k in range(half):
        from_upper, from_lower = rows_in[0, k], rows_in[1, k]
        vol[k, 8:16, 0:256] = jnp.where(row < 4, from_upper, from_lower)
        vol[half + k, 8:16, 0:256] = roll(jnp.where(row < 4, from_lower, from_upper), 4, 0)
    both = [jnp.where((lane & (slot - 1)) < slot - 4, strip[0, dy], strip[1, dy]) for dy in range(3)]
    side = jnp.where(rowl < 4, both[2], both[0])
    for k in range(2 * half):
        vol[k, 0:8, 256:384] = roll(both[1], -slot * k, 1)
        vol[k, 8:16, 256:384] = roll(side, -slot * k, 1)
    return both[1], both[2]


def plane_sums(vol, fs, psum):
    row = iota((8, 384), 0)
    lane = iota((8, 128), 1)

    def shifts(t, c):
        t0, t1, th = t[:, 0:128], t[:, 128:256], t[:, 256:384]
        u0 = roll(jnp.where(lane < c, t1, t0), -c, 1) + roll(jnp.where(lane >= 128 - c, th, t0), c, 1)
        u1 = roll(jnp.where(lane < c, th, t1), -c, 1) + roll(jnp.where(lane >= 128 - c, t0, t1), c, 1)
        return u0, u1

    def plane(p, _):
        low, high = vol[p, 0:8, :], vol[p, 8:16, :]
        ys = [low]
        for b in (1, 2, 3):
            up = roll(jnp.where(row < b, high, low), -b, 0)
            down = roll(jnp.where(row >= 8 - b, high, low), b, 0)
            ys.append(up + down)
        groups = {}
        for b in range(4):
            for c in range(4):
                if b * b + c * c < 12.25:
                    v = (ys[b][:, 0:128], ys[b][:, 128:256]) if c == 0 else shifts(ys[b], c)
                    key = (min(b, c), max(b, c))
                    groups[key] = tuple(s + t for s, t in zip(groups[key], v)) if key in groups else v
        for a in range(4):
            for half in range(2):
                f = None
                for (b, c), v in groups.items():
                    w = cone_weight(a, b, c)
                    if w > 0:
                        f = v[half] * w if f is None else f + v[half] * w
                fs[a, p, :, pl.ds(128 * half, 128)] = f
        return 0

    lax.fori_loop(0, 8, plane, 0)
    for k in range(14):
        total = None
        for a in range(-3, 4):
            p = k - 3 + a
            if 0 <= p < 8:
                total = fs[abs(a), p] if total is None else total + fs[abs(a), p]
        psum[k] = total


def node_halo(halo, main, side):
    lane = iota((8, 128), 1)
    for p in range(8):
        a = roll(main, -(16 * p + 3), 1)
        b = roll(roll(side, -(16 * p + 3) + 8, 1), -1, 0)
        halo[1 + p, :, 256:384] = jnp.where(lane < 8, a, b)


def node_modes(nodes, halo, modes, q):
    lane = iota((8, 128), 1)
    row = iota((8, 128), 0)
    hs = halo[q, :, 256:384]
    hm = jnp.where(row == 7, roll(hs, -8, 1), roll(hs, -1, 0))
    for f in range(6):
        n = [nodes[f, q, :, 0:128], nodes[f, q, :, 128:256]]
        e = [halo[q, f:f + 1, 0:128], halo[q, f:f + 1, 128:256]]
        m = [jnp.where(row == 7, jnp.broadcast_to(e[k], (8, 128)), roll(n[k], -1, 0)) for k in range(2)]

        def up(v, h):
            v0, v1 = roll(v[0], -1, 1), roll(v[1], -1, 1)
            return jnp.where(lane == 127, v1, v0), jnp.where(lane == 127, roll(h, 127 - f, 1), v1)

        s, r = up(n, hs), up(m, hm)
        for k in range(2):
            a, d = n[k] + s[k], s[k] - n[k]
            ay, dy = m[k] + r[k], r[k] - m[k]
            at = pl.ds(128 * k, 128)
            modes[q, f, 0, :, at] = a + ay
            modes[q, f, 1, :, at] = d + dy
            modes[q, f, 2, :, at] = ay - a
            modes[q, f, 3, :, at] = dy - d


def element_energy(modes, x, press, mult):
    shear = 1.0 / (2.0 * (1.0 + poisson))
    bulk = 1.0 / (3.0 * (1.0 - 2.0 * poisson))

    def both_of(f, m):
        return modes[x, f, m], modes[x + 1, f, m]

    def field(base):
        out = []
        for c in range(3):
            aa, ad, da, dd = (both_of(base + c, m) for m in range(4))
            out.append(dict(
                X=aa[1] - aa[0], Y=da[0] + da[1], Z=ad[0] + ad[1],
                XY=da[1] - da[0], XZ=ad[1] - ad[0], YZ=dd[0] + dd[1], XYZ=dd[1] - dd[0]))
        return out

    u, l = field(0), field(3)

    def strains(v):
        a, b, c = v
        one = (a["X"], b["Y"], c["Z"], a["Y"] + b["X"], b["Z"] + c["Y"], a["Z"] + c["X"])
        xi = (None, b["XY"], c["XZ"], a["XY"], b["XZ"] + c["XY"], a["XZ"])
        eta = (a["XY"], None, c["YZ"], b["XY"], b["YZ"], a["YZ"] + c["XY"])
        zeta = (a["XZ"], b["YZ"], None, a["YZ"] + b["XZ"], c["YZ"], c["XZ"])
        return one, xi, eta, zeta

    su, sl = strains(u), strains(l)
    total = None
    for kind in range(4):
        eu, el = su[kind], sl[kind]
        normal, tr_u, tr_l = None, None, None
        for k in range(3):
            if eu[k] is not None:
                t = eu[k] * el[k]
                normal = t if normal is None else normal + t
                tr_u = eu[k] if tr_u is None else tr_u + eu[k]
                tr_l = el[k] if tr_l is None else tr_l + el[k]
        gamma = eu[3] * el[3] + eu[4] * el[4] + eu[5] * el[5]
        scale = shear / 16.0 if kind == 0 else shear / 48.0
        part = (2.0 * (normal - tr_u * tr_l * (1.0 / 3.0)) + gamma) * scale
        if kind == 0:
            div_u, div_l = tr_u * 0.25, tr_l * 0.25
        total = part if total is None else total + part
    pure = u[0]["XYZ"] * l[0]["XYZ"] + u[1]["XYZ"] * l[1]["XYZ"] + u[2]["XYZ"] * l[2]["XYZ"]
    total = total + pure * (shear * (10.0 / 3.0) / 144.0)
    return total + div_l * press + mult * div_u - mult * press * (1.0 / bulk)


def kernel(grid, design, flags, disp, adj, press, mult, out,
           vol, vol2, fs, ysum, psum, sums_in, rows, rows_in, strip, pack, rows2, rows_in2, strip2, pack2,
           nodes, node_rows, halo, modes, aux, fl, inv, energy,
           load_sem, send1, recv1, send2, recv2, send3, recv3):
    barrier = pltpu.get_barrier_semaphore()
    count = jnp.int32(0)
    for o in OFFSETS:
        target, ok = peer(grid, o)

        @pl.when(ok)
        def _():
            pl.semaphore_signal(barrier, inc=1, device_id=target, device_id_type=MESH)

        count = count + ok.astype(jnp.int32)

    own = pl.ds(1, 8)
    loads = [
        (design, vol.at[:, pl.ds(0, 8), pl.ds(0, 256)]),
        (disp, nodes.at[pl.ds(0, 3), own]),
        (adj, nodes.at[pl.ds(3, 3), own]),
        (flags, fl), (press, aux.at[own, 0]), (mult, aux.at[own, 1]),
    ]
    loads = [pltpu.make_async_copy(s, d, load_sem.at[k]) for k, (s, d) in enumerate(loads)]
    for c in loads:
        c.start()
    inverse_weight(grid, inv)
    for c in loads:
        c.wait()
    for x in range(8):
        aux[1 + x, 2] = jnp.where(fl[x] >= 2, inv[3 + x] * COEF, 0.0)
    pack_strips(vol, 8, 16, pack, nodes)
    pack_rows(vol, 0, 4, rows)
    for p in range(8):
        for f in range(6):
            node_rows[p, f:f + 1, :] = nodes[f, 1 + p, 0:1, :]
        node_rows[p, 6:8, :] = jnp.zeros((2, 256), jnp.float32)
    pl.semaphore_wait(barrier, count)

    lower, upper = (-1, 0, 0), (1, 0, 0)
    far = Exchange(grid, send2, recv2)
    far.start(lower, nodes.at[:, 1], nodes.at[:, 9])
    far.start(upper, nodes.at[:, 8], nodes.at[:, 0])
    far.start(upper, aux.at[8], aux.at[0])
    near = Exchange(grid, send1, recv1)
    send_near(near, rows, pack, rows_in, strip)
    near.start((0, -1, 0), node_rows, halo.at[own, :, pl.ds(0, 256)])
    for k in range(9):
        near.finish_recv(k)

    main, side = assemble(vol, 4, 16, rows_in, strip)
    plane_sums(vol, fs, psum)
    far.start(lower, psum.at[pl.ds(0, 6)], sums_in.at[1])
    far.start(upper, psum.at[pl.ds(8, 6)], sums_in.at[0])
    node_halo(halo, main, side)
    far.start(lower, halo.at[1], halo.at[9])
    far.start(upper, halo.at[8], halo.at[0])

    def own_modes(q, _):
        node_modes(nodes, halo, modes, q)
        return 0

    lax.fori_loop(1, 9, own_modes, 0)

    def scaled(x):
        return element_energy(modes, x + 1, aux[x + 1, 0], aux[x + 1, 1]) * aux[x + 1, 2]

    def energies(x, _):
        energy[x + 3] = scaled(x)
        return 0

    lax.fori_loop(0, 7, energies, 0)
    far.start(lower, energy.at[pl.ds(3, 3)], energy.at[pl.ds(11, 3)])
    far.start(upper, energy.at[pl.ds(8, 2)], energy.at[pl.ds(0, 2)])
    for k in (0, 1, 2, 5, 6):
        far.finish_recv(k)
    for q in (0, 9):
        node_modes(nodes, halo, modes, q)
    for x in (-1, 7):
        energy[x + 3] = scaled(x)
    for k in (3, 4, 7, 8):
        far.finish_recv(k)

    denom = math.tanh(sharpness * threshold) + math.tanh(sharpness * (1.0 - threshold))
    base = math.tanh(sharpness * threshold)
    for k in range(14):
        total = psum[k]
        if k < 6:
            total = total + sums_in[0, k]
        if k >= 8:
            total = total + sums_in[1, k - 8]
        hyper = jnp.tanh(sharpness * (total * inv[k] - threshold))
        smooth = (base + hyper) * (1.0 / denom)
        slope = (1.0 - hyper * hyper) * (sharpness / denom)
        vol2[k, 0:8, 0:256] = smooth * smooth * slope * energy[k]

    pack_strips(vol2, 14, 8, pack2, None)
    pack_rows(vol2, 0, 7, rows2)
    last = Exchange(grid, send3, recv3)
    send_near(last, rows2, pack2, rows_in2, strip2)
    for k in range(8):
        last.finish_recv(k)
    assemble(vol2, 7, 8, rows_in2, strip2)

    def final(x, t0, t1):
        planes = pl.ds(x, 2)
        for half, t in enumerate((t0, t1)):
            at = pl.ds(128 * half, 128)
            out[planes, :, at] = jnp.where(fl[planes, :, at] >= 2, t, 0.0)

    cone_sum(vol2, ysum, final)
    for ex in (near, far, last):
        for k in range(len(ex.items)):
            ex.finish_send(k)


def on_device(grid, *args):
    f32, i32 = jnp.float32, jnp.int32
    V = pltpu.VMEM
    dma = pltpu.SemaphoreType.DMA
    strip, pack = V((2, 3, 8, 128), f32), V((2, 8, 128), f32)
    return pl.pallas_call(
        functools.partial(kernel, grid),
        out_shape=jax.ShapeDtypeStruct((8, 8, 256), f32),
        in_specs=[pl.BlockSpec(memory_space=pl.ANY)] * 6,
        out_specs=pl.BlockSpec(memory_space=pltpu.VMEM),
        scratch_shapes=[
            V((8, 16, 384), f32), V((14, 16, 384), f32), V((4, 8, 8, 256), f32), V((3, 14, 8, 384), f32),
            V((14, 8, 256), f32), V((2, 6, 8, 256), f32),
            V((2, 4, 8, 256), f32), V((2, 4, 8, 256), f32), strip, pack,
            V((2, 7, 8, 256), f32), V((2, 7, 8, 256), f32), strip, pack,
            V((6, 10, 8, 256), f32), V((8, 8, 256), f32), V((10, 8, 384), f32), V((10, 6, 4, 8, 256), f32),
            V((9, 3, 8, 256), f32), V((8, 8, 256), i32), V((14, 8, 256), f32), V((14, 8, 256), f32),
            dma((6,)), dma((9,)), dma((9,)), dma((9,)), dma((9,)), dma((8,)), dma((8,)),
        ],
        compiler_params=pltpu.CompilerParams(
            collective_id=0, has_side_effects=True, vmem_limit_bytes=63 << 20),
        name="sensitivity",
    )(*args)


def solution(mesh):
    grid = tuple(mesh.shape[a] for a in AXES)
    brick = P("gx", "gy", "gz")
    field = P(None, "gx", "gy", "gz")
    return jax.shard_map(
        functools.partial(on_device, grid), mesh=mesh,
        in_specs=(brick, brick, field, field, brick, brick), out_specs=brick, check_vma=False,
    )
```

```python
import functools
import itertools
import math

import jax
import jax.numpy as jnp
from jax import lax
from jax.experimental import pallas as pl
from jax.experimental.pallas import tpu as pltpu
from jax.sharding import PartitionSpec as P

poisson = 0.45
sharpness = 4.0
threshold = 0.5
stiff_floor = 0.001
cone_radius = 3.5

AXES = ("gx", "gy", "gz")
NX, NY, NZ = 8, 8, 256
MESH = pl.DeviceIdType.MESH
NEAR = [(0, 0, 1), (0, 0, -1), (0, 1, 1), (0, -1, 1), (0, 1, -1), (0, -1, -1), (0, 1, 0), (0, -1, 0)]
COEF = -3.0 * (1.0 - stiff_floor)


def cone_weight(a, b, c):
    r2 = a * a + b * b + c * c
    return cone_radius - math.sqrt(r2) if r2 < cone_radius * cone_radius else 0.0


def place(grid):
    return [lax.axis_index(a) for a in AXES]


def peer(grid, offset):
    at = [lax.axis_index(a) for a in AXES]
    target = tuple(a + o for a, o in zip(at, offset))
    ok = None
    for t, o, n in zip(target, offset, grid):
        if o:
            inside = t >= 0 if o < 0 else t < n
            ok = inside if ok is None else ok & inside
    return target, ok


def opposite(offset):
    return tuple(-o for o in offset)


class Exchange:
    def __init__(self, grid, send, recv):
        self.grid, self.send, self.recv = grid, send, recv
        self.items = []

    def copy(self, index):
        offset, src, dst = self.items[index]
        target, ok = peer(self.grid, offset)
        return ok, pltpu.make_async_remote_copy(
            src_ref=src, dst_ref=dst, send_sem=self.send.at[index], recv_sem=self.recv.at[index],
            device_id=target, device_id_type=MESH,
        )

    def start(self, offset, src, dst):
        self.items.append((offset, src, dst))
        ok, copy = self.copy(len(self.items) - 1)
        pl.when(ok)(copy.start)

    def finish_recv(self, index):
        offset, src, dst = self.items[index]
        _, ok = peer(self.grid, opposite(offset))
        _, copy = self.copy(index)
        pl.when(ok)(copy.wait_recv)

        @pl.when(jnp.logical_not(ok))
        def _():
            dst[...] = jnp.zeros(dst.shape, jnp.float32)

    def finish_send(self, index):
        ok, copy = self.copy(index)
        pl.when(ok)(copy.wait_send)


def roll(value, by, axis):
    by = by % value.shape[axis]
    return value if by == 0 else pltpu.roll(value, by, axis)


def iota(shape, dim):
    return lax.broadcasted_iota(jnp.int32, shape, dim)


def cone_sum(vol, ysum, emit):
    row = iota((2, 8, 384), 1)

    def rows(p, _):
        at = pl.ds(2 * p, 2)
        low, high = vol[at, 0:8, :], vol[at, 8:16, :]
        for b in (1, 2, 3):
            up = roll(jnp.where(row < b, high, low), -b, 1)
            down = roll(jnp.where(row >= 8 - b, high, low), b, 1)
            ysum[b - 1, at] = up + down
        return 0

    lax.fori_loop(0, 7, rows, 0)
    lane = iota((2, 8, 128), 2)

    def planes(p, _):
        x = 2 * p
        sums = {}

        def get(b, k):
            return vol[pl.ds(x + k, 2), 0:8, :] if b == 0 else ysum[b - 1, pl.ds(x + k, 2)]

        for a in range(4):
            for b in range(4):
                if a * a + b * b < 12.25:
                    sums[a, b] = get(b, 3) if a == 0 else get(b, 3 - a) + get(b, 3 + a)
        groups = {}
        for (a, b), value in sums.items():
            key = (min(a, b), max(a, b))
            groups[key] = groups[key] + value if key in groups else value
        total = None
        for c in range(4):
            g = None
            for (a, b), value in groups.items():
                w = cone_weight(a, b, c)
                if w > 0:
                    g = value * w if g is None else g + value * w
            g0, g1, gh = g[:, :, 0:128], g[:, :, 128:256], g[:, :, 256:384]
            if c == 0:
                t0, t1 = g0, g1
            else:
                t0 = t0 + roll(jnp.where(lane < c, g1, g0), -c, 2) + roll(
                    jnp.where(lane >= 128 - c, gh, g0), c, 2)
                t1 = t1 + roll(jnp.where(lane < c, gh, g1), -c, 2) + roll(
                    jnp.where(lane >= 128 - c, g0, g1), c, 2)
        emit(x, t0, t1)
        return 0

    lax.fori_loop(0, 4, planes, 0)


def inverse_weight(grid, out):
    gx, gy, gz = [lax.axis_index(a) for a in AXES]
    y = gy * NY + iota((NY, NZ), 0)
    z = gz * NZ + iota((NY, NZ), 1)

    def pairs(pos, by, size):
        def inside(v):
            return ((v >= 0) & (v < size)).astype(jnp.float32)
        return inside(pos + by) + inside(pos - by) if by else inside(pos)

    ys = [None] + [pairs(y, b, grid[1] * NY) for b in (1, 2, 3)]
    zs = [None] + [pairs(z, c, grid[2] * NZ) for c in (1, 2, 3)]
    fs = []
    for a in range(4):
        f = jnp.full((NY, NZ), 0.0, jnp.float32)
        for b in range(4):
            for c in range(4):
                w = cone_weight(a, b, c)
                if w > 0:
                    term = jnp.float32(w)
                    term = term if b == 0 else term * ys[b]
                    term = term if c == 0 else term * zs[c]
                    f = f + term
        fs.append(f)
    for k in range(14):
        px = gx * NX + k - 3
        w = fs[0] * pairs(px, 0, grid[0] * NX)
        for a in (1, 2, 3):
            w = w + fs[a] * pairs(px, a, grid[0] * NX)
        out[k] = 1.0 / w


def pack_rows(vol, first, half, rows):
    row = iota((8, 256), 0)
    for k in range(half):
        a, b = vol[first + k, 0:8, 0:256], vol[first + half + k, 0:8, 0:256]
        b = roll(b, 4, 0)
        rows[0, k] = jnp.where(row < 4, a, b)
        rows[1, k] = jnp.where(row < 4, b, a)


def pack_strips(vol, planes, slot, pack, nodes):
    lane = iota((8, 128), 1)
    down, up = None, None
    for i in range(planes):
        first, last = vol[i, 0:8, 0:128], vol[i, 0:8, 128:256]
        d, u = roll(first, slot * i, 1), roll(last, slot * i, 1)
        if i == 0:
            down, up = d, u
        else:
            down = jnp.where((lane >= slot * i) & (lane < slot * i + 3), d, down)
            up = jnp.where((lane >= slot * i - 3) & (lane < slot * i), u, up)
        if nodes is not None:
            for f in range(6):
                n = roll(nodes[f, 1 + i, :, 0:128], slot * i + 3 + f, 1)
                down = jnp.where(lane == slot * i + 3 + f, n, down)
    pack[0] = down
    pack[1] = up


def send_near(ex, rows, pack, rows_in, strip):
    for o in NEAR:
        _, dy, dz = o
        if dz:
            k = 0 if dz < 0 else 1
            ex.start(o, pack.at[k], strip.at[k, 1 - dy])
        else:
            k = 0 if dy < 0 else 1
            ex.start(o, rows.at[k], rows_in.at[k])


def assemble(vol, half, slot, rows_in, strip):
    row = iota((8, 256), 0)
    rowl = iota((8, 128), 0)
    lane = iota((8, 128), 1)
    for k in range(half):
        from_upper, from_lower = rows_in[0, k], rows_in[1, k]
        vol[k, 8:16, 0:256] = jnp.where(row < 4, from_upper, from_lower)
        vol[half + k, 8:16, 0:256] = roll(jnp.where(row < 4, from_lower, from_upper), 4, 0)
    both = [jnp.where((lane & (slot - 1)) < slot - 4, strip[0, dy], strip[1, dy]) for dy in range(3)]
    side = jnp.where(rowl < 4, both[2], both[0])
    for k in range(2 * half):
        vol[k, 0:8, 256:384] = roll(both[1], -slot * k, 1)
        vol[k, 8:16, 256:384] = roll(side, -slot * k, 1)
    return both[1], both[2]


def plane_sums(vol, fs, psum):
    row = iota((8, 384), 0)
    lane = iota((8, 128), 1)

    def shifts(t, c):
        t0, t1, th = t[:, 0:128], t[:, 128:256], t[:, 256:384]
        u0 = roll(jnp.where(lane < c, t1, t0), -c, 1) + roll(jnp.where(lane >= 128 - c, th, t0), c, 1)
        u1 = roll(jnp.where(lane < c, th, t1), -c, 1) + roll(jnp.where(lane >= 128 - c, t0, t1), c, 1)
        return u0, u1

    def plane(p, _):
        low, high = vol[p, 0:8, :], vol[p, 8:16, :]
        ys = [low]
        for b in (1, 2, 3):
            up = roll(jnp.where(row < b, high, low), -b, 0)
            down = roll(jnp.where(row >= 8 - b, high, low), b, 0)
            ys.append(up + down)
        groups = {}
        for b in range(4):
            for c in range(4):
                if b * b + c * c < 12.25:
                    v = (ys[b][:, 0:128], ys[b][:, 128:256]) if c == 0 else shifts(ys[b], c)
                    key = (min(b, c), max(b, c))
                    groups[key] = tuple(s + t for s, t in zip(groups[key], v)) if key in groups else v
        for a in range(4):
            for half in range(2):
                f = None
                for (b, c), v in groups.items():
                    w = cone_weight(a, b, c)
                    if w > 0:
                        f = v[half] * w if f is None else f + v[half] * w
                fs[a, p, :, pl.ds(128 * half, 128)] = f
        return 0

    lax.fori_loop(0, 8, plane, 0)
    for k in range(14):
        total = None
        for a in range(-3, 4):
            p = k - 3 + a
            if 0 <= p < 8:
                total = fs[abs(a), p] if total is None else total + fs[abs(a), p]
        psum[k] = total


def node_halo(halo, main, side):
    lane = iota((8, 128), 1)
    for p in range(8):
        a = roll(main, -(16 * p + 3), 1)
        b = roll(roll(side, -(16 * p + 3) + 8, 1), -1, 0)
        halo[1 + p, :, 256:384] = jnp.where(lane < 8, a, b)


def node_modes(nodes, halo, modes, q):
    lane = iota((8, 128), 1)
    row = iota((8, 128), 0)
    hs = halo[q, :, 256:384]
    hm = jnp.where(row == 7, roll(hs, -8, 1), roll(hs, -1, 0))
    for f in range(6):
        n = [nodes[f, q, :, 0:128], nodes[f, q, :, 128:256]]
        e = [halo[q, f:f + 1, 0:128], halo[q, f:f + 1, 128:256]]
        m = [jnp.where(row == 7, jnp.broadcast_to(e[k], (8, 128)), roll(n[k], -1, 0)) for k in range(2)]

        def up(v, h):
            v0, v1 = roll(v[0], -1, 1), roll(v[1], -1, 1)
            return jnp.where(lane == 127, v1, v0), jnp.where(lane == 127, roll(h, 127 - f, 1), v1)

        s, r = up(n, hs), up(m, hm)
        for k in range(2):
            a, d = n[k] + s[k], s[k] - n[k]
            ay, dy = m[k] + r[k], r[k] - m[k]
            at = pl.ds(128 * k, 128)
            modes[q, f, 0, :, at] = a + ay
            modes[q, f, 1, :, at] = d + dy
            modes[q, f, 2, :, at] = ay - a
            modes[q, f, 3, :, at] = dy - d


def element_energy(modes, x, press, mult):
    shear = 1.0 / (2.0 * (1.0 + poisson))
    bulk = 1.0 / (3.0 * (1.0 - 2.0 * poisson))

    def both_of(f, m):
        return modes[x, f, m], modes[x + 1, f, m]

    def field(base):
        out = []
        for c in range(3):
            aa, ad, da, dd = (both_of(base + c, m) for m in range(4))
            out.append(dict(
                X=aa[1] - aa[0], Y=da[0] + da[1], Z=ad[0] + ad[1],
                XY=da[1] - da[0], XZ=ad[1] - ad[0], YZ=dd[0] + dd[1], XYZ=dd[1] - dd[0]))
        return out

    u, l = field(0), field(3)

    def strains(v):
        a, b, c = v
        one = (a["X"], b["Y"], c["Z"], a["Y"] + b["X"], b["Z"] + c["Y"], a["Z"] + c["X"])
        xi = (None, b["XY"], c["XZ"], a["XY"], b["XZ"] + c["XY"], a["XZ"])
        eta = (a["XY"], None, c["YZ"], b["XY"], b["YZ"], a["YZ"] + c["XY"])
        zeta = (a["XZ"], b["YZ"], None, a["YZ"] + b["XZ"], c["YZ"], c["XZ"])
        return one, xi, eta, zeta

    su, sl = strains(u), strains(l)
    total = None
    for kind in range(4):
        eu, el = su[kind], sl[kind]
        normal, tr_u, tr_l = None, None, None
        for k in range(3):
            if eu[k] is not None:
                t = eu[k] * el[k]
                normal = t if normal is None else normal + t
                tr_u = eu[k] if tr_u is None else tr_u + eu[k]
                tr_l = el[k] if tr_l is None else tr_l + el[k]
        gamma = eu[3] * el[3] + eu[4] * el[4] + eu[5] * el[5]
        scale = shear / 16.0 if kind == 0 else shear / 48.0
        part = (2.0 * (normal - tr_u * tr_l * (1.0 / 3.0)) + gamma) * scale
        if kind == 0:
            div_u, div_l = tr_u * 0.25, tr_l * 0.25
        total = part if total is None else total + part
    pure = u[0]["XYZ"] * l[0]["XYZ"] + u[1]["XYZ"] * l[1]["XYZ"] + u[2]["XYZ"] * l[2]["XYZ"]
    total = total + pure * (shear * (10.0 / 3.0) / 144.0)
    return total + div_l * press + mult * div_u - mult * press * (1.0 / bulk)


def kernel(grid, design, flags, disp, adj, press, mult, out,
           vol, vol2, fs, ysum, psum, sums_in, rows, rows_in, strip, pack, rows2, rows_in2, strip2, pack2,
           nodes, node_rows, halo, modes, aux, fl, inv, energy,
           load_sem, ready, send1, recv1, send2, recv2, send3, recv3):
    barrier = pltpu.get_barrier_semaphore()
    at = [lax.axis_index(a) for a in AXES]
    first, last_x, half = 0, grid[0] - 1, grid[0] // 2
    beside = (at[0] == half - 1) | (at[0] == half)
    count = jnp.int32(0)

    def greet(target, ok, counts):
        @pl.when(ok)
        def _():
            pl.semaphore_signal(barrier, inc=1, device_id=target, device_id_type=MESH)

        return count + jnp.int32(1) * counts

    for o in NEAR:
        target, ok = peer(grid, o)
        count = greet(target, ok, ok)
    for dx in (-1, 1):
        target, ok = peer(grid, (dx, 0, 0))
        ok = ok & (at[0] != (half if dx < 0 else half - 1))
        count = greet(target, ok, ok)
    for end in (first, last_x):
        count = greet((end, at[1], at[2]), beside, 2 * (at[0] == end))

    own = pl.ds(1, 8)
    loads = [
        (design, vol.at[:, pl.ds(0, 8), pl.ds(0, 256)]),
        (disp, nodes.at[pl.ds(0, 3), own]),
        (adj, nodes.at[pl.ds(3, 3), own]),
        (flags, fl), (press, aux.at[own, 0]), (mult, aux.at[own, 1]),
    ]
    loads = [pltpu.make_async_copy(s, d, load_sem.at[k]) for k, (s, d) in enumerate(loads)]
    for c in loads:
        c.start()
    inverse_weight(grid, inv)
    for c in loads:
        c.wait()
    for x in range(8):
        aux[1 + x, 2] = jnp.where(fl[x] >= 2, inv[3 + x] * COEF, 0.0)
    pack_strips(vol, 8, 16, pack, nodes)
    pack_rows(vol, 0, 4, rows)
    for p in range(8):
        for f in range(6):
            node_rows[p, f:f + 1, :] = nodes[f, 1 + p, 0:1, :]
        node_rows[p, 6:8, :] = jnp.zeros((2, 256), jnp.float32)
    pl.semaphore_wait(barrier, count)
    for end, to in ((first, half - 1), (last_x, half)):
        @pl.when(at[0] == end)
        def _():
            pl.semaphore_signal(ready, inc=1, device_id=(to, at[1], at[2]), device_id_type=MESH)

    near = Exchange(grid, send1, recv1)
    send_near(near, rows, pack, rows_in, strip)
    near.start((0, -1, 0), node_rows, halo.at[own, :, pl.ds(0, 256)])
    for k in range(9):
        near.finish_recv(k)

    @pl.when(beside)
    def _():
        pl.semaphore_wait(ready, 1)

    lower, upper = (-1, 0, 0), (1, 0, 0)
    far = Exchange(grid, send2, recv2)
    far.start(lower, nodes.at[:, 1], nodes.at[:, 9])
    far.start(upper, nodes.at[:, 8], nodes.at[:, 0])
    far.start(upper, aux.at[8], aux.at[0])
    main, side = assemble(vol, 4, 16, rows_in, strip)
    plane_sums(vol, fs, psum)
    far.start(lower, psum.at[pl.ds(0, 6)], sums_in.at[1])
    far.start(upper, psum.at[pl.ds(8, 6)], sums_in.at[0])
    node_halo(halo, main, side)
    far.start(lower, halo.at[1], halo.at[9])
    far.start(upper, halo.at[8], halo.at[0])

    def own_modes(q, _):
        node_modes(nodes, halo, modes, q)
        return 0

    lax.fori_loop(1, 9, own_modes, 0)

    def scaled(x):
        return element_energy(modes, x + 1, aux[x + 1, 0], aux[x + 1, 1]) * aux[x + 1, 2]

    def energies(x, _):
        energy[x + 3] = scaled(x)
        return 0

    lax.fori_loop(0, 7, energies, 0)
    far.start(lower, energy.at[pl.ds(3, 3)], energy.at[pl.ds(11, 3)])
    far.start(upper, energy.at[pl.ds(8, 2)], energy.at[pl.ds(0, 2)])
    for k in (0, 1, 2, 5, 6):
        far.finish_recv(k)
    for q in (0, 9):
        node_modes(nodes, halo, modes, q)
    for x in (-1, 7):
        energy[x + 3] = scaled(x)
    for k in (3, 4, 7, 8):
        far.finish_recv(k)

    denom = math.tanh(sharpness * threshold) + math.tanh(sharpness * (1.0 - threshold))
    base = math.tanh(sharpness * threshold)
    for k in range(14):
        total = psum[k]
        if k < 6:
            total = total + sums_in[0, k]
        if k >= 8:
            total = total + sums_in[1, k - 8]
        hyper = jnp.tanh(sharpness * (total * inv[k] - threshold))
        smooth = (base + hyper) * (1.0 / denom)
        slope = (1.0 - hyper * hyper) * (sharpness / denom)
        vol2[k, 0:8, 0:256] = smooth * smooth * slope * energy[k]

    pack_strips(vol2, 14, 8, pack2, None)
    pack_rows(vol2, 0, 7, rows2)
    last = Exchange(grid, send3, recv3)
    send_near(last, rows2, pack2, rows_in2, strip2)
    for k in range(8):
        last.finish_recv(k)
    assemble(vol2, 7, 8, rows_in2, strip2)

    def final(x, t0, t1):
        planes = pl.ds(x, 2)
        for half, t in enumerate((t0, t1)):
            at = pl.ds(128 * half, 128)
            out[planes, :, at] = jnp.where(fl[planes, :, at] >= 2, t, 0.0)

    cone_sum(vol2, ysum, final)
    for ex in (near, far, last):
        for k in range(len(ex.items)):
            ex.finish_send(k)


def on_device(grid, *args):
    f32, i32 = jnp.float32, jnp.int32
    V = pltpu.VMEM
    dma = pltpu.SemaphoreType.DMA
    strip, pack = V((2, 3, 8, 128), f32), V((2, 8, 128), f32)
    return pl.pallas_call(
        functools.partial(kernel, grid),
        out_shape=jax.ShapeDtypeStruct((8, 8, 256), f32),
        in_specs=[pl.BlockSpec(memory_space=pl.ANY)] * 6,
        out_specs=pl.BlockSpec(memory_space=pltpu.VMEM),
        scratch_shapes=[
            V((8, 16, 384), f32), V((14, 16, 384), f32), V((4, 8, 8, 256), f32), V((3, 14, 8, 384), f32),
            V((14, 8, 256), f32), V((2, 6, 8, 256), f32),
            V((2, 4, 8, 256), f32), V((2, 4, 8, 256), f32), strip, pack,
            V((2, 7, 8, 256), f32), V((2, 7, 8, 256), f32), strip, pack,
            V((6, 10, 8, 256), f32), V((8, 8, 256), f32), V((10, 8, 384), f32), V((10, 6, 4, 8, 256), f32),
            V((9, 3, 8, 256), f32), V((8, 8, 256), i32), V((14, 8, 256), f32), V((14, 8, 256), f32),
            dma((6,)), pltpu.SemaphoreType.REGULAR, dma((9,)), dma((9,)), dma((9,)), dma((9,)), dma((8,)), dma((8,)),
        ],
        compiler_params=pltpu.CompilerParams(
            collective_id=0, has_side_effects=True, vmem_limit_bytes=63 << 20),
        name="sensitivity",
    )(*args)


def solution(mesh):
    grid = tuple(mesh.shape[a] for a in AXES)
    brick = P("gx", "gy", "gz")
    field = P(None, "gx", "gy", "gz")
    return jax.shard_map(
        functools.partial(on_device, grid), mesh=mesh,
        in_specs=(brick, brick, field, field, brick, brick), out_specs=brick, check_vma=False,
    )
```

```python
import functools
import itertools
import math

import jax
import jax.numpy as jnp
from jax import lax
from jax.experimental import pallas as pl
from jax.experimental.pallas import tpu as pltpu
from jax.sharding import PartitionSpec as P

poisson = 0.45
sharpness = 4.0
threshold = 0.5
stiff_floor = 0.001
cone_radius = 3.5

AXES = ("gx", "gy", "gz")
NX, NY, NZ = 8, 8, 256
MESH = pl.DeviceIdType.MESH
NEAR = [(0, 1, 1), (0, -1, 1), (0, 1, -1), (0, -1, -1), (0, -1, 0), (0, 1, 0), (0, 0, 1), (0, 0, -1)]
COEF = -3.0 * (1.0 - stiff_floor)


def cone_weight(a, b, c):
    r2 = a * a + b * b + c * c
    return cone_radius - math.sqrt(r2) if r2 < cone_radius * cone_radius else 0.0


def place(grid):
    return [lax.axis_index(a) for a in AXES]


def peer(grid, offset):
    at = [lax.axis_index(a) for a in AXES]
    target = tuple(a + o for a, o in zip(at, offset))
    ok = None
    for t, o, n in zip(target, offset, grid):
        if o:
            inside = t >= 0 if o < 0 else t < n
            ok = inside if ok is None else ok & inside
    return target, ok


def opposite(offset):
    return tuple(-o for o in offset)


class Exchange:
    def __init__(self, grid, send, recv):
        self.grid, self.send, self.recv = grid, send, recv
        self.items = []

    def copy(self, index):
        offset, src, dst = self.items[index]
        target, ok = peer(self.grid, offset)
        return ok, pltpu.make_async_remote_copy(
            src_ref=src, dst_ref=dst, send_sem=self.send.at[index], recv_sem=self.recv.at[index],
            device_id=target, device_id_type=MESH,
        )

    def add(self, offset, src, dst):
        self.items.append((offset, src, dst))
        return len(self.items) - 1

    def begin(self, index, when=None):
        ok, copy = self.copy(index)
        pl.when(ok if when is None else ok & when)(copy.start)

    def start(self, offset, src, dst):
        self.begin(self.add(offset, src, dst))

    def finish_recv(self, index):
        offset, src, dst = self.items[index]
        _, ok = peer(self.grid, opposite(offset))
        _, copy = self.copy(index)
        pl.when(ok)(copy.wait_recv)

        @pl.when(jnp.logical_not(ok))
        def _():
            dst[...] = jnp.zeros(dst.shape, jnp.float32)

    def finish_send(self, index):
        ok, copy = self.copy(index)
        pl.when(ok)(copy.wait_send)


def roll(value, by, axis):
    by = by % value.shape[axis]
    return value if by == 0 else pltpu.roll(value, by, axis)


def iota(shape, dim):
    return lax.broadcasted_iota(jnp.int32, shape, dim)


def cone_sum(vol, ysum, emit):
    row = iota((2, 8, 384), 1)

    def rows(p, _):
        at = pl.ds(2 * p, 2)
        low, high = vol[at, 0:8, :], vol[at, 8:16, :]
        for b in (1, 2, 3):
            up = roll(jnp.where(row < b, high, low), -b, 1)
            down = roll(jnp.where(row >= 8 - b, high, low), b, 1)
            ysum[b - 1, at] = up + down
        return 0

    lax.fori_loop(0, 7, rows, 0)
    lane = iota((2, 8, 128), 2)

    def planes(p, _):
        x = 2 * p
        sums = {}

        def get(b, k):
            return vol[pl.ds(x + k, 2), 0:8, :] if b == 0 else ysum[b - 1, pl.ds(x + k, 2)]

        for a in range(4):
            for b in range(4):
                if a * a + b * b < 12.25:
                    sums[a, b] = get(b, 3) if a == 0 else get(b, 3 - a) + get(b, 3 + a)
        groups = {}
        for (a, b), value in sums.items():
            key = (min(a, b), max(a, b))
            groups[key] = groups[key] + value if key in groups else value
        total = None
        for c in range(4):
            g = None
            for (a, b), value in groups.items():
                w = cone_weight(a, b, c)
                if w > 0:
                    g = value * w if g is None else g + value * w
            g0, g1, gh = g[:, :, 0:128], g[:, :, 128:256], g[:, :, 256:384]
            if c == 0:
                t0, t1 = g0, g1
            else:
                t0 = t0 + roll(jnp.where(lane < c, g1, g0), -c, 2) + roll(
                    jnp.where(lane >= 128 - c, gh, g0), c, 2)
                t1 = t1 + roll(jnp.where(lane < c, gh, g1), -c, 2) + roll(
                    jnp.where(lane >= 128 - c, g0, g1), c, 2)
        emit(x, t0, t1)
        return 0

    lax.fori_loop(0, 4, planes, 0)


def inverse_weight(grid, out):
    gx, gy, gz = [lax.axis_index(a) for a in AXES]
    y = gy * NY + iota((NY, NZ), 0)
    z = gz * NZ + iota((NY, NZ), 1)

    def pairs(pos, by, size):
        def inside(v):
            return ((v >= 0) & (v < size)).astype(jnp.float32)
        return inside(pos + by) + inside(pos - by) if by else inside(pos)

    ys = [None] + [pairs(y, b, grid[1] * NY) for b in (1, 2, 3)]
    zs = [None] + [pairs(z, c, grid[2] * NZ) for c in (1, 2, 3)]
    fs = []
    for a in range(4):
        f = jnp.full((NY, NZ), 0.0, jnp.float32)
        for b in range(4):
            for c in range(4):
                w = cone_weight(a, b, c)
                if w > 0:
                    term = jnp.float32(w)
                    term = term if b == 0 else term * ys[b]
                    term = term if c == 0 else term * zs[c]
                    f = f + term
        fs.append(f)
    for k in range(14):
        px = gx * NX + k - 3
        w = fs[0] * pairs(px, 0, grid[0] * NX)
        for a in (1, 2, 3):
            w = w + fs[a] * pairs(px, a, grid[0] * NX)
        out[k] = 1.0 / w


def pack_rows(vol, first, half, rows):
    row = iota((8, 256), 0)
    for k in range(half):
        a, b = vol[first + k, 0:8, 0:256], vol[first + half + k, 0:8, 0:256]
        b = roll(b, 4, 0)
        rows[0, k] = jnp.where(row < 4, a, b)
        rows[1, k] = jnp.where(row < 4, b, a)


def pack_strips(vol, planes, slot, pack, nodes):
    lane = iota((8, 128), 1)
    down, up = None, None
    for i in range(planes):
        first, last = vol[i, 0:8, 0:128], vol[i, 0:8, 128:256]
        d, u = roll(first, slot * i, 1), roll(last, slot * i, 1)
        if i == 0:
            down, up = d, u
        else:
            down = jnp.where((lane >= slot * i) & (lane < slot * i + 3), d, down)
            up = jnp.where((lane >= slot * i - 3) & (lane < slot * i), u, up)
        if nodes is not None:
            for f in range(6):
                n = roll(nodes[f, 1 + i, :, 0:128], slot * i + 3 + f, 1)
                down = jnp.where(lane == slot * i + 3 + f, n, down)
    pack[0] = down
    pack[1] = up


def send_near(ex, rows, pack, rows_in, strip):
    for o in NEAR:
        _, dy, dz = o
        if dz:
            k = 0 if dz < 0 else 1
            ex.start(o, pack.at[k], strip.at[k, 1 - dy])
        else:
            k = 0 if dy < 0 else 1
            ex.start(o, rows.at[k], rows_in.at[k])


def assemble(vol, half, slot, rows_in, strip):
    row = iota((8, 256), 0)
    rowl = iota((8, 128), 0)
    lane = iota((8, 128), 1)
    for k in range(half):
        from_upper, from_lower = rows_in[0, k], rows_in[1, k]
        vol[k, 8:16, 0:256] = jnp.where(row < 4, from_upper, from_lower)
        vol[half + k, 8:16, 0:256] = roll(jnp.where(row < 4, from_lower, from_upper), 4, 0)
    both = [jnp.where((lane & (slot - 1)) < slot - 4, strip[0, dy], strip[1, dy]) for dy in range(3)]
    side = jnp.where(rowl < 4, both[2], both[0])
    for k in range(2 * half):
        vol[k, 0:8, 256:384] = roll(both[1], -slot * k, 1)
        vol[k, 8:16, 256:384] = roll(side, -slot * k, 1)
    return both[1], both[2]


def plane_sums(vol, fs, psum):
    row = iota((8, 384), 0)
    lane = iota((8, 128), 1)

    def shifts(t, c):
        t0, t1, th = t[:, 0:128], t[:, 128:256], t[:, 256:384]
        u0 = roll(jnp.where(lane < c, t1, t0), -c, 1) + roll(jnp.where(lane >= 128 - c, th, t0), c, 1)
        u1 = roll(jnp.where(lane < c, th, t1), -c, 1) + roll(jnp.where(lane >= 128 - c, t0, t1), c, 1)
        return u0, u1

    def plane(p, _):
        low, high = vol[p, 0:8, :], vol[p, 8:16, :]
        ys = [low]
        for b in (1, 2, 3):
            up = roll(jnp.where(row < b, high, low), -b, 0)
            down = roll(jnp.where(row >= 8 - b, high, low), b, 0)
            ys.append(up + down)
        groups = {}
        for b in range(4):
            for c in range(4):
                if b * b + c * c < 12.25:
                    v = (ys[b][:, 0:128], ys[b][:, 128:256]) if c == 0 else shifts(ys[b], c)
                    key = (min(b, c), max(b, c))
                    groups[key] = tuple(s + t for s, t in zip(groups[key], v)) if key in groups else v
        for a in range(4):
            for half in range(2):
                f = None
                for (b, c), v in groups.items():
                    w = cone_weight(a, b, c)
                    if w > 0:
                        f = v[half] * w if f is None else f + v[half] * w
                fs[a, p, :, pl.ds(128 * half, 128)] = f
        return 0

    lax.fori_loop(0, 8, plane, 0)
    for k in range(14):
        total = None
        for a in range(-3, 4):
            p = k - 3 + a
            if 0 <= p < 8:
                total = fs[abs(a), p] if total is None else total + fs[abs(a), p]
        psum[k] = total


def node_halo(halo, main, side):
    lane = iota((8, 128), 1)
    for p in range(8):
        a = roll(main, -(16 * p + 3), 1)
        b = roll(roll(side, -(16 * p + 3) + 8, 1), -1, 0)
        halo[1 + p, :, 256:384] = jnp.where(lane < 8, a, b)


def node_modes(nodes, halo, modes, q):
    lane = iota((8, 128), 1)
    row = iota((8, 128), 0)
    hs = halo[q, :, 256:384]
    hm = jnp.where(row == 7, roll(hs, -8, 1), roll(hs, -1, 0))
    for f in range(6):
        n = [nodes[f, q, :, 0:128], nodes[f, q, :, 128:256]]
        e = [halo[q, f:f + 1, 0:128], halo[q, f:f + 1, 128:256]]
        m = [jnp.where(row == 7, jnp.broadcast_to(e[k], (8, 128)), roll(n[k], -1, 0)) for k in range(2)]

        def up(v, h):
            v0, v1 = roll(v[0], -1, 1), roll(v[1], -1, 1)
            return jnp.where(lane == 127, v1, v0), jnp.where(lane == 127, roll(h, 127 - f, 1), v1)

        s, r = up(n, hs), up(m, hm)
        for k in range(2):
            a, d = n[k] + s[k], s[k] - n[k]
            ay, dy = m[k] + r[k], r[k] - m[k]
            at = pl.ds(128 * k, 128)
            modes[q, f, 0, :, at] = a + ay
            modes[q, f, 1, :, at] = d + dy
            modes[q, f, 2, :, at] = ay - a
            modes[q, f, 3, :, at] = dy - d


def element_energy(modes, x, press, mult):
    shear = 1.0 / (2.0 * (1.0 + poisson))
    bulk = 1.0 / (3.0 * (1.0 - 2.0 * poisson))

    def both_of(f, m):
        return modes[x, f, m], modes[x + 1, f, m]

    def field(base):
        out = []
        for c in range(3):
            aa, ad, da, dd = (both_of(base + c, m) for m in range(4))
            out.append(dict(
                X=aa[1] - aa[0], Y=da[0] + da[1], Z=ad[0] + ad[1],
                XY=da[1] - da[0], XZ=ad[1] - ad[0], YZ=dd[0] + dd[1], XYZ=dd[1] - dd[0]))
        return out

    u, l = field(0), field(3)

    def strains(v):
        a, b, c = v
        one = (a["X"], b["Y"], c["Z"], a["Y"] + b["X"], b["Z"] + c["Y"], a["Z"] + c["X"])
        xi = (None, b["XY"], c["XZ"], a["XY"], b["XZ"] + c["XY"], a["XZ"])
        eta = (a["XY"], None, c["YZ"], b["XY"], b["YZ"], a["YZ"] + c["XY"])
        zeta = (a["XZ"], b["YZ"], None, a["YZ"] + b["XZ"], c["YZ"], c["XZ"])
        return one, xi, eta, zeta

    su, sl = strains(u), strains(l)
    total = None
    for kind in range(4):
        eu, el = su[kind], sl[kind]
        normal, tr_u, tr_l = None, None, None
        for k in range(3):
            if eu[k] is not None:
                t = eu[k] * el[k]
                normal = t if normal is None else normal + t
                tr_u = eu[k] if tr_u is None else tr_u + eu[k]
                tr_l = el[k] if tr_l is None else tr_l + el[k]
        gamma = eu[3] * el[3] + eu[4] * el[4] + eu[5] * el[5]
        scale = shear / 16.0 if kind == 0 else shear / 48.0
        part = (2.0 * (normal - tr_u * tr_l * (1.0 / 3.0)) + gamma) * scale
        if kind == 0:
            div_u, div_l = tr_u * 0.25, tr_l * 0.25
        total = part if total is None else total + part
    pure = u[0]["XYZ"] * l[0]["XYZ"] + u[1]["XYZ"] * l[1]["XYZ"] + u[2]["XYZ"] * l[2]["XYZ"]
    total = total + pure * (shear * (10.0 / 3.0) / 144.0)
    return total + div_l * press + mult * div_u - mult * press * (1.0 / bulk)


def kernel(grid, design, flags, disp, adj, press, mult, out,
           vol, vol2, fs, ysum, psum, sums_in, rows, rows_in, strip, pack, rows2, rows_in2, strip2, pack2,
           nodes, node_rows, halo, modes, aux, fl, inv, energy,
           load_sem, ready, send1, recv1, send2, recv2, send3, recv3):
    barrier = pltpu.get_barrier_semaphore()
    at = [lax.axis_index(a) for a in AXES]
    first, last_x, half = 0, grid[0] - 1, grid[0] // 2
    beside = (at[0] == half - 1) | (at[0] == half)
    count = jnp.int32(0)

    def greet(target, ok, counts):
        @pl.when(ok)
        def _():
            pl.semaphore_signal(barrier, inc=1, device_id=target, device_id_type=MESH)

        return count + jnp.int32(1) * counts

    for end in (first, last_x):
        count = greet((end, at[1], at[2]), beside, 2 * (at[0] == end))
    own = pl.ds(1, 8)
    loads = [
        (design, vol.at[:, pl.ds(0, 8), pl.ds(0, 256)]),
        (disp, nodes.at[pl.ds(0, 3), own]),
        (adj, nodes.at[pl.ds(3, 3), own]),
        (flags, fl), (press, aux.at[own, 0]), (mult, aux.at[own, 1]),
    ]
    loads = [pltpu.make_async_copy(s, d, load_sem.at[k]) for k, (s, d) in enumerate(loads)]
    for c in loads:
        c.start()
    for o in NEAR:
        target, ok = peer(grid, o)
        count = greet(target, ok, ok)
    for dx in (-1, 1):
        target, ok = peer(grid, (dx, 0, 0))
        ok = ok & (at[0] != (half if dx < 0 else half - 1))
        count = greet(target, ok, ok)
    for c in loads[:3]:
        c.wait()
    pack_strips(vol, 8, 16, pack, nodes)
    pack_rows(vol, 0, 4, rows)
    for p in range(8):
        for f in range(6):
            node_rows[p, f:f + 1, :] = nodes[f, 1 + p, 0:1, :]
        node_rows[p, 6:8, :] = jnp.zeros((2, 256), jnp.float32)
    pl.semaphore_wait(barrier, count)
    for end, to in ((first, half - 1), (last_x, half)):
        @pl.when(at[0] == end)
        def _():
            pl.semaphore_signal(ready, inc=1, device_id=(to, at[1], at[2]), device_id_type=MESH)

    near = Exchange(grid, send1, recv1)
    send_near(near, rows, pack, rows_in, strip)
    near.start((0, -1, 0), node_rows, halo.at[own, :, pl.ds(0, 256)])
    inverse_weight(grid, inv)
    for c in loads[3:]:
        c.wait()
    for x in range(8):
        aux[1 + x, 2] = jnp.where(fl[x] >= 2, inv[3 + x] * COEF, 0.0)

    @pl.when(beside)
    def _():
        pl.semaphore_wait(ready, 1)

    lower, upper = (-1, 0, 0), (1, 0, 0)
    far = Exchange(grid, send2, recv2)
    far.start(lower, nodes.at[:, 1], nodes.at[:, 9])
    far.start(upper, nodes.at[:, 8], nodes.at[:, 0])
    far.start(upper, aux.at[8], aux.at[0])
    for k in range(9):
        near.finish_recv(k)
    main, side = assemble(vol, 4, 16, rows_in, strip)
    node_halo(halo, main, side)
    far.start(lower, halo.at[1], halo.at[9])
    far.start(upper, halo.at[8], halo.at[0])
    plane_sums(vol, fs, psum)
    far.start(lower, psum.at[pl.ds(0, 6)], sums_in.at[1])
    far.start(upper, psum.at[pl.ds(8, 6)], sums_in.at[0])

    def scaled(x):
        return element_energy(modes, x + 1, aux[x + 1, 0], aux[x + 1, 1]) * aux[x + 1, 2]

    down_first = (at[0] == half).astype(jnp.int32)

    def own_modes(i, _):
        node_modes(nodes, halo, modes, jnp.where(down_first == 1, 1 + i, 8 - i))
        return 0

    def energies(i, _):
        x = jnp.where(down_first == 1, i, 6 - i)
        energy[x + 3] = scaled(x)
        return 0

    lax.fori_loop(0, 4, own_modes, 0)
    lax.fori_loop(0, 3, energies, 0)
    far.add(lower, energy.at[pl.ds(3, 3)], energy.at[pl.ds(11, 3)])
    far.add(upper, energy.at[pl.ds(8, 2)], energy.at[pl.ds(0, 2)])
    far.begin(7, down_first == 1)
    far.begin(8, down_first == 0)
    lax.fori_loop(4, 8, own_modes, 0)
    lax.fori_loop(3, 7, energies, 0)
    far.begin(7, down_first == 0)
    far.begin(8, down_first == 1)
    for k in (0, 1, 2, 3, 4):
        far.finish_recv(k)
    for q in (0, 9):
        node_modes(nodes, halo, modes, q)
    for x in (-1, 7):
        energy[x + 3] = scaled(x)
    for k in (5, 6, 7, 8):
        far.finish_recv(k)

    denom = math.tanh(sharpness * threshold) + math.tanh(sharpness * (1.0 - threshold))
    base = math.tanh(sharpness * threshold)
    for k in range(14):
        total = psum[k]
        if k < 6:
            total = total + sums_in[0, k]
        if k >= 8:
            total = total + sums_in[1, k - 8]
        hyper = jnp.tanh(sharpness * (total * inv[k] - threshold))
        smooth = (base + hyper) * (1.0 / denom)
        slope = (1.0 - hyper * hyper) * (sharpness / denom)
        vol2[k, 0:8, 0:256] = smooth * smooth * slope * energy[k]

    pack_strips(vol2, 14, 8, pack2, None)
    pack_rows(vol2, 0, 7, rows2)
    last = Exchange(grid, send3, recv3)
    send_near(last, rows2, pack2, rows_in2, strip2)
    for k in range(8):
        last.finish_recv(k)
    assemble(vol2, 7, 8, rows_in2, strip2)

    def final(x, t0, t1):
        planes = pl.ds(x, 2)
        for half, t in enumerate((t0, t1)):
            at = pl.ds(128 * half, 128)
            out[planes, :, at] = jnp.where(fl[planes, :, at] >= 2, t, 0.0)

    cone_sum(vol2, ysum, final)
    for ex in (near, far, last):
        for k in range(len(ex.items)):
            ex.finish_send(k)


def on_device(grid, *args):
    f32, i32 = jnp.float32, jnp.int32
    V = pltpu.VMEM
    dma = pltpu.SemaphoreType.DMA
    strip, pack = V((2, 3, 8, 128), f32), V((2, 8, 128), f32)
    return pl.pallas_call(
        functools.partial(kernel, grid),
        out_shape=pltpu.VMEM((8, 8, 256), f32),
        in_specs=[pl.BlockSpec(memory_space=pl.ANY)] * 6,
        out_specs=pl.BlockSpec(memory_space=pltpu.VMEM),
        scratch_shapes=[
            V((8, 16, 384), f32), V((14, 16, 384), f32), V((4, 8, 8, 256), f32), V((3, 14, 8, 384), f32),
            V((14, 8, 256), f32), V((2, 6, 8, 256), f32),
            V((2, 4, 8, 256), f32), V((2, 4, 8, 256), f32), strip, pack,
            V((2, 7, 8, 256), f32), V((2, 7, 8, 256), f32), strip, pack,
            V((6, 10, 8, 256), f32), V((8, 8, 256), f32), V((10, 8, 384), f32), V((10, 6, 4, 8, 256), f32),
            V((9, 3, 8, 256), f32), V((8, 8, 256), i32), V((14, 8, 256), f32), V((14, 8, 256), f32),
            dma((6,)), pltpu.SemaphoreType.REGULAR, dma((9,)), dma((9,)), dma((9,)), dma((9,)), dma((8,)), dma((8,)),
        ],
        compiler_params=pltpu.CompilerParams(
            collective_id=0, has_side_effects=True, vmem_limit_bytes=63 << 20),
        name="sensitivity",
    )(*args)


def solution(mesh):
    grid = tuple(mesh.shape[a] for a in AXES)
    brick = P("gx", "gy", "gz")
    field = P(None, "gx", "gy", "gz")
    return jax.shard_map(
        functools.partial(on_device, grid), mesh=mesh,
        in_specs=(brick, brick, field, field, brick, brick), out_specs=brick, check_vma=False,
    )
```

```python
import functools
import itertools
import math

import jax
import jax.numpy as jnp
from jax import lax
from jax.experimental import pallas as pl
from jax.experimental.pallas import tpu as pltpu
from jax.sharding import PartitionSpec as P

poisson = 0.45
sharpness = 4.0
threshold = 0.5
stiff_floor = 0.001
cone_radius = 3.5

AXES = ("gx", "gy", "gz")
NX, NY, NZ = 8, 8, 256
MESH = pl.DeviceIdType.MESH
NEAR = [(0, 1, 1), (0, -1, 1), (0, 1, -1), (0, -1, -1), (0, -1, 0), (0, 1, 0), (0, 0, 1), (0, 0, -1)]
COEF = -3.0 * (1.0 - stiff_floor)


def cone_weight(a, b, c):
    r2 = a * a + b * b + c * c
    return cone_radius - math.sqrt(r2) if r2 < cone_radius * cone_radius else 0.0


def place(grid):
    return [lax.axis_index(a) for a in AXES]


def peer(grid, offset):
    at = [lax.axis_index(a) for a in AXES]
    target = tuple(a + o for a, o in zip(at, offset))
    ok = None
    for t, o, n in zip(target, offset, grid):
        if o:
            inside = t >= 0 if o < 0 else t < n
            ok = inside if ok is None else ok & inside
    return target, ok


def opposite(offset):
    return tuple(-o for o in offset)


class Exchange:
    def __init__(self, grid, send, recv):
        self.grid, self.send, self.recv = grid, send, recv
        self.items, self.unless = [], []

    def copy(self, index):
        offset, src, dst = self.items[index]
        target, ok = peer(self.grid, offset)
        return ok, pltpu.make_async_remote_copy(
            src_ref=src, dst_ref=dst, send_sem=self.send.at[index], recv_sem=self.recv.at[index],
            device_id=target, device_id_type=MESH,
        )

    def add(self, offset, src, dst, unless=None):
        self.items.append((offset, src, dst))
        self.unless.append(unless)
        return len(self.items) - 1

    def sends(self, index):
        ok, copy = self.copy(index)
        unless = self.unless[index]
        return (ok if unless is None else ok & jnp.logical_not(unless)), copy

    def begin(self, index, when=None):
        ok, copy = self.sends(index)
        pl.when(ok if when is None else ok & when)(copy.start)

    def start(self, offset, src, dst, unless=None):
        self.begin(self.add(offset, src, dst, unless))

    def finish_recv(self, index, when=None):
        offset, src, dst = self.items[index]
        _, ok = peer(self.grid, opposite(offset))
        _, copy = self.copy(index)
        pl.when(ok if when is None else ok & when)(copy.wait_recv)
        missing = jnp.logical_not(ok)

        @pl.when(missing if when is None else missing & when)
        def _():
            dst[...] = jnp.zeros(dst.shape, jnp.float32)

    def finish_send(self, index):
        ok, copy = self.sends(index)
        pl.when(ok)(copy.wait_send)


def roll(value, by, axis):
    by = by % value.shape[axis]
    return value if by == 0 else pltpu.roll(value, by, axis)


def iota(shape, dim):
    return lax.broadcasted_iota(jnp.int32, shape, dim)


def row_sums(vol, ysum, first, count):
    row = iota((2, 8, 384), 1)

    def rows(p, _):
        at = pl.ds(first + 2 * p, 2)
        low, high = vol[at, 0:8, :], vol[at, 8:16, :]
        for b in (1, 2, 3):
            up = roll(jnp.where(row < b, high, low), -b, 1)
            down = roll(jnp.where(row >= 8 - b, high, low), b, 1)
            ysum[b - 1, at] = up + down
        return 0

    lax.fori_loop(0, count // 2, rows, 0, unroll=True)


def cone_pair(vol, ysum, x):
    lane = iota((2, 8, 128), 2)
    sums = {}

    def get(b, k):
        return vol[pl.ds(x + k, 2), 0:8, :] if b == 0 else ysum[b - 1, pl.ds(x + k, 2)]

    for a in range(4):
        for b in range(4):
            if a * a + b * b < 12.25:
                sums[a, b] = get(b, 3) if a == 0 else get(b, 3 - a) + get(b, 3 + a)
    groups = {}
    for (a, b), value in sums.items():
        key = (min(a, b), max(a, b))
        groups[key] = groups[key] + value if key in groups else value
    for c in range(4):
        g = None
        for (a, b), value in groups.items():
            w = cone_weight(a, b, c)
            if w > 0:
                g = value * w if g is None else g + value * w
        g0, g1, gh = g[:, :, 0:128], g[:, :, 128:256], g[:, :, 256:384]
        if c == 0:
            t0, t1 = g0, g1
        else:
            t0 = t0 + roll(jnp.where(lane < c, g1, g0), -c, 2) + roll(
                jnp.where(lane >= 128 - c, gh, g0), c, 2)
            t1 = t1 + roll(jnp.where(lane < c, gh, g1), -c, 2) + roll(
                jnp.where(lane >= 128 - c, g0, g1), c, 2)
    return t0, t1


def inverse_weight(grid, out):
    gx, gy, gz = [lax.axis_index(a) for a in AXES]
    y = gy * NY + iota((NY, NZ), 0)
    z = gz * NZ + iota((NY, NZ), 1)

    def pairs(pos, by, size):
        def inside(v):
            return ((v >= 0) & (v < size)).astype(jnp.float32)
        return inside(pos + by) + inside(pos - by) if by else inside(pos)

    ys = [None] + [pairs(y, b, grid[1] * NY) for b in (1, 2, 3)]
    zs = [None] + [pairs(z, c, grid[2] * NZ) for c in (1, 2, 3)]
    fs = []
    for a in range(4):
        f = jnp.full((NY, NZ), 0.0, jnp.float32)
        for b in range(4):
            for c in range(4):
                w = cone_weight(a, b, c)
                if w > 0:
                    term = jnp.float32(w)
                    term = term if b == 0 else term * ys[b]
                    term = term if c == 0 else term * zs[c]
                    f = f + term
        fs.append(f)
    for k in range(14):
        px = gx * NX + k - 3
        w = fs[0] * pairs(px, 0, grid[0] * NX)
        for a in (1, 2, 3):
            w = w + fs[a] * pairs(px, a, grid[0] * NX)
        out[k] = 1.0 / w


def pack_rows(vol, first, half, rows):
    row = iota((8, 256), 0)
    for k in range(half):
        a, b = vol[first + k, 0:8, 0:256], vol[first + half + k, 0:8, 0:256]
        b = roll(b, 4, 0)
        rows[0, k] = jnp.where(row < 4, a, b)
        rows[1, k] = jnp.where(row < 4, b, a)


def pack_thin(vol, rows, node_rows, nodes):
    for p in range(8):
        for f in range(6):
            node_rows[p, f:f + 1, :] = nodes[f, 1 + p, 0:1, :]
        node_rows[p, 6:8, :] = vol[6 + p, 0:2, 0:256]
        for j, r in enumerate((2, 5, 6, 7)):
            rows[j, p:p + 1, :] = vol[6 + p, r:r + 1, 0:256]


def unpack_thin(vol, rows_in, halo):
    row = iota((8, 256), 0)
    for p in range(8):
        value = roll(halo[1 + p, :, 0:256], 2, 0)
        for j, r in enumerate((2, 5, 6, 7)):
            value = jnp.where(row == r, jnp.broadcast_to(rows_in[j, p:p + 1, :], (8, 256)), value)
        vol[6 + p, 8:16, 0:256] = value


def pack_strips(vol, places, slot, pack, nodes):
    lane = iota((8, 128), 1)
    down, up = pack[0], pack[1]
    for i, p in places:
        first, last = vol[p, 0:8, 0:128], vol[p, 0:8, 128:256]
        d, u = roll(first, slot * i, 1), roll(last, slot * i, 1)
        if i == 0:
            down, up = d, u
        else:
            down = jnp.where((lane >= slot * i) & (lane < slot * i + 3), d, down)
            up = jnp.where((lane >= slot * i - 3) & (lane < slot * i), u, up)
        if nodes is not None:
            for f in range(6):
                n = roll(nodes[f, 1 + i, :, 0:128], slot * i + 3 + f, 1)
                down = jnp.where(lane == slot * i + 3 + f, n, down)
    pack[0] = down
    pack[1] = up


def send_strips(ex, pack, strip):
    for o in NEAR:
        _, dy, dz = o
        if dz:
            k = 0 if dz < 0 else 1
            ex.start(o, pack.at[k], strip.at[k, 1 - dy])


def send_rows(ex, rows, rows_in):
    for k, dy in enumerate((-1, 1)):
        ex.start((0, dy, 0), rows.at[k], rows_in.at[k])


def unpack_rows(vol, first, half, rows_in):
    row = iota((8, 256), 0)
    for k in range(half):
        from_upper, from_lower = rows_in[0, k], rows_in[1, k]
        vol[first + k, 8:16, 0:256] = jnp.where(row < 4, from_upper, from_lower)
        vol[first + half + k, 8:16, 0:256] = roll(jnp.where(row < 4, from_lower, from_upper), 4, 0)


def unpack_strips(vol, places, slot, strip):
    rowl = iota((8, 128), 0)
    lane = iota((8, 128), 1)
    both = [jnp.where((lane & (slot - 1)) < slot - 4, strip[0, dy], strip[1, dy]) for dy in range(3)]
    side = jnp.where(rowl < 4, both[2], both[0])
    for i, p in places:
        vol[p, 0:8, 256:384] = roll(both[1], -slot * i, 1)
        vol[p, 8:16, 256:384] = roll(side, -slot * i, 1)
    return both[1], both[2]


def node_halo(halo, main, side):
    lane = iota((8, 128), 1)
    for p in range(8):
        a = roll(main, -(16 * p + 3), 1)
        b = roll(roll(side, -(16 * p + 3) + 8, 1), -1, 0)
        halo[1 + p, :, 256:384] = jnp.where(lane < 8, a, b)


def node_ahead(nodes, ahead, q):
    lane = iota((8, 128), 1)
    for f in range(6):
        v0, v1 = roll(nodes[f, q, :, 0:128], -1, 1), roll(nodes[f, q, :, 128:256], -1, 1)
        ahead[q, f, :, 0:128] = jnp.where(lane == 127, v1, v0)
        ahead[q, f, :, 128:256] = v1


def node_modes(nodes, ahead, halo, halo_up, modes, q):
    lane = iota((8, 128), 1)
    row = iota((8, 128), 0)
    hs = halo[q, :, 256:384]
    hm = jnp.where(row == 7, roll(hs, -8, 1), roll(hs, -1, 0))
    v0, v1 = roll(halo[q, :, 0:128], -1, 1), roll(halo[q, :, 128:256], -1, 1)
    halo_up[q, :, 0:128] = jnp.where(lane == 127, v1, v0)
    halo_up[q, :, 128:256] = v1

    def spread(ref, f, k):
        return jnp.broadcast_to(ref[q, f:f + 1, 128 * k:128 * k + 128], (8, 128))

    for f in range(6):
        for k in range(2):
            at = pl.ds(128 * k, 128)
            n, s = nodes[f, q, :, at], ahead[q, f, :, at]
            e, r = spread(halo, f, k), spread(halo_up, f, k)
            if k == 1:
                s = jnp.where(lane == 127, roll(hs, 127 - f, 1), s)
                r = jnp.where(lane == 127, roll(hm, 127 - f, 1), r)
            a, d = n + s, s - n
            ay = jnp.where(row == 7, e + r, roll(a, -1, 0))
            dy = jnp.where(row == 7, r - e, roll(d, -1, 0))
            modes[q, f, 0, :, at] = a + ay
            modes[q, f, 1, :, at] = d + dy
            modes[q, f, 2, :, at] = ay - a
            modes[q, f, 3, :, at] = dy - d


def element_energy(modes, x, press, mult):
    shear = 1.0 / (2.0 * (1.0 + poisson))
    bulk = 1.0 / (3.0 * (1.0 - 2.0 * poisson))

    def both_of(f, m):
        return modes[x, f, m], modes[x + 1, f, m]

    def field(base):
        out = []
        for c in range(3):
            aa, ad, da, dd = (both_of(base + c, m) for m in range(4))
            out.append(dict(
                X=aa[1] - aa[0], Y=da[0] + da[1], Z=ad[0] + ad[1],
                XY=da[1] - da[0], XZ=ad[1] - ad[0], YZ=dd[0] + dd[1], XYZ=dd[1] - dd[0]))
        return out

    u, l = field(0), field(3)

    def strains(v):
        a, b, c = v
        one = (a["X"], b["Y"], c["Z"], a["Y"] + b["X"], b["Z"] + c["Y"], a["Z"] + c["X"])
        xi = (None, b["XY"], c["XZ"], a["XY"], b["XZ"] + c["XY"], a["XZ"])
        eta = (a["XY"], None, c["YZ"], b["XY"], b["YZ"], a["YZ"] + c["XY"])
        zeta = (a["XZ"], b["YZ"], None, a["YZ"] + b["XZ"], c["YZ"], c["XZ"])
        return one, xi, eta, zeta

    su, sl = strains(u), strains(l)
    total = None
    for kind in range(4):
        eu, el = su[kind], sl[kind]
        normal, tr_u, tr_l = None, None, None
        for k in range(3):
            if eu[k] is not None:
                t = eu[k] * el[k]
                normal = t if normal is None else normal + t
                tr_u = eu[k] if tr_u is None else tr_u + eu[k]
                tr_l = el[k] if tr_l is None else tr_l + el[k]
        gamma = eu[3] * el[3] + eu[4] * el[4] + eu[5] * el[5]
        scale = shear / 16.0 if kind == 0 else shear / 48.0
        part = (2.0 * (normal - tr_u * tr_l * (1.0 / 3.0)) + gamma) * scale
        if kind == 0:
            div_u, div_l = tr_u * 0.25, tr_l * 0.25
        total = part if total is None else total + part
    pure = u[0]["XYZ"] * l[0]["XYZ"] + u[1]["XYZ"] * l[1]["XYZ"] + u[2]["XYZ"] * l[2]["XYZ"]
    total = total + pure * (shear * (10.0 / 3.0) / 144.0)
    return total + div_l * press + mult * div_u - mult * press * (1.0 / bulk)


def kernel(grid, design, flags, disp, adj, press, mult, out,
           vol, vol2, ysum, ysum2, psum, sums_in, rows, rows_in, strip, pack, rows2, rows_in2, rows3, rows_in3, strip2, pack2,
           nodes, node_rows, ahead, halo, halo_up, modes, aux, fl, inv, energy,
           relay, load_sem, ready, leave, pause, onward, send1, recv1, send2, recv2, send3, recv3):
    barrier = pltpu.get_barrier_semaphore()
    at = [lax.axis_index(a) for a in AXES]
    first, last_x, half = 0, grid[0] - 1, grid[0] // 2
    beside = (at[0] == half - 1) | (at[0] == half)
    count = jnp.int32(0)

    def greet(target, ok, counts):
        @pl.when(ok)
        def _():
            pl.semaphore_signal(barrier, inc=1, device_id=target, device_id_type=MESH)

        return count + jnp.int32(1) * counts

    for end in (first, last_x):
        count = greet((end, at[1], at[2]), beside, 2 * (at[0] == end))
    for end, to in ((first, half - 1), (last_x, half)):
        count = greet((to, at[1], at[2]), at[0] == end, at[0] == to)
    own = pl.ds(1, 8)
    loads = [
        (design, vol.at[pl.ds(6, 8), pl.ds(0, 8), pl.ds(0, 256)]),
        (disp, nodes.at[pl.ds(0, 3), own]),
        (adj, nodes.at[pl.ds(3, 3), own]),
        (flags, fl), (press, aux.at[own, 0]), (mult, aux.at[own, 1]),
    ]
    loads = [pltpu.make_async_copy(s, d, load_sem.at[k]) for k, (s, d) in enumerate(loads)]
    for c in loads:
        c.start()
    for o in NEAR:
        target, ok = peer(grid, o)
        count = greet(target, ok, ok)
    for dx in (-1, 1):
        target, ok = peer(grid, (dx, 0, 0))
        ok = ok & (at[0] != (half if dx < 0 else half - 1))
        count = greet(target, ok, ok)
    for c in loads[:3]:
        c.wait()
    own_places = [(i, 6 + i) for i in range(8)]
    pack_strips(vol, own_places, 16, pack, nodes)
    pack_thin(vol, rows, node_rows, nodes)
    pl.semaphore_wait(barrier, count)
    for end, to in ((first, half - 1), (last_x, half)):
        @pl.when(at[0] == end)
        def _():
            pl.semaphore_signal(ready, inc=1, device_id=(to, at[1], at[2]), device_id_type=MESH)

    near = Exchange(grid, send1, recv1)
    send_strips(near, pack, strip)
    near.start((0, -1, 0), node_rows, halo.at[own, :, pl.ds(0, 256)])
    near.start((0, -1, 0), rows.at[pl.ds(0, 1)], rows_in.at[pl.ds(0, 1)])
    near.start((0, 1, 0), rows.at[pl.ds(1, 3)], rows_in.at[pl.ds(1, 3)])
    inverse_weight(grid, inv)
    for c in loads[3:]:
        c.wait()
    for x in range(8):
        aux[1 + x, 2] = jnp.where(fl[x] >= 2, inv[3 + x] * COEF, 0.0)
    lower, upper = (-1, 0, 0), (1, 0, 0)
    far = Exchange(grid, send2, recv2)
    far.start(lower, nodes.at[:, 1], nodes.at[:, 9], at[0] == half)
    far.start(upper, nodes.at[:, 8], nodes.at[:, 0], at[0] == half - 1)
    far.start(upper, aux.at[8], aux.at[0], at[0] == half - 1)
    held, more = relay.at[pl.ds(0, 6)], relay.at[pl.ds(6, 3)]
    ways = [
        (half - 1, first, half, nodes.at[:, 8], held, nodes.at[:, 0], 1),
        (half - 1, first, half, aux.at[8], more, aux.at[0], 2),
        (half, last_x, half - 1, nodes.at[:, 1], held, nodes.at[:, 9], 0),
    ]

    def way(j, leg):
        start, end, to, src, mid, dst, index = ways[j]
        if leg == 0:
            return at[0] == start, at[0] == end, pltpu.make_async_remote_copy(
                src_ref=src, dst_ref=mid, send_sem=leave.at[j], recv_sem=pause.at[j],
                device_id=(end, at[1], at[2]), device_id_type=MESH)
        return at[0] == end, at[0] == to, pltpu.make_async_remote_copy(
            src_ref=mid, dst_ref=dst, send_sem=onward.at[j], recv_sem=recv2.at[index],
            device_id=(to, at[1], at[2]), device_id_type=MESH)

    for j in range(3):
        here, _, copy = way(j, 0)
        pl.when(here)(copy.start)
    for j in range(3):
        _, there, copy = way(j, 0)
        pl.when(there)(copy.wait_recv)
        here, _, copy = way(j, 1)
        pl.when(here)(copy.start)
    sums_in[6:8] = jnp.zeros((2, 8, 256), jnp.float32)
    for k in (0, 14):
        vol[k:k + 6, 0:8, :] = jnp.zeros((6, 8, 384), jnp.float32)
        for b in range(3):
            ysum[b, k:k + 6] = jnp.zeros((6, 8, 384), jnp.float32)

    def own_ahead(q, _):
        node_ahead(nodes, ahead, q)
        return 0

    lax.fori_loop(1, 9, own_ahead, 0)

    for k in range(9):
        near.finish_recv(k)
    for k in range(9):
        near.finish_send(k)
    down_first = at[0] == half
    unpack_thin(vol, rows_in, halo)
    main, side = unpack_strips(vol, own_places, 16, strip)
    node_halo(halo, main, side)

    @pl.when(beside)
    def _():
        pl.semaphore_wait(ready, 1)

    far.start(lower, halo.at[1], halo.at[9])
    far.start(upper, halo.at[8], halo.at[0])
    row_sums(vol, ysum, 6, 8)

    def own_sums(i, _):
        x = jnp.where(down_first, 2 * i, 12 - 2 * i)
        t0, t1 = cone_pair(vol, ysum, x)
        psum[pl.ds(x, 2), :, 0:128] = t0
        psum[pl.ds(x, 2), :, 128:256] = t1
        return 0

    far.add(lower, psum.at[pl.ds(0, 6)], sums_in.at[pl.ds(8, 6)])
    far.add(upper, psum.at[pl.ds(8, 6)], sums_in.at[pl.ds(0, 6)])
    far.add(lower, energy.at[pl.ds(3, 3)], energy.at[pl.ds(11, 3)])
    far.add(upper, energy.at[pl.ds(8, 2)], energy.at[pl.ds(0, 2)])

    def begin(low, high, one):
        far.begin(low, down_first if one else jnp.logical_not(down_first))
        far.begin(high, jnp.logical_not(down_first) if one else down_first)

    lax.fori_loop(0, 3, own_sums, 0, unroll=True)
    begin(5, 6, True)

    def scaled(x):
        return element_energy(modes, x + 1, aux[x + 1, 0], aux[x + 1, 1]) * aux[x + 1, 2]

    def own_modes(i, _):
        node_modes(nodes, ahead, halo, halo_up, modes, jnp.where(down_first, 1 + i, 8 - i))
        return 0

    def energies(i, _):
        x = jnp.where(down_first, i, 6 - i)
        energy[x + 3] = scaled(x)
        return 0

    lax.fori_loop(0, 4, own_modes, 0, unroll=True)
    lax.fori_loop(0, 3, energies, 0, unroll=True)
    begin(7, 8, True)
    lax.fori_loop(3, 7, own_sums, 0)
    begin(5, 6, False)
    lax.fori_loop(4, 8, own_modes, 0)
    lax.fori_loop(3, 7, energies, 0)
    begin(7, 8, False)
    denom = math.tanh(sharpness * threshold) + math.tanh(sharpness * (1.0 - threshold))
    base = math.tanh(sharpness * threshold)
    up_first = jnp.logical_not(down_first)
    last = Exchange(grid, send3, recv3)

    def side_planes(low):
        high = jnp.logical_not(low)
        for k in (1, 2, 4):
            far.finish_recv(k, low)
        for k in (0, 3):
            far.finish_recv(k, high)
        q, x = jnp.where(low, 0, 9), jnp.where(low, -1, 7)
        node_ahead(nodes, ahead, q)
        node_modes(nodes, ahead, halo, halo_up, modes, q)
        energy[x + 3] = scaled(x)
        for k in (6, 8):
            far.finish_recv(k, low)
        for k in (5, 7):
            far.finish_recv(k, high)

    def chain(first, planes):
        for j in range(planes):
            k = first + j
            total = psum[k] + sums_in[k]
            hyper = jnp.tanh(sharpness * (total * inv[k] - threshold))
            smooth = (base + hyper) * (1.0 / denom)
            slope = (1.0 - hyper * hyper) * (sharpness / denom)
            vol2[k, 0:8, 0:256] = smooth * smooth * slope * energy[k]

    early, late = jnp.where(down_first, 6, 0), jnp.where(down_first, 0, 8)
    places = [(i, early + i) for i in range(8)] + [(8 + i, late + i) for i in range(6)]
    side_planes(up_first)
    chain(early, 8)
    pack_rows(vol2, early, 4, rows2)
    send_rows(last, rows2, rows_in2)
    pack_strips(vol2, places[:8], 8, pack2, None)
    side_planes(down_first)
    chain(late, 6)
    pack_strips(vol2, places[8:], 8, pack2, None)
    send_strips(last, pack2, strip2)
    pack_rows(vol2, late, 3, rows3)
    send_rows(last, rows3, rows_in3)
    for ex in (far, last):
        for k in range(len(ex.items)):
            ex.finish_send(k)
    for j in range(3):
        for leg in range(2):
            here, _, copy = way(j, leg)
            pl.when(here)(copy.wait_send)
    for k in (0, 1):
        last.finish_recv(k)
    unpack_rows(vol2, early, 4, rows_in2)
    for k in range(2, 10):
        last.finish_recv(k)
    unpack_strips(vol2, places, 8, strip2)
    unpack_rows(vol2, late, 3, rows_in3)
    row_sums(vol2, ysum2, 0, 14)

    def final(i, _):
        planes = pl.ds(2 * i, 2)
        t0, t1 = cone_pair(vol2, ysum2, 2 * i)
        out[planes, :, 0:128] = jnp.where(fl[planes, :, 0:128] >= 2, t0, 0.0)
        out[planes, :, 128:256] = jnp.where(fl[planes, :, 128:256] >= 2, t1, 0.0)
        return 0

    lax.fori_loop(0, 4, final, 0, unroll=True)


def on_device(grid, *args):
    f32, i32 = jnp.float32, jnp.int32
    V = pltpu.VMEM
    dma = pltpu.SemaphoreType.DMA
    strip, pack = V((2, 3, 8, 128), f32), V((2, 8, 128), f32)
    return pl.pallas_call(
        functools.partial(kernel, grid),
        out_shape=pltpu.VMEM((8, 8, 256), f32),
        in_specs=[pl.BlockSpec(memory_space=pl.ANY)] * 6,
        out_specs=pl.BlockSpec(memory_space=pltpu.VMEM),
        scratch_shapes=[
            V((20, 16, 384), f32), V((14, 16, 384), f32), V((3, 20, 8, 384), f32), V((3, 14, 8, 384), f32),
            V((14, 8, 256), f32), V((14, 8, 256), f32),
            V((4, 8, 256), f32), V((4, 8, 256), f32), strip, pack,
            V((2, 4, 8, 256), f32), V((2, 4, 8, 256), f32), V((2, 3, 8, 256), f32), V((2, 3, 8, 256), f32), strip, pack,
            V((6, 10, 8, 256), f32), V((8, 8, 256), f32), V((10, 6, 8, 256), f32), V((10, 8, 384), f32), V((10, 8, 256), f32),
            V((10, 6, 4, 8, 256), f32),
            V((9, 3, 8, 256), f32), V((8, 8, 256), i32), V((14, 8, 256), f32), V((14, 8, 256), f32),
            V((9, 8, 256), f32),
            dma((6,)), pltpu.SemaphoreType.REGULAR, dma((3,)), dma((3,)), dma((3,)), dma((9,)), dma((9,)), dma((9,)), dma((9,)), dma((10,)), dma((10,)),
        ],
        compiler_params=pltpu.CompilerParams(
            collective_id=0, has_side_effects=True, vmem_limit_bytes=63 << 20),
        name="sensitivity",
    )(*args)


def solution(mesh):
    grid = tuple(mesh.shape[a] for a in AXES)
    brick = P("gx", "gy", "gz")
    field = P(None, "gx", "gy", "gz")
    return jax.shard_map(
        functools.partial(on_device, grid), mesh=mesh,
        in_specs=(brick, brick, field, field, brick, brick), out_specs=brick, check_vma=False,
    )
```

```python
import functools
import itertools
import math

import jax
import jax.numpy as jnp
from jax import lax
from jax.experimental import pallas as pl
from jax.experimental.pallas import tpu as pltpu
from jax.sharding import PartitionSpec as P

poisson = 0.45
sharpness = 4.0
threshold = 0.5
stiff_floor = 0.001
cone_radius = 3.5

AXES = ("gx", "gy", "gz")
NX, NY, NZ = 8, 8, 256
MESH = pl.DeviceIdType.MESH
NEAR = [(0, 1, 1), (0, -1, 1), (0, 1, -1), (0, -1, -1), (0, -1, 0), (0, 1, 0), (0, 0, 1), (0, 0, -1)]
COEF = -3.0 * (1.0 - stiff_floor)


def cone_weight(a, b, c):
    r2 = a * a + b * b + c * c
    return cone_radius - math.sqrt(r2) if r2 < cone_radius * cone_radius else 0.0


def place(grid):
    return [lax.axis_index(a) for a in AXES]


def peer(grid, offset):
    at = [lax.axis_index(a) for a in AXES]
    target = tuple(a + o for a, o in zip(at, offset))
    ok = None
    for t, o, n in zip(target, offset, grid):
        if o:
            inside = t >= 0 if o < 0 else t < n
            ok = inside if ok is None else ok & inside
    return target, ok


def opposite(offset):
    return tuple(-o for o in offset)


class Exchange:
    def __init__(self, grid, send, recv):
        self.grid, self.send, self.recv = grid, send, recv
        self.items, self.unless = [], []

    def copy(self, index):
        offset, src, dst = self.items[index]
        target, ok = peer(self.grid, offset)
        return ok, pltpu.make_async_remote_copy(
            src_ref=src, dst_ref=dst, send_sem=self.send.at[index], recv_sem=self.recv.at[index],
            device_id=target, device_id_type=MESH,
        )

    def add(self, offset, src, dst, unless=None):
        self.items.append((offset, src, dst))
        self.unless.append(unless)
        return len(self.items) - 1

    def sends(self, index):
        ok, copy = self.copy(index)
        unless = self.unless[index]
        return (ok if unless is None else ok & jnp.logical_not(unless)), copy

    def begin(self, index, when=None):
        ok, copy = self.sends(index)
        pl.when(ok if when is None else ok & when)(copy.start)

    def start(self, offset, src, dst, unless=None):
        self.begin(self.add(offset, src, dst, unless))

    def finish_recv(self, index, when=None):
        offset, src, dst = self.items[index]
        _, ok = peer(self.grid, opposite(offset))
        _, copy = self.copy(index)
        pl.when(ok if when is None else ok & when)(copy.wait_recv)
        missing = jnp.logical_not(ok)

        @pl.when(missing if when is None else missing & when)
        def _():
            dst[...] = jnp.zeros(dst.shape, jnp.float32)

    def finish_send(self, index, done=None):
        ok, copy = self.sends(index)
        pl.when(ok if done is None else ok & jnp.logical_not(done))(copy.wait_send)


def roll(value, by, axis):
    by = by % value.shape[axis]
    return value if by == 0 else pltpu.roll(value, by, axis)


def iota(shape, dim):
    return lax.broadcasted_iota(jnp.int32, shape, dim)


def row_sums(vol, ysum, first, count, lanes=(0, 384)):
    at, wide = pl.ds(lanes[0], lanes[1] - lanes[0]), lanes[1] - lanes[0]
    row = iota((2, 8, wide), 1)

    def rows(p, _):
        planes = pl.ds(first + 2 * p, 2)
        low, high = vol[planes, 0:8, at], vol[planes, 8:16, at]
        for b in (1, 2, 3):
            up = roll(jnp.where(row < b, high, low), -b, 1)
            down = roll(jnp.where(row >= 8 - b, high, low), b, 1)
            ysum[b - 1, planes, :, at] = up + down
        return 0

    lax.fori_loop(0, count // 2, rows, 0, unroll=True)


def plane_sums(vol, ysum, x, lanes):
    at = pl.ds(lanes[0], lanes[1] - lanes[0])
    sums = {}

    def get(b, k):
        return vol[pl.ds(x + k, 2), 0:8, at] if b == 0 else ysum[b - 1, pl.ds(x + k, 2), :, at]

    for a in range(4):
        for b in range(4):
            if a * a + b * b < 12.25:
                sums[a, b] = get(b, 3) if a == 0 else get(b, 3 - a) + get(b, 3 + a)
    groups = {}
    for (a, b), value in sums.items():
        key = (min(a, b), max(a, b))
        groups[key] = groups[key] + value if key in groups else value
    shifted = []
    for c in range(4):
        g = None
        for (a, b), value in groups.items():
            w = cone_weight(a, b, c)
            if w > 0:
                g = value * w if g is None else g + value * w
        shifted.append(g)
    return shifted


def cone_pair(vol, ysum, x):
    lane = iota((2, 8, 128), 2)
    for c, g in enumerate(plane_sums(vol, ysum, x, (0, 384))):
        g0, g1, gh = g[:, :, 0:128], g[:, :, 128:256], g[:, :, 256:384]
        if c == 0:
            t0, t1 = g0, g1
        else:
            t0 = t0 + roll(jnp.where(lane < c, g1, g0), -c, 2) + roll(
                jnp.where(lane >= 128 - c, gh, g0), c, 2)
            t1 = t1 + roll(jnp.where(lane < c, gh, g1), -c, 2) + roll(
                jnp.where(lane >= 128 - c, g0, g1), c, 2)
    return t0, t1


def cone_inner(vol, ysum, x):
    lane = iota((2, 8, 128), 2)
    for c, g in enumerate(plane_sums(vol, ysum, x, (0, 256))):
        g0, g1 = g[:, :, 0:128], g[:, :, 128:256]
        if c == 0:
            t0, t1 = g0, g1
        else:
            t0 = t0 + roll(jnp.where(lane < c, g1, g0), -c, 2) + roll(
                jnp.where(lane >= 128 - c, 0.0, g0), c, 2)
            t1 = t1 + roll(jnp.where(lane < c, 0.0, g1), -c, 2) + roll(
                jnp.where(lane >= 128 - c, g0, g1), c, 2)
    return t0, t1


def cone_halo(vol, ysum, x):
    lane = iota((2, 8, 128), 2)
    t0, t1 = 0.0, 0.0
    for c, g in enumerate(plane_sums(vol, ysum, x, (256, 384))):
        if c:
            t0 = t0 + roll(jnp.where(lane >= 128 - c, g, 0.0), c, 2)
            t1 = t1 + roll(jnp.where(lane < c, g, 0.0), -c, 2)
    return t0, t1


def inverse_weight(grid, out):
    gx, gy, gz = [lax.axis_index(a) for a in AXES]
    y = gy * NY + iota((NY, NZ), 0)
    z = gz * NZ + iota((NY, NZ), 1)

    def pairs(pos, by, size):
        def inside(v):
            return ((v >= 0) & (v < size)).astype(jnp.float32)
        return inside(pos + by) + inside(pos - by) if by else inside(pos)

    ys = [None] + [pairs(y, b, grid[1] * NY) for b in (1, 2, 3)]
    zs = [None] + [pairs(z, c, grid[2] * NZ) for c in (1, 2, 3)]
    fs = []
    for a in range(4):
        f = jnp.full((NY, NZ), 0.0, jnp.float32)
        for b in range(4):
            for c in range(4):
                w = cone_weight(a, b, c)
                if w > 0:
                    term = jnp.float32(w)
                    term = term if b == 0 else term * ys[b]
                    term = term if c == 0 else term * zs[c]
                    f = f + term
        fs.append(f)
    for k in range(14):
        px = gx * NX + k - 3
        w = fs[0] * pairs(px, 0, grid[0] * NX)
        for a in (1, 2, 3):
            w = w + fs[a] * pairs(px, a, grid[0] * NX)
        out[k] = 1.0 / w


def pack_rows(vol, first, half, rows):
    row = iota((8, 256), 0)
    for k in range(half):
        a, b = vol[first + k, 0:8, 0:256], vol[first + half + k, 0:8, 0:256]
        b = roll(b, 4, 0)
        rows[0, k] = jnp.where(row < 4, a, b)
        rows[1, k] = jnp.where(row < 4, b, a)


def pack_thin(vol, rows, node_rows, nodes):
    for p in range(8):
        for f in range(6):
            node_rows[p, f:f + 1, :] = nodes[f, 1 + p, 0:1, :]
        node_rows[p, 6:8, :] = jnp.zeros((2, 256), jnp.float32)
        for j, r in enumerate((0, 1, 2, 5, 6, 7)):
            rows[j, p:p + 1, :] = vol[6 + p, r:r + 1, 0:256]


def unpack_thin(vol, rows_in):
    row = iota((8, 256), 0)
    for p in range(8):
        value = None
        for j, r in enumerate((0, 1, 2, 5, 6, 7)):
            here = jnp.broadcast_to(rows_in[j, p:p + 1, :], (8, 256))
            value = here if value is None else jnp.where(row == r, here, value)
        vol[6 + p, 8:16, 0:256] = value


def pack_strips(vol, places, slot, pack, nodes):
    lane = iota((8, 128), 1)
    down, up = pack[0], pack[1]
    for i, p in places:
        first, last = vol[p, 0:8, 0:128], vol[p, 0:8, 128:256]
        d, u = roll(first, slot * i, 1), roll(last, slot * i, 1)
        if i == 0:
            down, up = d, u
        else:
            down = jnp.where((lane >= slot * i) & (lane < slot * i + 3), d, down)
            up = jnp.where((lane >= slot * i - 3) & (lane < slot * i), u, up)
        if nodes is not None:
            for f in range(6):
                n = roll(nodes[f, 1 + i, :, 0:128], slot * i + 3 + f, 1)
                down = jnp.where(lane == slot * i + 3 + f, n, down)
    pack[0] = down
    pack[1] = up


def send_strips(ex, pack, strip):
    for o in NEAR:
        _, dy, dz = o
        if dz:
            k = 0 if dz < 0 else 1
            ex.start(o, pack.at[k], strip.at[k, 1 - dy])


def send_rows(ex, rows, rows_in):
    for k, dy in enumerate((-1, 1)):
        ex.start((0, dy, 0), rows.at[k], rows_in.at[k])


def unpack_rows(vol, first, half, rows_in):
    row = iota((8, 256), 0)
    for k in range(half):
        from_upper, from_lower = rows_in[0, k], rows_in[1, k]
        vol[first + k, 8:16, 0:256] = jnp.where(row < 4, from_upper, from_lower)
        vol[first + half + k, 8:16, 0:256] = roll(jnp.where(row < 4, from_lower, from_upper), 4, 0)


def unpack_strips(vol, places, slot, strip):
    rowl = iota((8, 128), 0)
    lane = iota((8, 128), 1)
    both = [jnp.where((lane & (slot - 1)) < slot - 4, strip[0, dy], strip[1, dy]) for dy in range(3)]
    side = jnp.where(rowl < 4, both[2], both[0])
    for i, p in places:
        vol[p, 0:8, 256:384] = roll(both[1], -slot * i, 1)
        vol[p, 8:16, 256:384] = roll(side, -slot * i, 1)
    return both[1], both[2]


def node_halo(halo, main, side):
    lane = iota((8, 128), 1)
    for p in range(8):
        a = roll(main, -(16 * p + 3), 1)
        b = roll(roll(side, -(16 * p + 3) + 8, 1), -1, 0)
        halo[1 + p, :, 256:384] = jnp.where(lane < 8, a, b)


def node_ahead(nodes, ahead, q):
    lane = iota((8, 128), 1)
    for f in range(6):
        v0, v1 = roll(nodes[f, q, :, 0:128], -1, 1), roll(nodes[f, q, :, 128:256], -1, 1)
        ahead[q, f, :, 0:128] = jnp.where(lane == 127, v1, v0)
        ahead[q, f, :, 128:256] = v1


def node_modes(nodes, ahead, halo, halo_up, modes, q):
    lane = iota((8, 128), 1)
    row = iota((8, 128), 0)
    hs = halo[q, :, 256:384]
    hm = jnp.where(row == 7, roll(hs, -8, 1), roll(hs, -1, 0))
    v0, v1 = roll(halo[q, :, 0:128], -1, 1), roll(halo[q, :, 128:256], -1, 1)
    halo_up[q, :, 0:128] = jnp.where(lane == 127, v1, v0)
    halo_up[q, :, 128:256] = v1

    def spread(ref, f, k):
        return jnp.broadcast_to(ref[q, f:f + 1, 128 * k:128 * k + 128], (8, 128))

    for f in range(6):
        for k in range(2):
            at = pl.ds(128 * k, 128)
            n, s = nodes[f, q, :, at], ahead[q, f, :, at]
            e, r = spread(halo, f, k), spread(halo_up, f, k)
            if k == 1:
                s = jnp.where(lane == 127, roll(hs, 127 - f, 1), s)
                r = jnp.where(lane == 127, roll(hm, 127 - f, 1), r)
            a, d = n + s, s - n
            ay = jnp.where(row == 7, e + r, roll(a, -1, 0))
            dy = jnp.where(row == 7, r - e, roll(d, -1, 0))
            modes[q, f, 0, :, at] = a + ay
            modes[q, f, 1, :, at] = d + dy
            modes[q, f, 2, :, at] = ay - a
            modes[q, f, 3, :, at] = dy - d


def element_energy(modes, x, press, mult):
    shear = 1.0 / (2.0 * (1.0 + poisson))
    bulk = 1.0 / (3.0 * (1.0 - 2.0 * poisson))

    def both_of(f, m):
        return modes[x, f, m], modes[x + 1, f, m]

    def field(base):
        out = []
        for c in range(3):
            aa, ad, da, dd = (both_of(base + c, m) for m in range(4))
            out.append(dict(
                X=aa[1] - aa[0], Y=da[0] + da[1], Z=ad[0] + ad[1],
                XY=da[1] - da[0], XZ=ad[1] - ad[0], YZ=dd[0] + dd[1], XYZ=dd[1] - dd[0]))
        return out

    u, l = field(0), field(3)

    def strains(v):
        a, b, c = v
        one = (a["X"], b["Y"], c["Z"], a["Y"] + b["X"], b["Z"] + c["Y"], a["Z"] + c["X"])
        xi = (None, b["XY"], c["XZ"], a["XY"], b["XZ"] + c["XY"], a["XZ"])
        eta = (a["XY"], None, c["YZ"], b["XY"], b["YZ"], a["YZ"] + c["XY"])
        zeta = (a["XZ"], b["YZ"], None, a["YZ"] + b["XZ"], c["YZ"], c["XZ"])
        return one, xi, eta, zeta

    su, sl = strains(u), strains(l)
    total = None
    for kind in range(4):
        eu, el = su[kind], sl[kind]
        normal, tr_u, tr_l = None, None, None
        for k in range(3):
            if eu[k] is not None:
                t = eu[k] * el[k]
                normal = t if normal is None else normal + t
                tr_u = eu[k] if tr_u is None else tr_u + eu[k]
                tr_l = el[k] if tr_l is None else tr_l + el[k]
        gamma = eu[3] * el[3] + eu[4] * el[4] + eu[5] * el[5]
        scale = shear / 16.0 if kind == 0 else shear / 48.0
        part = (2.0 * (normal - tr_u * tr_l * (1.0 / 3.0)) + gamma) * scale
        if kind == 0:
            div_u, div_l = tr_u * 0.25, tr_l * 0.25
        total = part if total is None else total + part
    pure = u[0]["XYZ"] * l[0]["XYZ"] + u[1]["XYZ"] * l[1]["XYZ"] + u[2]["XYZ"] * l[2]["XYZ"]
    total = total + pure * (shear * (10.0 / 3.0) / 144.0)
    return total + div_l * press + mult * div_u - mult * press * (1.0 / bulk)


def kernel(grid, design, flags, disp, adj, press, mult, out,
           vol, vol2, ysum, ysum2, inner, psum, sums_in, rows, rows_in, strip, pack, rows2, rows_in2, rows3, rows_in3, strip2, pack2,
           nodes, node_rows, ahead, halo, halo_up, modes, aux, fl, inv, energy,
           relay, blank, edge_out, edge_in, load_sem, ready, leave, pause, onward, send1, recv1, send2, recv2, send3, recv3):
    barrier = pltpu.get_barrier_semaphore()
    at = [lax.axis_index(a) for a in AXES]
    first, last_x, half = 0, grid[0] - 1, grid[0] // 2
    beside = (at[0] == half - 1) | (at[0] == half)
    count = jnp.int32(0)

    def greet(target, ok, counts):
        @pl.when(ok)
        def _():
            pl.semaphore_signal(barrier, inc=1, device_id=target, device_id_type=MESH)

        return count + jnp.int32(1) * counts

    for end in (first, last_x):
        count = greet((end, at[1], at[2]), beside, 2 * (at[0] == end))
    for end, to in ((first, half - 1), (last_x, half)):
        count = greet((to, at[1], at[2]), at[0] == end, at[0] == to)
    own = pl.ds(1, 8)
    loads = [
        (design, vol.at[pl.ds(6, 8), pl.ds(0, 8), pl.ds(0, 256)]),
        (disp, nodes.at[pl.ds(0, 3), own]),
        (adj, nodes.at[pl.ds(3, 3), own]),
        (flags, fl), (press, aux.at[own, 0]), (mult, aux.at[own, 1]),
    ]
    loads = [pltpu.make_async_copy(s, d, load_sem.at[k]) for k, (s, d) in enumerate(loads)]
    for c in loads[:3]:
        c.start()
    for o in NEAR:
        target, ok = peer(grid, o)
        count = greet(target, ok, ok)
    for dx in (-1, 1):
        target, ok = peer(grid, (dx, 0, 0))
        ok = ok & (at[0] != (half if dx < 0 else half - 1))
        count = greet(target, ok, ok)
    for c in loads[:3]:
        c.wait()
    for c in loads[3:]:
        c.start()
    own_places = [(i, 6 + i) for i in range(8)]
    pack_strips(vol, own_places, 16, pack, nodes)
    pack_thin(vol, rows, node_rows, nodes)
    pl.semaphore_wait(barrier, count)
    for end, to in ((first, half - 1), (last_x, half)):
        @pl.when(at[0] == end)
        def _():
            pl.semaphore_signal(ready, inc=1, device_id=(to, at[1], at[2]), device_id_type=MESH)

    near = Exchange(grid, send1, recv1)
    send_strips(near, pack, strip)
    near.start((0, -1, 0), rows.at[pl.ds(0, 3)], rows_in.at[pl.ds(0, 3)])
    near.start((0, 1, 0), rows.at[pl.ds(3, 3)], rows_in.at[pl.ds(3, 3)])
    near.start((0, -1, 0), node_rows, halo.at[own, :, pl.ds(0, 256)])
    inverse_weight(grid, inv)
    for c in loads[3:]:
        c.wait()
    for x in range(8):
        aux[1 + x, 2] = jnp.where(fl[x] >= 2, inv[3 + x] * COEF, 0.0)
    lower, upper = (-1, 0, 0), (1, 0, 0)
    far = Exchange(grid, send2, recv2)
    far.start(lower, nodes.at[:, 1], nodes.at[:, 9], at[0] == half)
    far.start(upper, nodes.at[:, 8], nodes.at[:, 0], at[0] == half - 1)
    far.start(upper, aux.at[8], aux.at[0], at[0] == half - 1)
    held, more = relay.at[pl.ds(0, 6)], relay.at[pl.ds(6, 3)]
    ways = [
        (half - 1, first, half, nodes.at[:, 8], held, nodes.at[:, 0], 1),
        (half - 1, first, half, aux.at[8], more, aux.at[0], 2),
        (half, last_x, half - 1, nodes.at[:, 1], held, nodes.at[:, 9], 0),
    ]

    def way(j, leg):
        start, end, to, src, mid, dst, index = ways[j]
        if leg == 0:
            return at[0] == start, at[0] == end, pltpu.make_async_remote_copy(
                src_ref=src, dst_ref=mid, send_sem=leave.at[j], recv_sem=pause.at[j],
                device_id=(end, at[1], at[2]), device_id_type=MESH)
        return at[0] == end, at[0] == to, pltpu.make_async_remote_copy(
            src_ref=mid, dst_ref=dst, send_sem=onward.at[j], recv_sem=recv2.at[index],
            device_id=(to, at[1], at[2]), device_id_type=MESH)

    for j in range(3):
        here, _, copy = way(j, 0)
        pl.when(here)(copy.start)
    for j in range(3):
        _, there, copy = way(j, 0)
        pl.when(there)(copy.wait_recv)
        here, _, copy = way(j, 1)
        pl.when(here)(copy.start)
    sums_in[6:8] = jnp.zeros((2, 8, 256), jnp.float32)
    for k in (0, 14):
        vol[k:k + 6, 0:8, :] = jnp.zeros((6, 8, 384), jnp.float32)
        for b in range(3):
            ysum[b, k:k + 6] = jnp.zeros((6, 8, 384), jnp.float32)

    def own_ahead(q, _):
        node_ahead(nodes, ahead, q)
        return 0

    lax.fori_loop(1, 9, own_ahead, 0)

    down_first = at[0] == half
    def scaled(x):
        return element_energy(modes, x + 1, aux[x + 1, 0], aux[x + 1, 1]) * aux[x + 1, 2]

    def own_modes(i, _):
        node_modes(nodes, ahead, halo, halo_up, modes, jnp.where(down_first, 1 + i, 8 - i))
        return 0

    def first_modes(i, _):
        node_modes(nodes, ahead, blank, halo_up, modes, jnp.where(down_first, 1 + i, 8 - i))
        return 0

    def energies(i, _):
        x = jnp.where(down_first, i, 6 - i)
        energy[x + 3] = scaled(x)
        return 0


    @pl.when(beside)
    def _():
        blank[...] = jnp.zeros(blank.shape, jnp.float32)
        lax.fori_loop(0, 4, first_modes, 0, unroll=True)
        lax.fori_loop(0, 3, energies, 0, unroll=True)
        pl.semaphore_wait(ready, 1)

    for k in (3, 4):
        far.add(*((lower, halo.at[1], halo.at[9]) if k == 3 else (upper, halo.at[8], halo.at[0])))
    far.add(lower, psum.at[pl.ds(0, 6)], sums_in.at[pl.ds(8, 6)])
    far.add(upper, psum.at[pl.ds(8, 6)], sums_in.at[pl.ds(0, 6)])
    far.add(lower, energy.at[pl.ds(3, 3)], energy.at[pl.ds(11, 3)])
    far.add(upper, energy.at[pl.ds(8, 2)], energy.at[pl.ds(0, 2)])
    far.add(lower, edge_out, edge_in, at[0] != half)
    far.add(upper, edge_out, edge_in, at[0] != half - 1)
    far.begin(7, at[0] == half)
    far.begin(8, at[0] == half - 1)

    for k in range(8):
        near.finish_recv(k)
    unpack_thin(vol, rows_in)
    main, side = unpack_strips(vol, own_places, 16, strip)
    node_halo(halo, main, side)

    row_sums(vol, ysum, 6, 8)

    def own_sums(i, _):
        x = jnp.where(down_first, 2 * i, 12 - 2 * i)
        t0, t1 = cone_pair(vol, ysum, x)
        psum[pl.ds(x, 2), :, 0:128] = t0
        psum[pl.ds(x, 2), :, 128:256] = t1
        return 0


    def begin(low, high, one):
        far.begin(low, down_first if one else jnp.logical_not(down_first))
        far.begin(high, jnp.logical_not(down_first) if one else down_first)

    lax.fori_loop(0, 3, own_sums, 0, unroll=True)
    begin(5, 6, True)
    near.finish_recv(8)
    for k in (3, 4):
        far.begin(k)
    for k in range(9):
        near.finish_send(k)

    lax.fori_loop(0, 4, own_modes, 0, unroll=True)
    for ex, low in ((7, True), (8, False)):
        pl.when(beside & (down_first if low else jnp.logical_not(down_first)))(far.sends(ex)[1].wait_send)
    lax.fori_loop(0, 3, energies, 0, unroll=True)

    @pl.when(beside)
    def _():
        lane = iota((8, 128), 1)
        first_plane = jnp.where(down_first, 3, 8)
        strip_of = None
        for j in range(3):
            edge_out[j:j + 1, 0:256] = energy[first_plane + j, 7:8, :]
            moved = roll(energy[first_plane + j, :, 128:256], j - 127, 1)
            strip_of = moved if j == 0 else jnp.where(lane == j, moved, strip_of)
        edge_out[:, 256:384] = strip_of

    far.begin(9)
    far.begin(10)
    far.begin(7, jnp.logical_not(beside) & down_first)
    far.begin(8, jnp.logical_not(beside) & jnp.logical_not(down_first))
    lax.fori_loop(3, 7, own_sums, 0)
    begin(5, 6, False)
    lax.fori_loop(4, 8, own_modes, 0)
    lax.fori_loop(3, 7, energies, 0)
    begin(7, 8, False)
    denom = math.tanh(sharpness * threshold) + math.tanh(sharpness * (1.0 - threshold))
    base = math.tanh(sharpness * threshold)
    up_first = jnp.logical_not(down_first)
    last = Exchange(grid, send3, recv3)

    def side_planes(low):
        high = jnp.logical_not(low)
        for k in (1, 2, 4):
            far.finish_recv(k, low)
        for k in (0, 3):
            far.finish_recv(k, high)
        q, x = jnp.where(low, 0, 9), jnp.where(low, -1, 7)
        node_ahead(nodes, ahead, q)
        node_modes(nodes, ahead, halo, halo_up, modes, q)
        energy[x + 3] = scaled(x)
        for k in (6, 8):
            far.finish_recv(k, low)
        for k in (5, 7):
            far.finish_recv(k, high)

    def put_edge():
        far.finish_recv(9, at[0] == half - 1)
        far.finish_recv(10, at[0] == half)
        row, lane = iota((8, 256), 0), iota((8, 256), 1)
        for j in range(3):
            @pl.when(beside & up_first if j == 2 else beside)
            def _():
                k = jnp.where(down_first, 0, 11) + j
                edge = roll(edge_in[:, 256:384], 127 - j, 1)
                value = jnp.where(lane == 255, jnp.concatenate([edge, edge], axis=1), energy[k])
                energy[k] = jnp.where(row == 7, jnp.broadcast_to(edge_in[j:j + 1, 0:256], (8, 256)), value)

    def chain(first, planes):
        for j in range(planes):
            k = first + j
            total = psum[k] + sums_in[k]
            hyper = jnp.tanh(sharpness * (total * inv[k] - threshold))
            smooth = (base + hyper) * (1.0 / denom)
            slope = (1.0 - hyper * hyper) * (sharpness / denom)
            vol2[k, 0:8, 0:256] = smooth * smooth * slope * energy[k]

    early, late = jnp.where(down_first, 6, 0), jnp.where(down_first, 0, 8)
    places = [(i, early + i) for i in range(8)] + [(8 + i, late + i) for i in range(6)]
    side_planes(up_first)
    chain(early, 8)
    pack_rows(vol2, early, 4, rows2)
    send_rows(last, rows2, rows_in2)
    pack_strips(vol2, places[:8], 8, pack2, None)
    side_planes(down_first)
    put_edge()
    chain(late, 6)
    pack_strips(vol2, places[8:], 8, pack2, None)
    send_strips(last, pack2, strip2)
    pack_rows(vol2, late, 3, rows3)
    send_rows(last, rows3, rows_in3)
    for ex in (far, last):
        for k in range(len(ex.items)):
            done = beside & (down_first if k == 7 else up_first) if ex is far and k in (7, 8) else None
            ex.finish_send(k, done)
    for j in range(3):
        for leg in range(2):
            here, _, copy = way(j, leg)
            pl.when(here)(copy.wait_send)
    for k in (0, 1):
        last.finish_recv(k)
    unpack_rows(vol2, early, 4, rows_in2)
    for k in (8, 9):
        last.finish_recv(k)
    unpack_rows(vol2, late, 3, rows_in3)
    row_sums(vol2, ysum2, 0, 14, (0, 256))
    for i in range(4):
        planes = pl.ds(2 * i, 2)
        t0, t1 = cone_inner(vol2, ysum2, 2 * i)
        inner[planes, :, 0:128] = t0
        inner[planes, :, 128:256] = t1
    for k in range(2, 8):
        last.finish_recv(k)
    unpack_strips(vol2, places, 8, strip2)
    row_sums(vol2, ysum2, 0, 14, (256, 384))
    for i in range(4):
        planes = pl.ds(2 * i, 2)
        for half_at, t in zip((0, 128), cone_halo(vol2, ysum2, 2 * i)):
            lanes = pl.ds(half_at, 128)
            out[planes, :, lanes] = jnp.where(fl[planes, :, lanes] >= 2, inner[planes, :, lanes] + t, 0.0)


def on_device(grid, *args):
    f32, i32 = jnp.float32, jnp.int32
    V = pltpu.VMEM
    dma = pltpu.SemaphoreType.DMA
    strip, pack = V((2, 3, 8, 128), f32), V((2, 8, 128), f32)
    return pl.pallas_call(
        functools.partial(kernel, grid),
        out_shape=pltpu.VMEM((8, 8, 256), f32),
        in_specs=[pl.BlockSpec(memory_space=pl.ANY)] * 6,
        out_specs=pl.BlockSpec(memory_space=pltpu.VMEM),
        scratch_shapes=[
            V((20, 16, 384), f32), V((14, 16, 384), f32), V((3, 20, 8, 384), f32), V((3, 14, 8, 384), f32), V((8, 8, 256), f32),
            V((14, 8, 256), f32), V((14, 8, 256), f32),
            V((6, 8, 256), f32), V((6, 8, 256), f32), strip, pack,
            V((2, 4, 8, 256), f32), V((2, 4, 8, 256), f32), V((2, 3, 8, 256), f32), V((2, 3, 8, 256), f32), strip, pack,
            V((6, 10, 8, 256), f32), V((8, 8, 256), f32), V((10, 6, 8, 256), f32), V((10, 8, 384), f32), V((10, 8, 256), f32),
            V((10, 6, 4, 8, 256), f32),
            V((9, 3, 8, 256), f32), V((8, 8, 256), i32), V((14, 8, 256), f32), V((14, 8, 256), f32),
            V((9, 8, 256), f32), V((10, 8, 384), f32), V((8, 384), f32), V((8, 384), f32),
            dma((6,)), pltpu.SemaphoreType.REGULAR, dma((3,)), dma((3,)), dma((3,)), dma((9,)), dma((9,)), dma((11,)), dma((11,)), dma((10,)), dma((10,)),
        ],
        compiler_params=pltpu.CompilerParams(
            collective_id=0, has_side_effects=True, vmem_limit_bytes=63 << 20),
        name="sensitivity",
    )(*args)


def solution(mesh):
    grid = tuple(mesh.shape[a] for a in AXES)
    brick = P("gx", "gy", "gz")
    field = P(None, "gx", "gy", "gz")
    return jax.shard_map(
        functools.partial(on_device, grid), mesh=mesh,
        in_specs=(brick, brick, field, field, brick, brick), out_specs=brick, check_vma=False,
    )
```

```python
import functools
import itertools
import math

import jax
import jax.numpy as jnp
from jax import lax
from jax.experimental import pallas as pl
from jax.experimental.pallas import tpu as pltpu
from jax.sharding import PartitionSpec as P

poisson = 0.45
sharpness = 4.0
threshold = 0.5
stiff_floor = 0.001
cone_radius = 3.5

AXES = ("gx", "gy", "gz")
NX, NY, NZ = 8, 8, 256
MESH = pl.DeviceIdType.MESH
NEAR = [(0, 1, 1), (0, -1, 1), (0, 1, -1), (0, -1, -1), (0, -1, 0), (0, 1, 0), (0, 0, 1), (0, 0, -1)]
COEF = -3.0 * (1.0 - stiff_floor)


def cone_weight(a, b, c):
    r2 = a * a + b * b + c * c
    return cone_radius - math.sqrt(r2) if r2 < cone_radius * cone_radius else 0.0


def place(grid):
    return [lax.axis_index(a) for a in AXES]


def peer(grid, offset):
    at = [lax.axis_index(a) for a in AXES]
    target = tuple(a + o for a, o in zip(at, offset))
    ok = None
    for t, o, n in zip(target, offset, grid):
        if o:
            inside = t >= 0 if o < 0 else t < n
            ok = inside if ok is None else ok & inside
    return target, ok


def opposite(offset):
    return tuple(-o for o in offset)


class Exchange:
    def __init__(self, grid, send, recv):
        self.grid, self.send, self.recv = grid, send, recv
        self.items, self.unless = [], []

    def copy(self, index):
        offset, src, dst = self.items[index]
        target, ok = peer(self.grid, offset)
        return ok, pltpu.make_async_remote_copy(
            src_ref=src, dst_ref=dst, send_sem=self.send.at[index], recv_sem=self.recv.at[index],
            device_id=target, device_id_type=MESH,
        )

    def add(self, offset, src, dst, unless=None):
        self.items.append((offset, src, dst))
        self.unless.append(unless)
        return len(self.items) - 1

    def sends(self, index):
        ok, copy = self.copy(index)
        unless = self.unless[index]
        return (ok if unless is None else ok & jnp.logical_not(unless)), copy

    def begin(self, index, when=None):
        ok, copy = self.sends(index)
        pl.when(ok if when is None else ok & when)(copy.start)

    def start(self, offset, src, dst, unless=None):
        self.begin(self.add(offset, src, dst, unless))

    def finish_recv(self, index, when=None):
        offset, src, dst = self.items[index]
        _, ok = peer(self.grid, opposite(offset))
        _, copy = self.copy(index)
        pl.when(ok if when is None else ok & when)(copy.wait_recv)
        missing = jnp.logical_not(ok)

        @pl.when(missing if when is None else missing & when)
        def _():
            dst[...] = jnp.zeros(dst.shape, jnp.float32)

    def finish_send(self, index, done=None):
        ok, copy = self.sends(index)
        pl.when(ok if done is None else ok & jnp.logical_not(done))(copy.wait_send)


def roll(value, by, axis):
    by = by % value.shape[axis]
    return value if by == 0 else pltpu.roll(value, by, axis)


def iota(shape, dim):
    return lax.broadcasted_iota(jnp.int32, shape, dim)


def row_sums(vol, ysum, first, count, lanes=(0, 384)):
    at, wide = pl.ds(lanes[0], lanes[1] - lanes[0]), lanes[1] - lanes[0]
    row = iota((2, 8, wide), 1)

    def rows(p, _):
        planes = pl.ds(first + 2 * p, 2)
        low, high = vol[planes, 0:8, at], vol[planes, 8:16, at]
        for b in (1, 2, 3):
            up = roll(jnp.where(row < b, high, low), -b, 1)
            down = roll(jnp.where(row >= 8 - b, high, low), b, 1)
            ysum[b - 1, planes, :, at] = up + down
        return 0

    lax.fori_loop(0, count // 2, rows, 0, unroll=True)


def plane_sums(vol, ysum, x, lanes):
    at = pl.ds(lanes[0], lanes[1] - lanes[0])
    sums = {}

    def get(b, k):
        return vol[pl.ds(x + k, 2), 0:8, at] if b == 0 else ysum[b - 1, pl.ds(x + k, 2), :, at]

    for a in range(4):
        for b in range(4):
            if a * a + b * b < 12.25:
                sums[a, b] = get(b, 3) if a == 0 else get(b, 3 - a) + get(b, 3 + a)
    groups = {}
    for (a, b), value in sums.items():
        key = (min(a, b), max(a, b))
        groups[key] = groups[key] + value if key in groups else value
    shifted = []
    for c in range(4):
        g = None
        for (a, b), value in groups.items():
            w = cone_weight(a, b, c)
            if w > 0:
                g = value * w if g is None else g + value * w
        shifted.append(g)
    return shifted


def cone_pair(vol, ysum, x):
    lane = iota((2, 8, 128), 2)
    for c, g in enumerate(plane_sums(vol, ysum, x, (0, 384))):
        g0, g1, gh = g[:, :, 0:128], g[:, :, 128:256], g[:, :, 256:384]
        if c == 0:
            t0, t1 = g0, g1
        else:
            t0 = t0 + roll(jnp.where(lane < c, g1, g0), -c, 2) + roll(
                jnp.where(lane >= 128 - c, gh, g0), c, 2)
            t1 = t1 + roll(jnp.where(lane < c, gh, g1), -c, 2) + roll(
                jnp.where(lane >= 128 - c, g0, g1), c, 2)
    return t0, t1


def cone_inner(vol, ysum, x):
    lane = iota((2, 8, 128), 2)
    for c, g in enumerate(plane_sums(vol, ysum, x, (0, 256))):
        g0, g1 = g[:, :, 0:128], g[:, :, 128:256]
        if c == 0:
            t0, t1 = g0, g1
        else:
            t0 = t0 + roll(jnp.where(lane < c, g1, g0), -c, 2) + roll(
                jnp.where(lane >= 128 - c, 0.0, g0), c, 2)
            t1 = t1 + roll(jnp.where(lane < c, 0.0, g1), -c, 2) + roll(
                jnp.where(lane >= 128 - c, g0, g1), c, 2)
    return t0, t1


def cone_halo(vol, ysum, x):
    lane = iota((2, 8, 128), 2)
    t0, t1 = 0.0, 0.0
    for c, g in enumerate(plane_sums(vol, ysum, x, (256, 384))):
        if c:
            t0 = t0 + roll(jnp.where(lane >= 128 - c, g, 0.0), c, 2)
            t1 = t1 + roll(jnp.where(lane < c, g, 0.0), -c, 2)
    return t0, t1


def inverse_weight(grid, out):
    gx, gy, gz = [lax.axis_index(a) for a in AXES]
    y = gy * NY + iota((NY, NZ), 0)
    z = gz * NZ + iota((NY, NZ), 1)

    def pairs(pos, by, size):
        def inside(v):
            return ((v >= 0) & (v < size)).astype(jnp.float32)
        return inside(pos + by) + inside(pos - by) if by else inside(pos)

    ys = [None] + [pairs(y, b, grid[1] * NY) for b in (1, 2, 3)]
    zs = [None] + [pairs(z, c, grid[2] * NZ) for c in (1, 2, 3)]
    fs = []
    for a in range(4):
        f = jnp.full((NY, NZ), 0.0, jnp.float32)
        for b in range(4):
            for c in range(4):
                w = cone_weight(a, b, c)
                if w > 0:
                    term = jnp.float32(w)
                    term = term if b == 0 else term * ys[b]
                    term = term if c == 0 else term * zs[c]
                    f = f + term
        fs.append(f)
    for k in range(14):
        px = gx * NX + k - 3
        w = fs[0] * pairs(px, 0, grid[0] * NX)
        for a in (1, 2, 3):
            w = w + fs[a] * pairs(px, a, grid[0] * NX)
        out[k] = 1.0 / w


def pack_rows(vol, first, half, rows):
    row = iota((8, 256), 0)
    for k in range(half):
        a, b = vol[first + k, 0:8, 0:256], vol[first + half + k, 0:8, 0:256]
        b = roll(b, 4, 0)
        rows[0, k] = jnp.where(row < 4, a, b)
        rows[1, k] = jnp.where(row < 4, b, a)


def pack_thin(vol, rows, node_rows, nodes):
    for p in range(8):
        for f in range(6):
            node_rows[p, f:f + 1, :] = nodes[f, 1 + p, 0:1, :]
        node_rows[p, 6:8, :] = jnp.zeros((2, 256), jnp.float32)
        for j, r in enumerate((0, 1, 2, 5, 6, 7)):
            rows[j, p:p + 1, :] = vol[6 + p, r:r + 1, 0:256]


def unpack_thin(vol, rows_in):
    row = iota((8, 256), 0)
    for p in range(8):
        value = None
        for j, r in enumerate((0, 1, 2, 5, 6, 7)):
            here = jnp.broadcast_to(rows_in[j, p:p + 1, :], (8, 256))
            value = here if value is None else jnp.where(row == r, here, value)
        vol[6 + p, 8:16, 0:256] = value


def pack_strips(vol, places, slot, pack, nodes):
    lane = iota((8, 128), 1)
    down, up = pack[0], pack[1]
    for i, p in places:
        first, last = vol[p, 0:8, 0:128], vol[p, 0:8, 128:256]
        d, u = roll(first, slot * i, 1), roll(last, slot * i, 1)
        if i == 0:
            down, up = d, u
        else:
            down = jnp.where((lane >= slot * i) & (lane < slot * i + 3), d, down)
            up = jnp.where((lane >= slot * i - 3) & (lane < slot * i), u, up)
        if nodes is not None:
            for f in range(6):
                n = roll(nodes[f, 1 + i, :, 0:128], slot * i + 3 + f, 1)
                down = jnp.where(lane == slot * i + 3 + f, n, down)
    pack[0] = down
    pack[1] = up


def send_strips(ex, pack, strip):
    for o in NEAR:
        _, dy, dz = o
        if dz:
            k = 0 if dz < 0 else 1
            ex.start(o, pack.at[k], strip.at[k, 1 - dy])


def send_rows(ex, rows, rows_in):
    for k, dy in enumerate((-1, 1)):
        ex.start((0, dy, 0), rows.at[k], rows_in.at[k])


def unpack_rows(vol, first, half, rows_in):
    row = iota((8, 256), 0)
    for k in range(half):
        from_upper, from_lower = rows_in[0, k], rows_in[1, k]
        vol[first + k, 8:16, 0:256] = jnp.where(row < 4, from_upper, from_lower)
        vol[first + half + k, 8:16, 0:256] = roll(jnp.where(row < 4, from_lower, from_upper), 4, 0)


def unpack_strips(vol, places, slot, strip):
    rowl = iota((8, 128), 0)
    lane = iota((8, 128), 1)
    both = [jnp.where((lane & (slot - 1)) < slot - 4, strip[0, dy], strip[1, dy]) for dy in range(3)]
    side = jnp.where(rowl < 4, both[2], both[0])
    for i, p in places:
        vol[p, 0:8, 256:384] = roll(both[1], -slot * i, 1)
        vol[p, 8:16, 256:384] = roll(side, -slot * i, 1)
    return both[1], both[2]


def node_halo(halo, main, side):
    lane = iota((8, 128), 1)
    for p in range(8):
        a = roll(main, -(16 * p + 3), 1)
        b = roll(roll(side, -(16 * p + 3) + 8, 1), -1, 0)
        halo[1 + p, :, 256:384] = jnp.where(lane < 8, a, b)


def node_ahead(nodes, ahead, q):
    lane = iota((8, 128), 1)
    for f in range(6):
        v0, v1 = roll(nodes[f, q, :, 0:128], -1, 1), roll(nodes[f, q, :, 128:256], -1, 1)
        ahead[q, f, :, 0:128] = jnp.where(lane == 127, v1, v0)
        ahead[q, f, :, 128:256] = v1


def node_modes(nodes, ahead, halo, halo_up, modes, q):
    lane = iota((8, 128), 1)
    row = iota((8, 128), 0)
    hs = halo[q, :, 256:384]
    hm = jnp.where(row == 7, roll(hs, -8, 1), roll(hs, -1, 0))
    v0, v1 = roll(halo[q, :, 0:128], -1, 1), roll(halo[q, :, 128:256], -1, 1)
    halo_up[q, :, 0:128] = jnp.where(lane == 127, v1, v0)
    halo_up[q, :, 128:256] = v1

    def spread(ref, f, k):
        return jnp.broadcast_to(ref[q, f:f + 1, 128 * k:128 * k + 128], (8, 128))

    for f in range(6):
        for k in range(2):
            at = pl.ds(128 * k, 128)
            n, s = nodes[f, q, :, at], ahead[q, f, :, at]
            e, r = spread(halo, f, k), spread(halo_up, f, k)
            if k == 1:
                s = jnp.where(lane == 127, roll(hs, 127 - f, 1), s)
                r = jnp.where(lane == 127, roll(hm, 127 - f, 1), r)
            a, d = n + s, s - n
            ay = jnp.where(row == 7, e + r, roll(a, -1, 0))
            dy = jnp.where(row == 7, r - e, roll(d, -1, 0))
            modes[q, f, 0, :, at] = a + ay
            modes[q, f, 1, :, at] = d + dy
            modes[q, f, 2, :, at] = ay - a
            modes[q, f, 3, :, at] = dy - d


def element_energy(modes, x, press, mult):
    shear = 1.0 / (2.0 * (1.0 + poisson))
    bulk = 1.0 / (3.0 * (1.0 - 2.0 * poisson))

    def both_of(f, m):
        return modes[x, f, m], modes[x + 1, f, m]

    def field(base):
        out = []
        for c in range(3):
            aa, ad, da, dd = (both_of(base + c, m) for m in range(4))
            out.append(dict(
                X=aa[1] - aa[0], Y=da[0] + da[1], Z=ad[0] + ad[1],
                XY=da[1] - da[0], XZ=ad[1] - ad[0], YZ=dd[0] + dd[1], XYZ=dd[1] - dd[0]))
        return out

    u, l = field(0), field(3)

    def strains(v):
        a, b, c = v
        one = (a["X"], b["Y"], c["Z"], a["Y"] + b["X"], b["Z"] + c["Y"], a["Z"] + c["X"])
        xi = (None, b["XY"], c["XZ"], a["XY"], b["XZ"] + c["XY"], a["XZ"])
        eta = (a["XY"], None, c["YZ"], b["XY"], b["YZ"], a["YZ"] + c["XY"])
        zeta = (a["XZ"], b["YZ"], None, a["YZ"] + b["XZ"], c["YZ"], c["XZ"])
        return one, xi, eta, zeta

    su, sl = strains(u), strains(l)
    total = None
    for kind in range(4):
        eu, el = su[kind], sl[kind]
        normal, tr_u, tr_l = None, None, None
        for k in range(3):
            if eu[k] is not None:
                t = eu[k] * el[k]
                normal = t if normal is None else normal + t
                tr_u = eu[k] if tr_u is None else tr_u + eu[k]
                tr_l = el[k] if tr_l is None else tr_l + el[k]
        gamma = eu[3] * el[3] + eu[4] * el[4] + eu[5] * el[5]
        scale = shear / 16.0 if kind == 0 else shear / 48.0
        part = (2.0 * (normal - tr_u * tr_l * (1.0 / 3.0)) + gamma) * scale
        if kind == 0:
            div_u, div_l = tr_u * 0.25, tr_l * 0.25
        total = part if total is None else total + part
    pure = u[0]["XYZ"] * l[0]["XYZ"] + u[1]["XYZ"] * l[1]["XYZ"] + u[2]["XYZ"] * l[2]["XYZ"]
    total = total + pure * (shear * (10.0 / 3.0) / 144.0)
    return total + div_l * press + mult * div_u - mult * press * (1.0 / bulk)


def kernel(grid, design, flags, disp, adj, press, mult, out,
           vol, vol2, ysum, ysum2, inner, psum, sums_in, rows, rows_in, strip, pack, rows2, rows_in2, rows3, rows_in3, strip2, pack2,
           nodes, node_rows, ahead, halo, halo_up, modes, aux, fl, inv, energy,
           relay, blank, edge_out, edge_in, load_sem, ready, leave, pause, onward, send1, recv1, send2, recv2, send3, recv3):
    barrier = pltpu.get_barrier_semaphore()
    at = [lax.axis_index(a) for a in AXES]
    first, last_x, half = 0, grid[0] - 1, grid[0] // 2
    beside = (at[0] == half - 1) | (at[0] == half)
    count = jnp.int32(0)

    def greet(target, ok, counts):
        @pl.when(ok)
        def _():
            pl.semaphore_signal(barrier, inc=1, device_id=target, device_id_type=MESH)

        return count + jnp.int32(1) * counts

    for end in (first, last_x):
        count = greet((end, at[1], at[2]), beside, 2 * (at[0] == end))
    for end, to in ((first, half - 1), (last_x, half)):
        count = greet((to, at[1], at[2]), at[0] == end, at[0] == to)
    own = pl.ds(1, 8)
    loads = [
        (design, vol.at[pl.ds(6, 8), pl.ds(0, 8), pl.ds(0, 256)]),
        (disp, nodes.at[pl.ds(0, 3), own]),
        (adj, nodes.at[pl.ds(3, 3), own]),
        (flags, fl), (press, aux.at[own, 0]), (mult, aux.at[own, 1]),
    ]
    loads = [pltpu.make_async_copy(s, d, load_sem.at[k]) for k, (s, d) in enumerate(loads)]
    for c in loads[:3]:
        c.start()
    for o in NEAR:
        target, ok = peer(grid, o)
        count = greet(target, ok, ok)
    for dx in (-1, 1):
        target, ok = peer(grid, (dx, 0, 0))
        ok = ok & (at[0] != (half if dx < 0 else half - 1))
        count = greet(target, ok, ok)
    for c in loads[:3]:
        c.wait()
    for c in loads[3:]:
        c.start()
    own_places = [(i, 6 + i) for i in range(8)]
    pack_strips(vol, own_places, 16, pack, nodes)
    pack_thin(vol, rows, node_rows, nodes)
    pl.semaphore_wait(barrier, count)
    for end, to in ((first, half - 1), (last_x, half)):
        @pl.when(at[0] == end)
        def _():
            pl.semaphore_signal(ready, inc=1, device_id=(to, at[1], at[2]), device_id_type=MESH)

    near = Exchange(grid, send1, recv1)
    send_strips(near, pack, strip)
    near.start((0, -1, 0), rows.at[pl.ds(0, 3)], rows_in.at[pl.ds(0, 3)])
    near.start((0, 1, 0), rows.at[pl.ds(3, 3)], rows_in.at[pl.ds(3, 3)])
    near.start((0, -1, 0), node_rows, halo.at[own, :, pl.ds(0, 256)])
    inverse_weight(grid, inv)
    for c in loads[3:]:
        c.wait()
    for x in range(8):
        aux[1 + x, 2] = jnp.where(fl[x] >= 2, inv[3 + x] * COEF, 0.0)
    lower, upper = (-1, 0, 0), (1, 0, 0)
    far = Exchange(grid, send2, recv2)
    far.start(lower, nodes.at[:, 1], nodes.at[:, 9], at[0] == half)
    far.start(upper, nodes.at[:, 8], nodes.at[:, 0], at[0] == half - 1)
    far.start(upper, aux.at[8], aux.at[0], at[0] == half - 1)
    held, more = relay.at[pl.ds(0, 6)], relay.at[pl.ds(6, 3)]
    ways = [
        (half - 1, first, half, nodes.at[:, 8], held, nodes.at[:, 0], 1),
        (half - 1, first, half, aux.at[8], more, aux.at[0], 2),
        (half, last_x, half - 1, nodes.at[:, 1], held, nodes.at[:, 9], 0),
    ]

    def way(j, leg):
        start, end, to, src, mid, dst, index = ways[j]
        if leg == 0:
            return at[0] == start, at[0] == end, pltpu.make_async_remote_copy(
                src_ref=src, dst_ref=mid, send_sem=leave.at[j], recv_sem=pause.at[j],
                device_id=(end, at[1], at[2]), device_id_type=MESH)
        return at[0] == end, at[0] == to, pltpu.make_async_remote_copy(
            src_ref=mid, dst_ref=dst, send_sem=onward.at[j], recv_sem=recv2.at[index],
            device_id=(to, at[1], at[2]), device_id_type=MESH)

    for j in range(3):
        here, _, copy = way(j, 0)
        pl.when(here)(copy.start)
    for j in range(3):
        _, there, copy = way(j, 0)
        pl.when(there)(copy.wait_recv)
        here, _, copy = way(j, 1)
        pl.when(here)(copy.start)
    sums_in[6:8] = jnp.zeros((2, 8, 256), jnp.float32)
    for k in (0, 14):
        vol[k:k + 6, 0:8, :] = jnp.zeros((6, 8, 384), jnp.float32)
        for b in range(3):
            ysum[b, k:k + 6] = jnp.zeros((6, 8, 384), jnp.float32)

    def own_ahead(q, _):
        node_ahead(nodes, ahead, q)
        return 0

    lax.fori_loop(1, 9, own_ahead, 0, unroll=True)

    down_first = at[0] == half
    def scaled(x):
        return element_energy(modes, x + 1, aux[x + 1, 0], aux[x + 1, 1]) * aux[x + 1, 2]

    def own_modes(i, _):
        node_modes(nodes, ahead, halo, halo_up, modes, jnp.where(down_first, 1 + i, 8 - i))
        return 0

    def first_modes(i, _):
        node_modes(nodes, ahead, blank, halo_up, modes, jnp.where(down_first, 1 + i, 8 - i))
        return 0

    def energies(i, _):
        x = jnp.where(down_first, i, 6 - i)
        energy[x + 3] = scaled(x)
        return 0


    @pl.when(beside)
    def _():
        blank[...] = jnp.zeros(blank.shape, jnp.float32)
        lax.fori_loop(0, 4, first_modes, 0, unroll=True)
        lax.fori_loop(0, 3, energies, 0, unroll=True)
        pl.semaphore_wait(ready, 1)

    for k in (3, 4):
        far.add(*((lower, halo.at[1], halo.at[9]) if k == 3 else (upper, halo.at[8], halo.at[0])))
    far.add(lower, psum.at[pl.ds(0, 6)], sums_in.at[pl.ds(8, 6)])
    far.add(upper, psum.at[pl.ds(8, 6)], sums_in.at[pl.ds(0, 6)])
    far.add(lower, energy.at[pl.ds(3, 3)], energy.at[pl.ds(11, 3)])
    far.add(upper, energy.at[pl.ds(8, 2)], energy.at[pl.ds(0, 2)])
    far.add(lower, edge_out, edge_in, at[0] != half)
    far.add(upper, edge_out, edge_in, at[0] != half - 1)
    far.begin(7, at[0] == half)
    far.begin(8, at[0] == half - 1)

    for k in range(8):
        near.finish_recv(k)
    unpack_thin(vol, rows_in)
    main, side = unpack_strips(vol, own_places, 16, strip)
    node_halo(halo, main, side)

    row_sums(vol, ysum, 6, 8)

    def own_sums(i, _):
        x = jnp.where(down_first, 2 * i, 12 - 2 * i)
        t0, t1 = cone_pair(vol, ysum, x)
        psum[pl.ds(x, 2), :, 0:128] = t0
        psum[pl.ds(x, 2), :, 128:256] = t1
        return 0


    def begin(low, high, one):
        far.begin(low, down_first if one else jnp.logical_not(down_first))
        far.begin(high, jnp.logical_not(down_first) if one else down_first)

    lax.fori_loop(0, 3, own_sums, 0, unroll=True)
    begin(5, 6, True)
    near.finish_recv(8)
    for k in (3, 4):
        far.begin(k)
    for k in range(9):
        near.finish_send(k)

    lax.fori_loop(0, 4, own_modes, 0, unroll=True)
    for ex, low in ((7, True), (8, False)):
        pl.when(beside & (down_first if low else jnp.logical_not(down_first)))(far.sends(ex)[1].wait_send)
    lax.fori_loop(0, 3, energies, 0, unroll=True)

    @pl.when(beside)
    def _():
        lane = iota((8, 128), 1)
        first_plane = jnp.where(down_first, 3, 8)
        strip_of = None
        for j in range(3):
            edge_out[j:j + 1, 0:256] = energy[first_plane + j, 7:8, :]
            moved = roll(energy[first_plane + j, :, 128:256], j - 127, 1)
            strip_of = moved if j == 0 else jnp.where(lane == j, moved, strip_of)
        edge_out[:, 256:384] = strip_of

    far.begin(9)
    far.begin(10)
    far.begin(7, jnp.logical_not(beside) & down_first)
    far.begin(8, jnp.logical_not(beside) & jnp.logical_not(down_first))
    lax.fori_loop(3, 7, own_sums, 0, unroll=True)
    begin(5, 6, False)
    lax.fori_loop(4, 8, own_modes, 0, unroll=True)
    lax.fori_loop(3, 7, energies, 0, unroll=True)
    begin(7, 8, False)
    denom = math.tanh(sharpness * threshold) + math.tanh(sharpness * (1.0 - threshold))
    base = math.tanh(sharpness * threshold)
    up_first = jnp.logical_not(down_first)
    last = Exchange(grid, send3, recv3)

    def side_planes(low):
        high = jnp.logical_not(low)
        for k in (1, 2, 4):
            far.finish_recv(k, low)
        for k in (0, 3):
            far.finish_recv(k, high)
        q, x = jnp.where(low, 0, 9), jnp.where(low, -1, 7)
        node_ahead(nodes, ahead, q)
        node_modes(nodes, ahead, halo, halo_up, modes, q)
        energy[x + 3] = scaled(x)
        for k in (6, 8):
            far.finish_recv(k, low)
        for k in (5, 7):
            far.finish_recv(k, high)

    def put_edge():
        far.finish_recv(9, at[0] == half - 1)
        far.finish_recv(10, at[0] == half)
        row, lane = iota((8, 256), 0), iota((8, 256), 1)
        for j in range(3):
            @pl.when(beside & up_first if j == 2 else beside)
            def _():
                k = jnp.where(down_first, 0, 11) + j
                edge = roll(edge_in[:, 256:384], 127 - j, 1)
                value = jnp.where(lane == 255, jnp.concatenate([edge, edge], axis=1), energy[k])
                energy[k] = jnp.where(row == 7, jnp.broadcast_to(edge_in[j:j + 1, 0:256], (8, 256)), value)

    def chain(first, planes):
        for j in range(planes):
            k = first + j
            total = psum[k] + sums_in[k]
            hyper = jnp.tanh(sharpness * (total * inv[k] - threshold))
            smooth = (base + hyper) * (1.0 / denom)
            slope = (1.0 - hyper * hyper) * (sharpness / denom)
            vol2[k, 0:8, 0:256] = smooth * smooth * slope * energy[k]

    early, late = jnp.where(down_first, 6, 0), jnp.where(down_first, 0, 8)
    places = [(i, early + i) for i in range(8)] + [(8 + i, late + i) for i in range(6)]
    side_planes(up_first)
    chain(early, 8)
    pack_rows(vol2, early, 4, rows2)
    send_rows(last, rows2, rows_in2)
    pack_strips(vol2, places[:8], 8, pack2, None)
    side_planes(down_first)
    put_edge()
    chain(late, 6)
    pack_strips(vol2, places[8:], 8, pack2, None)
    send_strips(last, pack2, strip2)
    pack_rows(vol2, late, 3, rows3)
    send_rows(last, rows3, rows_in3)
    for ex in (far, last):
        for k in range(len(ex.items)):
            done = beside & (down_first if k == 7 else up_first) if ex is far and k in (7, 8) else None
            ex.finish_send(k, done)
    for j in range(3):
        for leg in range(2):
            here, _, copy = way(j, leg)
            pl.when(here)(copy.wait_send)
    for k in (0, 1):
        last.finish_recv(k)
    unpack_rows(vol2, early, 4, rows_in2)
    for k in (8, 9):
        last.finish_recv(k)
    unpack_rows(vol2, late, 3, rows_in3)
    row_sums(vol2, ysum2, 0, 14, (0, 256))
    for i in range(4):
        planes = pl.ds(2 * i, 2)
        t0, t1 = cone_inner(vol2, ysum2, 2 * i)
        inner[planes, :, 0:128] = t0
        inner[planes, :, 128:256] = t1
    for k in range(2, 8):
        last.finish_recv(k)
    unpack_strips(vol2, places, 8, strip2)
    row_sums(vol2, ysum2, 0, 14, (256, 384))
    for i in range(4):
        planes = pl.ds(2 * i, 2)
        for half_at, t in zip((0, 128), cone_halo(vol2, ysum2, 2 * i)):
            lanes = pl.ds(half_at, 128)
            out[planes, :, lanes] = jnp.where(fl[planes, :, lanes] >= 2, inner[planes, :, lanes] + t, 0.0)


def on_device(grid, *args):
    f32, i32 = jnp.float32, jnp.int32
    V = pltpu.VMEM
    dma = pltpu.SemaphoreType.DMA
    strip, pack = V((2, 3, 8, 128), f32), V((2, 8, 128), f32)
    return pl.pallas_call(
        functools.partial(kernel, grid),
        out_shape=pltpu.VMEM((8, 8, 256), f32),
        in_specs=[pl.BlockSpec(memory_space=pl.ANY)] * 6,
        out_specs=pl.BlockSpec(memory_space=pltpu.VMEM),
        scratch_shapes=[
            V((20, 16, 384), f32), V((14, 16, 384), f32), V((3, 20, 8, 384), f32), V((3, 14, 8, 384), f32), V((8, 8, 256), f32),
            V((14, 8, 256), f32), V((14, 8, 256), f32),
            V((6, 8, 256), f32), V((6, 8, 256), f32), strip, pack,
            V((2, 4, 8, 256), f32), V((2, 4, 8, 256), f32), V((2, 3, 8, 256), f32), V((2, 3, 8, 256), f32), strip, pack,
            V((6, 10, 8, 256), f32), V((8, 8, 256), f32), V((10, 6, 8, 256), f32), V((10, 8, 384), f32), V((10, 8, 256), f32),
            V((10, 6, 4, 8, 256), f32),
            V((9, 3, 8, 256), f32), V((8, 8, 256), i32), V((14, 8, 256), f32), V((14, 8, 256), f32),
            V((9, 8, 256), f32), V((10, 8, 384), f32), V((8, 384), f32), V((8, 384), f32),
            dma((6,)), pltpu.SemaphoreType.REGULAR, dma((3,)), dma((3,)), dma((3,)), dma((9,)), dma((9,)), dma((11,)), dma((11,)), dma((10,)), dma((10,)),
        ],
        compiler_params=pltpu.CompilerParams(
            collective_id=0, has_side_effects=True, vmem_limit_bytes=63 << 20),
        name="sensitivity",
    )(*args)


def solution(mesh):
    grid = tuple(mesh.shape[a] for a in AXES)
    brick = P("gx", "gy", "gz")
    field = P(None, "gx", "gy", "gz")
    return jax.shard_map(
        functools.partial(on_device, grid), mesh=mesh,
        in_specs=(brick, brick, field, field, brick, brick), out_specs=brick, check_vma=False,
    )
```

```python
import functools
import itertools
import math

import jax
import jax.numpy as jnp
from jax import lax
from jax.experimental import pallas as pl
from jax.experimental.pallas import tpu as pltpu
from jax.sharding import PartitionSpec as P

poisson = 0.45
sharpness = 4.0
threshold = 0.5
stiff_floor = 0.001
cone_radius = 3.5

AXES = ("gx", "gy", "gz")
NX, NY, NZ = 8, 8, 256
MESH = pl.DeviceIdType.MESH
NEAR = [(0, 1, 1), (0, -1, 1), (0, 1, -1), (0, -1, -1), (0, -1, 0), (0, 1, 0), (0, 0, 1), (0, 0, -1)]
COEF = -3.0 * (1.0 - stiff_floor)


def cone_weight(a, b, c):
    r2 = a * a + b * b + c * c
    return cone_radius - math.sqrt(r2) if r2 < cone_radius * cone_radius else 0.0


def place(grid):
    return [lax.axis_index(a) for a in AXES]


def peer(grid, offset):
    at = [lax.axis_index(a) for a in AXES]
    target = tuple(a + o for a, o in zip(at, offset))
    ok = None
    for t, o, n in zip(target, offset, grid):
        if o:
            inside = t >= 0 if o < 0 else t < n
            ok = inside if ok is None else ok & inside
    return target, ok


def opposite(offset):
    return tuple(-o for o in offset)


class Exchange:
    def __init__(self, grid, send, recv):
        self.grid, self.send, self.recv = grid, send, recv
        self.items, self.unless = [], []

    def copy(self, index):
        offset, src, dst = self.items[index]
        target, ok = peer(self.grid, offset)
        return ok, pltpu.make_async_remote_copy(
            src_ref=src, dst_ref=dst, send_sem=self.send.at[index], recv_sem=self.recv.at[index],
            device_id=target, device_id_type=MESH,
        )

    def add(self, offset, src, dst, unless=None):
        self.items.append((offset, src, dst))
        self.unless.append(unless)
        return len(self.items) - 1

    def sends(self, index):
        ok, copy = self.copy(index)
        unless = self.unless[index]
        return (ok if unless is None else ok & jnp.logical_not(unless)), copy

    def begin(self, index, when=None):
        ok, copy = self.sends(index)
        pl.when(ok if when is None else ok & when)(copy.start)

    def start(self, offset, src, dst, unless=None):
        self.begin(self.add(offset, src, dst, unless))

    def finish_recv(self, index, when=None):
        offset, src, dst = self.items[index]
        _, ok = peer(self.grid, opposite(offset))
        _, copy = self.copy(index)
        pl.when(ok if when is None else ok & when)(copy.wait_recv)
        missing = jnp.logical_not(ok)

        @pl.when(missing if when is None else missing & when)
        def _():
            dst[...] = jnp.zeros(dst.shape, jnp.float32)

    def finish_send(self, index, done=None):
        ok, copy = self.sends(index)
        pl.when(ok if done is None else ok & jnp.logical_not(done))(copy.wait_send)


def roll(value, by, axis):
    by = by % value.shape[axis]
    return value if by == 0 else pltpu.roll(value, by, axis)


def iota(shape, dim):
    return lax.broadcasted_iota(jnp.int32, shape, dim)


def row_sums(vol, ysum, first, count, lanes=(0, 384)):
    at, wide = pl.ds(lanes[0], lanes[1] - lanes[0]), lanes[1] - lanes[0]
    row = iota((2, 8, wide), 1)

    def rows(p, _):
        planes = pl.ds(first + 2 * p, 2)
        low, high = vol[planes, 0:8, at], vol[planes, 8:16, at]
        for b in (1, 2, 3):
            up = roll(jnp.where(row < b, high, low), -b, 1)
            down = roll(jnp.where(row >= 8 - b, high, low), b, 1)
            ysum[b - 1, planes, :, at] = up + down
        return 0

    lax.fori_loop(0, count // 2, rows, 0, unroll=True)


def plane_sums(vol, ysum, x, lanes):
    at = pl.ds(lanes[0], lanes[1] - lanes[0])
    sums = {}

    def get(b, k):
        return vol[pl.ds(x + k, 2), 0:8, at] if b == 0 else ysum[b - 1, pl.ds(x + k, 2), :, at]

    for a in range(4):
        for b in range(4):
            if a * a + b * b < 12.25:
                sums[a, b] = get(b, 3) if a == 0 else get(b, 3 - a) + get(b, 3 + a)
    groups = {}
    for (a, b), value in sums.items():
        key = (min(a, b), max(a, b))
        groups[key] = groups[key] + value if key in groups else value
    shifted = []
    for c in range(4):
        g = None
        for (a, b), value in groups.items():
            w = cone_weight(a, b, c)
            if w > 0:
                g = value * w if g is None else g + value * w
        shifted.append(g)
    return shifted


def cone_pair(vol, ysum, x):
    lane = iota((2, 8, 128), 2)
    for c, g in enumerate(plane_sums(vol, ysum, x, (0, 384))):
        g0, g1, gh = g[:, :, 0:128], g[:, :, 128:256], g[:, :, 256:384]
        if c == 0:
            t0, t1 = g0, g1
        else:
            t0 = t0 + roll(jnp.where(lane < c, g1, g0), -c, 2) + roll(
                jnp.where(lane >= 128 - c, gh, g0), c, 2)
            t1 = t1 + roll(jnp.where(lane < c, gh, g1), -c, 2) + roll(
                jnp.where(lane >= 128 - c, g0, g1), c, 2)
    return t0, t1


def cone_inner(vol, ysum, x):
    lane = iota((2, 8, 128), 2)
    for c, g in enumerate(plane_sums(vol, ysum, x, (0, 256))):
        g0, g1 = g[:, :, 0:128], g[:, :, 128:256]
        if c == 0:
            t0, t1 = g0, g1
        else:
            t0 = t0 + roll(jnp.where(lane < c, g1, g0), -c, 2) + roll(
                jnp.where(lane >= 128 - c, 0.0, g0), c, 2)
            t1 = t1 + roll(jnp.where(lane < c, 0.0, g1), -c, 2) + roll(
                jnp.where(lane >= 128 - c, g0, g1), c, 2)
    return t0, t1


def cone_halo(vol, ysum, x):
    lane = iota((2, 8, 128), 2)
    t0, t1 = 0.0, 0.0
    for c, g in enumerate(plane_sums(vol, ysum, x, (256, 384))):
        if c:
            t0 = t0 + roll(jnp.where(lane >= 128 - c, g, 0.0), c, 2)
            t1 = t1 + roll(jnp.where(lane < c, g, 0.0), -c, 2)
    return t0, t1


def inverse_weight(grid, out):
    gx, gy, gz = [lax.axis_index(a) for a in AXES]
    y = gy * NY + iota((NY, NZ), 0)
    z = gz * NZ + iota((NY, NZ), 1)

    def pairs(pos, by, size):
        def inside(v):
            return ((v >= 0) & (v < size)).astype(jnp.float32)
        return inside(pos + by) + inside(pos - by) if by else inside(pos)

    ys = [None] + [pairs(y, b, grid[1] * NY) for b in (1, 2, 3)]
    zs = [None] + [pairs(z, c, grid[2] * NZ) for c in (1, 2, 3)]
    fs = []
    for a in range(4):
        f = jnp.full((NY, NZ), 0.0, jnp.float32)
        for b in range(4):
            for c in range(4):
                w = cone_weight(a, b, c)
                if w > 0:
                    term = jnp.float32(w)
                    term = term if b == 0 else term * ys[b]
                    term = term if c == 0 else term * zs[c]
                    f = f + term
        fs.append(f)
    for k in range(14):
        px = gx * NX + k - 3
        w = fs[0] * pairs(px, 0, grid[0] * NX)
        for a in (1, 2, 3):
            w = w + fs[a] * pairs(px, a, grid[0] * NX)
        out[k] = 1.0 / w


def pack_rows(vol, first, half, rows):
    row = iota((8, 256), 0)
    for k in range(half):
        a, b = vol[first + k, 0:8, 0:256], vol[first + half + k, 0:8, 0:256]
        b = roll(b, 4, 0)
        rows[0, k] = jnp.where(row < 4, a, b)
        rows[1, k] = jnp.where(row < 4, b, a)


def pack_thin(vol, rows, node_rows, nodes):
    for p in range(8):
        for f in range(6):
            node_rows[p, f:f + 1, :] = nodes[f, 1 + p, 0:1, :]
        node_rows[p, 6:8, :] = jnp.zeros((2, 256), jnp.float32)
        for j, r in enumerate((0, 1, 2, 5, 6, 7)):
            rows[j, p:p + 1, :] = vol[6 + p, r:r + 1, 0:256]


def unpack_thin(vol, rows_in):
    row = iota((8, 256), 0)
    for p in range(8):
        value = None
        for j, r in enumerate((0, 1, 2, 5, 6, 7)):
            here = jnp.broadcast_to(rows_in[j, p:p + 1, :], (8, 256))
            value = here if value is None else jnp.where(row == r, here, value)
        vol[6 + p, 8:16, 0:256] = value


def pack_strips(vol, places, slot, pack, nodes):
    lane = iota((8, 128), 1)
    down, up = pack[0], pack[1]
    for i, p in places:
        first, last = vol[p, 0:8, 0:128], vol[p, 0:8, 128:256]
        d, u = roll(first, slot * i, 1), roll(last, slot * i, 1)
        if i == 0:
            down, up = d, u
        else:
            down = jnp.where((lane >= slot * i) & (lane < slot * i + 3), d, down)
            up = jnp.where((lane >= slot * i - 3) & (lane < slot * i), u, up)
        if nodes is not None:
            for f in range(6):
                n = roll(nodes[f, 1 + i, :, 0:128], slot * i + 3 + f, 1)
                down = jnp.where(lane == slot * i + 3 + f, n, down)
    pack[0] = down
    pack[1] = up


def send_strips(ex, pack, strip):
    for o in NEAR:
        _, dy, dz = o
        if dz:
            k = 0 if dz < 0 else 1
            ex.start(o, pack.at[k], strip.at[k, 1 - dy])


def send_rows(ex, rows, rows_in):
    for k, dy in enumerate((-1, 1)):
        ex.start((0, dy, 0), rows.at[k], rows_in.at[k])


def unpack_rows(vol, first, half, rows_in):
    row = iota((8, 256), 0)
    for k in range(half):
        from_upper, from_lower = rows_in[0, k], rows_in[1, k]
        vol[first + k, 8:16, 0:256] = jnp.where(row < 4, from_upper, from_lower)
        vol[first + half + k, 8:16, 0:256] = roll(jnp.where(row < 4, from_lower, from_upper), 4, 0)


def unpack_strips(vol, places, slot, strip):
    rowl = iota((8, 128), 0)
    lane = iota((8, 128), 1)
    both = [jnp.where((lane & (slot - 1)) < slot - 4, strip[0, dy], strip[1, dy]) for dy in range(3)]
    side = jnp.where(rowl < 4, both[2], both[0])
    for i, p in places:
        vol[p, 0:8, 256:384] = roll(both[1], -slot * i, 1)
        vol[p, 8:16, 256:384] = roll(side, -slot * i, 1)
    return both[1], both[2]


def node_halo(halo, main, side):
    lane = iota((8, 128), 1)
    for p in range(8):
        a = roll(main, -(16 * p + 3), 1)
        b = roll(roll(side, -(16 * p + 3) + 8, 1), -1, 0)
        halo[1 + p, :, 256:384] = jnp.where(lane < 8, a, b)


def node_ahead(nodes, ahead, q):
    lane = iota((8, 128), 1)
    for f in range(6):
        v0, v1 = roll(nodes[f, q, :, 0:128], -1, 1), roll(nodes[f, q, :, 128:256], -1, 1)
        ahead[q, f, :, 0:128] = jnp.where(lane == 127, v1, v0)
        ahead[q, f, :, 128:256] = v1


def node_modes(nodes, ahead, halo, halo_up, modes, q):
    lane = iota((8, 128), 1)
    row = iota((8, 128), 0)
    hs = halo[q, :, 256:384]
    hm = jnp.where(row == 7, roll(hs, -8, 1), roll(hs, -1, 0))
    v0, v1 = roll(halo[q, :, 0:128], -1, 1), roll(halo[q, :, 128:256], -1, 1)
    halo_up[q, :, 0:128] = jnp.where(lane == 127, v1, v0)
    halo_up[q, :, 128:256] = v1

    def spread(ref, f, k):
        return jnp.broadcast_to(ref[q, f:f + 1, 128 * k:128 * k + 128], (8, 128))

    for f in range(6):
        for k in range(2):
            at = pl.ds(128 * k, 128)
            n, s = nodes[f, q, :, at], ahead[q, f, :, at]
            e, r = spread(halo, f, k), spread(halo_up, f, k)
            if k == 1:
                s = jnp.where(lane == 127, roll(hs, 127 - f, 1), s)
                r = jnp.where(lane == 127, roll(hm, 127 - f, 1), r)
            a, d = n + s, s - n
            ay = jnp.where(row == 7, e + r, roll(a, -1, 0))
            dy = jnp.where(row == 7, r - e, roll(d, -1, 0))
            modes[q, f, 0, :, at] = a + ay
            modes[q, f, 1, :, at] = d + dy
            modes[q, f, 2, :, at] = ay - a
            modes[q, f, 3, :, at] = dy - d


def element_energy(modes, x, press, mult):
    shear = 1.0 / (2.0 * (1.0 + poisson))
    bulk = 1.0 / (3.0 * (1.0 - 2.0 * poisson))

    def both_of(f, m):
        return modes[x, f, m], modes[x + 1, f, m]

    def field(base):
        out = []
        for c in range(3):
            aa, ad, da, dd = (both_of(base + c, m) for m in range(4))
            out.append(dict(
                X=aa[1] - aa[0], Y=da[0] + da[1], Z=ad[0] + ad[1],
                XY=da[1] - da[0], XZ=ad[1] - ad[0], YZ=dd[0] + dd[1], XYZ=dd[1] - dd[0]))
        return out

    u, l = field(0), field(3)

    def strains(v):
        a, b, c = v
        one = (a["X"], b["Y"], c["Z"], a["Y"] + b["X"], b["Z"] + c["Y"], a["Z"] + c["X"])
        xi = (None, b["XY"], c["XZ"], a["XY"], b["XZ"] + c["XY"], a["XZ"])
        eta = (a["XY"], None, c["YZ"], b["XY"], b["YZ"], a["YZ"] + c["XY"])
        zeta = (a["XZ"], b["YZ"], None, a["YZ"] + b["XZ"], c["YZ"], c["XZ"])
        return one, xi, eta, zeta

    su, sl = strains(u), strains(l)
    total = None
    for kind in range(4):
        eu, el = su[kind], sl[kind]
        normal, tr_u, tr_l = None, None, None
        for k in range(3):
            if eu[k] is not None:
                t = eu[k] * el[k]
                normal = t if normal is None else normal + t
                tr_u = eu[k] if tr_u is None else tr_u + eu[k]
                tr_l = el[k] if tr_l is None else tr_l + el[k]
        gamma = eu[3] * el[3] + eu[4] * el[4] + eu[5] * el[5]
        scale = shear / 16.0 if kind == 0 else shear / 48.0
        part = (2.0 * (normal - tr_u * tr_l * (1.0 / 3.0)) + gamma) * scale
        if kind == 0:
            div_u, div_l = tr_u * 0.25, tr_l * 0.25
        total = part if total is None else total + part
    pure = u[0]["XYZ"] * l[0]["XYZ"] + u[1]["XYZ"] * l[1]["XYZ"] + u[2]["XYZ"] * l[2]["XYZ"]
    total = total + pure * (shear * (10.0 / 3.0) / 144.0)
    return total + div_l * press + mult * div_u - mult * press * (1.0 / bulk)


def kernel(grid, design, flags, disp, adj, press, mult, out,
           vol, vol2, ysum, ysum2, inner, psum, sums_in, rows, rows_in, strip, pack, rows2, rows_in2, rows3, rows_in3, strip2, pack2,
           nodes, node_rows, ahead, halo, halo_up, modes, aux, fl, inv, energy,
           relay, blank, edge_out, edge_in, load_sem, ready, leave, pause, onward, send1, recv1, send2, recv2, send3, recv3):
    barrier = pltpu.get_barrier_semaphore()
    at = [lax.axis_index(a) for a in AXES]
    first, last_x, half = 0, grid[0] - 1, grid[0] // 2
    beside = (at[0] == half - 1) | (at[0] == half)
    count = jnp.int32(0)

    def greet(target, ok, counts):
        @pl.when(ok)
        def _():
            pl.semaphore_signal(barrier, inc=1, device_id=target, device_id_type=MESH)

        return count + jnp.int32(1) * counts

    for end in (first, last_x):
        count = greet((end, at[1], at[2]), beside, 2 * (at[0] == end))
    for end, to in ((first, half - 1), (last_x, half)):
        count = greet((to, at[1], at[2]), at[0] == end, at[0] == to)
    own = pl.ds(1, 8)
    loads = [
        (design, vol.at[pl.ds(6, 8), pl.ds(0, 8), pl.ds(0, 256)]),
        (disp, nodes.at[pl.ds(0, 3), own]),
        (adj, nodes.at[pl.ds(3, 3), own]),
        (flags, fl), (press, aux.at[own, 0]), (mult, aux.at[own, 1]),
    ]
    loads = [pltpu.make_async_copy(s, d, load_sem.at[k]) for k, (s, d) in enumerate(loads)]
    for c in loads[:3]:
        c.start()
    for o in NEAR:
        target, ok = peer(grid, o)
        count = greet(target, ok, ok)
    for dx in (-1, 1):
        target, ok = peer(grid, (dx, 0, 0))
        ok = ok & (at[0] != (half if dx < 0 else half - 1))
        count = greet(target, ok, ok)
    for c in loads[:3]:
        c.wait()
    for c in loads[3:]:
        c.start()
    own_places = [(i, 6 + i) for i in range(8)]
    pack_strips(vol, own_places, 16, pack, nodes)
    pack_thin(vol, rows, node_rows, nodes)
    pl.semaphore_wait(barrier, count)
    for end, to in ((first, half - 1), (last_x, half)):
        @pl.when(at[0] == end)
        def _():
            pl.semaphore_signal(ready, inc=1, device_id=(to, at[1], at[2]), device_id_type=MESH)

    near = Exchange(grid, send1, recv1)
    send_strips(near, pack, strip)
    near.start((0, -1, 0), rows.at[pl.ds(0, 3)], rows_in.at[pl.ds(0, 3)])
    near.start((0, 1, 0), rows.at[pl.ds(3, 3)], rows_in.at[pl.ds(3, 3)])
    near.start((0, -1, 0), node_rows, halo.at[own, :, pl.ds(0, 256)])
    inverse_weight(grid, inv)
    for c in loads[3:]:
        c.wait()
    for x in range(8):
        aux[1 + x, 2] = jnp.where(fl[x] >= 2, inv[3 + x] * COEF, 0.0)
    lower, upper = (-1, 0, 0), (1, 0, 0)
    far = Exchange(grid, send2, recv2)
    far.start(lower, nodes.at[:, 1], nodes.at[:, 9], at[0] == half)
    far.start(upper, nodes.at[:, 8], nodes.at[:, 0], at[0] == half - 1)
    far.start(upper, aux.at[8], aux.at[0], at[0] == half - 1)
    held, more = relay.at[pl.ds(0, 6)], relay.at[pl.ds(6, 3)]
    ways = [
        (half - 1, first, half, nodes.at[:, 8], held, nodes.at[:, 0], 1),
        (half - 1, first, half, aux.at[8], more, aux.at[0], 2),
        (half, last_x, half - 1, nodes.at[:, 1], held, nodes.at[:, 9], 0),
    ]

    def way(j, leg):
        start, end, to, src, mid, dst, index = ways[j]
        if leg == 0:
            return at[0] == start, at[0] == end, pltpu.make_async_remote_copy(
                src_ref=src, dst_ref=mid, send_sem=leave.at[j], recv_sem=pause.at[j],
                device_id=(end, at[1], at[2]), device_id_type=MESH)
        return at[0] == end, at[0] == to, pltpu.make_async_remote_copy(
            src_ref=mid, dst_ref=dst, send_sem=onward.at[j], recv_sem=recv2.at[index],
            device_id=(to, at[1], at[2]), device_id_type=MESH)

    for j in range(3):
        here, _, copy = way(j, 0)
        pl.when(here)(copy.start)
    for j in range(3):
        _, there, copy = way(j, 0)
        pl.when(there)(copy.wait_recv)
        here, _, copy = way(j, 1)
        pl.when(here)(copy.start)
    sums_in[6:8] = jnp.zeros((2, 8, 256), jnp.float32)
    for k in (0, 14):
        vol[k:k + 6, 0:8, :] = jnp.zeros((6, 8, 384), jnp.float32)
        for b in range(3):
            ysum[b, k:k + 6] = jnp.zeros((6, 8, 384), jnp.float32)

    def own_ahead(q, _):
        node_ahead(nodes, ahead, q)
        return 0

    lax.fori_loop(1, 9, own_ahead, 0, unroll=True)

    down_first = at[0] == half
    def scaled(x):
        return element_energy(modes, x + 1, aux[x + 1, 0], aux[x + 1, 1]) * aux[x + 1, 2]

    def own_modes(i, _):
        node_modes(nodes, ahead, halo, halo_up, modes, jnp.where(down_first, 1 + i, 8 - i))
        return 0

    def first_modes(i, _):
        node_modes(nodes, ahead, blank, halo_up, modes, jnp.where(down_first, 1 + i, 8 - i))
        return 0

    def energies(i, _):
        x = jnp.where(down_first, i, 6 - i)
        energy[x + 3] = scaled(x)
        return 0


    @pl.when(beside)
    def _():
        blank[...] = jnp.zeros(blank.shape, jnp.float32)
        lax.fori_loop(0, 4, first_modes, 0, unroll=True)
        lax.fori_loop(0, 3, energies, 0, unroll=True)
        pl.semaphore_wait(ready, 1)

    for k in (3, 4):
        far.add(*((lower, halo.at[1], halo.at[9]) if k == 3 else (upper, halo.at[8], halo.at[0])))
    far.add(lower, psum.at[pl.ds(0, 6)], sums_in.at[pl.ds(8, 6)])
    far.add(upper, psum.at[pl.ds(8, 6)], sums_in.at[pl.ds(0, 6)])
    far.add(lower, energy.at[pl.ds(3, 3)], energy.at[pl.ds(11, 3)])
    far.add(upper, energy.at[pl.ds(8, 2)], energy.at[pl.ds(0, 2)])
    far.add(lower, edge_out, edge_in, at[0] != half)
    far.add(upper, edge_out, edge_in, at[0] != half - 1)
    far.begin(7, at[0] == half)
    far.begin(8, at[0] == half - 1)

    for k in range(8):
        near.finish_recv(k)
    unpack_thin(vol, rows_in)
    main, side = unpack_strips(vol, own_places, 16, strip)
    node_halo(halo, main, side)

    row_sums(vol, ysum, 6, 8)

    def own_sums(i, _):
        x = jnp.where(down_first, 2 * i, 12 - 2 * i)
        t0, t1 = cone_pair(vol, ysum, x)
        psum[pl.ds(x, 2), :, 0:128] = t0
        psum[pl.ds(x, 2), :, 128:256] = t1
        return 0


    def begin(low, high, one):
        far.begin(low, down_first if one else jnp.logical_not(down_first))
        far.begin(high, jnp.logical_not(down_first) if one else down_first)

    lax.fori_loop(0, 3, own_sums, 0, unroll=True)
    begin(5, 6, True)
    near.finish_recv(8)
    begin(3, 4, True)

    lax.fori_loop(0, 4, own_modes, 0, unroll=True)
    for ex, low in ((7, True), (8, False)):
        pl.when(beside & (down_first if low else jnp.logical_not(down_first)))(far.sends(ex)[1].wait_send)
    lax.fori_loop(0, 3, energies, 0, unroll=True)

    @pl.when(beside)
    def _():
        lane = iota((8, 128), 1)
        first_plane = jnp.where(down_first, 3, 8)
        strip_of = None
        for j in range(3):
            edge_out[j:j + 1, 0:256] = energy[first_plane + j, 7:8, :]
            moved = roll(energy[first_plane + j, :, 128:256], j - 127, 1)
            strip_of = moved if j == 0 else jnp.where(lane == j, moved, strip_of)
        edge_out[:, 256:384] = strip_of

    far.begin(9)
    far.begin(10)
    begin(3, 4, False)
    far.begin(7, jnp.logical_not(beside) & down_first)
    far.begin(8, jnp.logical_not(beside) & jnp.logical_not(down_first))
    lax.fori_loop(3, 7, own_sums, 0, unroll=True)
    begin(5, 6, False)
    lax.fori_loop(4, 8, own_modes, 0, unroll=True)
    lax.fori_loop(3, 7, energies, 0, unroll=True)
    begin(7, 8, False)
    denom = math.tanh(sharpness * threshold) + math.tanh(sharpness * (1.0 - threshold))
    base = math.tanh(sharpness * threshold)
    up_first = jnp.logical_not(down_first)
    last = Exchange(grid, send3, recv3)

    def side_planes(low):
        high = jnp.logical_not(low)
        for k in (1, 2, 4):
            far.finish_recv(k, low)
        for k in (0, 3):
            far.finish_recv(k, high)
        q, x = jnp.where(low, 0, 9), jnp.where(low, -1, 7)
        node_ahead(nodes, ahead, q)
        node_modes(nodes, ahead, halo, halo_up, modes, q)
        energy[x + 3] = scaled(x)
        for k in (6, 8):
            far.finish_recv(k, low)
        for k in (5, 7):
            far.finish_recv(k, high)

    def put_edge():
        far.finish_recv(9, at[0] == half - 1)
        far.finish_recv(10, at[0] == half)
        row, lane = iota((8, 256), 0), iota((8, 256), 1)
        for j in range(3):
            @pl.when(beside & up_first if j == 2 else beside)
            def _():
                k = jnp.where(down_first, 0, 11) + j
                edge = roll(edge_in[:, 256:384], 127 - j, 1)
                value = jnp.where(lane == 255, jnp.concatenate([edge, edge], axis=1), energy[k])
                energy[k] = jnp.where(row == 7, jnp.broadcast_to(edge_in[j:j + 1, 0:256], (8, 256)), value)

    def chain(first, planes):
        for j in range(planes):
            k = first + j
            total = psum[k] + sums_in[k]
            hyper = jnp.tanh(sharpness * (total * inv[k] - threshold))
            smooth = (base + hyper) * (1.0 / denom)
            slope = (1.0 - hyper * hyper) * (sharpness / denom)
            vol2[k, 0:8, 0:256] = smooth * smooth * slope * energy[k]

    early, late = jnp.where(down_first, 6, 0), jnp.where(down_first, 0, 8)
    places = [(i, early + i) for i in range(8)] + [(8 + i, late + i) for i in range(6)]
    side_planes(up_first)
    chain(early, 8)
    pack_rows(vol2, early, 4, rows2)
    send_rows(last, rows2, rows_in2)
    pack_strips(vol2, places[:8], 8, pack2, None)
    side_planes(down_first)
    put_edge()
    chain(late, 6)
    pack_strips(vol2, places[8:], 8, pack2, None)
    send_strips(last, pack2, strip2)
    pack_rows(vol2, late, 3, rows3)
    send_rows(last, rows3, rows_in3)
    for ex in (near, far, last):
        for k in range(len(ex.items)):
            done = beside & (down_first if k == 7 else up_first) if ex is far and k in (7, 8) else None
            ex.finish_send(k, done)
    for j in range(3):
        for leg in range(2):
            here, _, copy = way(j, leg)
            pl.when(here)(copy.wait_send)
    for k in (0, 1):
        last.finish_recv(k)
    unpack_rows(vol2, early, 4, rows_in2)
    for k in (8, 9):
        last.finish_recv(k)
    unpack_rows(vol2, late, 3, rows_in3)
    row_sums(vol2, ysum2, 0, 14, (0, 256))
    for i in range(4):
        planes = pl.ds(2 * i, 2)
        t0, t1 = cone_inner(vol2, ysum2, 2 * i)
        inner[planes, :, 0:128] = t0
        inner[planes, :, 128:256] = t1
    for k in range(2, 8):
        last.finish_recv(k)
    unpack_strips(vol2, places, 8, strip2)
    row_sums(vol2, ysum2, 0, 14, (256, 384))
    for i in range(4):
        planes = pl.ds(2 * i, 2)
        for half_at, t in zip((0, 128), cone_halo(vol2, ysum2, 2 * i)):
            lanes = pl.ds(half_at, 128)
            out[planes, :, lanes] = jnp.where(fl[planes, :, lanes] >= 2, inner[planes, :, lanes] + t, 0.0)


def on_device(grid, *args):
    f32, i32 = jnp.float32, jnp.int32
    V = pltpu.VMEM
    dma = pltpu.SemaphoreType.DMA
    strip, pack = V((2, 3, 8, 128), f32), V((2, 8, 128), f32)
    return pl.pallas_call(
        functools.partial(kernel, grid),
        out_shape=pltpu.VMEM((8, 8, 256), f32),
        in_specs=[pl.BlockSpec(memory_space=pl.ANY)] * 6,
        out_specs=pl.BlockSpec(memory_space=pltpu.VMEM),
        scratch_shapes=[
            V((20, 16, 384), f32), V((14, 16, 384), f32), V((3, 20, 8, 384), f32), V((3, 14, 8, 384), f32), V((8, 8, 256), f32),
            V((14, 8, 256), f32), V((14, 8, 256), f32),
            V((6, 8, 256), f32), V((6, 8, 256), f32), strip, pack,
            V((2, 4, 8, 256), f32), V((2, 4, 8, 256), f32), V((2, 3, 8, 256), f32), V((2, 3, 8, 256), f32), strip, pack,
            V((6, 10, 8, 256), f32), V((8, 8, 256), f32), V((10, 6, 8, 256), f32), V((10, 8, 384), f32), V((10, 8, 256), f32),
            V((10, 6, 4, 8, 256), f32),
            V((9, 3, 8, 256), f32), V((8, 8, 256), i32), V((14, 8, 256), f32), V((14, 8, 256), f32),
            V((9, 8, 256), f32), V((10, 8, 384), f32), V((8, 384), f32), V((8, 384), f32),
            dma((6,)), pltpu.SemaphoreType.REGULAR, dma((3,)), dma((3,)), dma((3,)), dma((9,)), dma((9,)), dma((11,)), dma((11,)), dma((10,)), dma((10,)),
        ],
        compiler_params=pltpu.CompilerParams(
            collective_id=0, has_side_effects=True, vmem_limit_bytes=63 << 20),
        name="sensitivity",
    )(*args)


def solution(mesh):
    grid = tuple(mesh.shape[a] for a in AXES)
    brick = P("gx", "gy", "gz")
    field = P(None, "gx", "gy", "gz")
    return jax.shard_map(
        functools.partial(on_device, grid), mesh=mesh,
        in_specs=(brick, brick, field, field, brick, brick), out_specs=brick, check_vma=False,
    )
```
